32 devices in a mesh: dp: 8 (over y, x, core), seq: 4 (over z).
Axes of the slice: x: 2, y: 2, z: 4, core: 2. Of those that a mesh axis runs over, the one named last changes fastest.
Arguments:
- tokens: bfloat16 [16, 4096, 512], P('dp', 'seq'), may hold values from -6 to 6
- item_lengths: int32 [16, 65], P('dp'), may hold values from 64 to 250, as said below
- w_qkv: bfloat16 [512, 1536], replicated, may hold values from -0.25 to 0.25
- w_out: bfloat16 [512, 512], replicated, may hold values from -6 to 6
- w_up: bfloat16 [512, 2048], replicated, may hold values from -0.25 to 0.25
- w_down: bfloat16 [2048, 512], replicated, may hold values from -0.125 to 0.125
- gain_one: float32 [512], replicated, may hold values from 0.1 to 1.9
- gain_two: float32 [512], replicated, may hold values from 0.1 to 1.9
- cotangent: bfloat16 [16, 4096, 512], P('dp', 'seq'), may hold values from -6 to 6
Outputs:
- output: bfloat16 [16, 4096, 512], P('dp', 'seq')
- grad_tokens: bfloat16 [16, 4096, 512], P('dp', 'seq')
- grad_qkv: float32 [512, 1536], replicated
- grad_out: float32 [512, 512], replicated
- grad_up: float32 [512, 2048], replicated
- grad_down: float32 [2048, 512], replicated
- grad_gain_one: float32 [512], replicated
- grad_gain_two: float32 [512], replicated
The draws below stay inside these ranges and needn't reach their ends.
Inputs may be any that keep to these rules, and one draw needn't show every extreme that they name: `item_lengths`: each row's items are laid end to end from position 0 in slot order; an item that would end past 4096 and all slots after it are left out, and the rest of the row is empty. Every length is 64, 128 or 250, and no item ends at a multiple of 512 below 4096.
All inputs are finite; a program needn't handle non-finite values.
Results may differ from the reference program's by a relative error of at most 0.013.
Values may be sent and summed in bfloat16 or wider, within the bound.
A program may use at most 192 MiB of HBM per device.

```python
import jax
import jax.numpy as jnp
from jax import lax

D = 512
H = 8
E = 64
FF = 2048
SEQ_LEN = 4096
LEN_SMALL = 64
LEN_MID = 128
LEN_LONG = 250
ROWS = 16
SLOTS = 65


def draw_item_lengths(key, part):
    key = jax.random.fold_in(key, 11)
    picked = jax.random.randint(key, (ROWS, SLOTS), 0, 3)
    row_ids = jnp.arange(ROWS)[:, None]
    slot_ids = jnp.arange(SLOTS)[None, :]
    picked = jnp.where((row_ids == 0) & (slot_ids == 0), 2, picked)
    picked = jnp.where((row_ids == 0) & (slot_ids == 1), 0, picked)
    length_table = jnp.array([LEN_SMALL, LEN_MID, LEN_LONG], jnp.int32)
    spacing = SEQ_LEN // 8

    def place_item(item_ends, choice_now):
        item_length = length_table[choice_now]
        item_end = item_ends + item_length
        lands_on = (item_end % spacing == 0) & (item_end < SEQ_LEN)
        item_length = jnp.where(lands_on, length_table[(choice_now + 1) % 3], item_length)
        return (item_ends + item_length, item_length)
    _, lengths = lax.scan(place_item, jnp.zeros((ROWS,), jnp.int32), picked.T.astype(jnp.int32))
    return lengths.T.astype(jnp.int32)


def level_of(key, shape, cuts, least, top_value):
    factor_of = 1.0
    for position, blocks in cuts:
        heights = jax.random.uniform(jax.random.fold_in(jax.random.fold_in(key, 6), position), (blocks,), jnp.float32, least / len(cuts), top_value / len(cuts))
        factor_of = factor_of * jnp.repeat(jnp.exp(heights), shape[position] // blocks).reshape((-1,) + (1,) * (len(shape) - 1 - position))
    return factor_of


def scatter_about(key, extent, scale, limit, pieces=(), held_as=jnp.bfloat16):
    level = level_of(key, extent, pieces, -0.22, 0.18) if pieces else 1.0
    entries = jax.random.normal(key, extent, jnp.float32) * scale * level
    return jnp.minimum(jnp.maximum(entries, -limit), limit).astype(held_as)


def setup_inputs(seed: int = 0) -> dict:
    streams_of = jax.random.split(jax.random.key(seed), 10)
    tokens = scatter_about(streams_of[0], (ROWS, SEQ_LEN, D), 1.0, 6.0, ((0, 8), (1, 4)))
    item_lengths = draw_item_lengths(jax.random.fold_in(streams_of[9], 71), 0)
    w_qkv = scatter_about(streams_of[2], (D, 3 * D), D ** -0.5, 0.25)
    w_out = scatter_about(streams_of[3], (D, D), ((LEN_LONG / (2 * D)) ** 0.5), 6.0)
    w_up = scatter_about(streams_of[4], (D, FF), D ** -0.5, 0.25)
    w_down = scatter_about(streams_of[5], (FF, D), FF ** -0.5, 0.125)
    gain_one = jnp.clip(1.0 + 0.18 * jax.random.normal(streams_of[6], (D,), jnp.float32), 0.1, 1.9)
    gain_two = jnp.clip(1.0 + 0.18 * jax.random.normal(streams_of[7], (D,), jnp.float32), 0.1, 1.9)
    cotangent = scatter_about(streams_of[8], (ROWS, SEQ_LEN, D), 1.0, 6.0, ((0, 8), (1, 4)))
    return dict(tokens=tokens, item_lengths=item_lengths, w_qkv=w_qkv, w_out=w_out, w_up=w_up, w_down=w_down, gain_one=gain_one, gain_two=gain_two, cotangent=cotangent)


EPSILON = 1e-05
NEGATIVE = -1e+30
HIGHEST_PRECISION = lax.Precision.HIGHEST

@jax.custom_vjp
def low(v):
    return lax.optimization_barrier(v.astype(jnp.bfloat16)).astype(jnp.float32)

@jax.custom_vjp
def low_back(v):
    return v

def low_keep(v):
    return (low(v), None)

def low_pass(kept, grad):
    return (grad,)

def back_keep(v):
    return (v, None)

def back_low(kept, grad):
    return (low(grad),)
low.defvjp(low_keep, low_pass)
low_back.defvjp(back_keep, back_low)

def layer_norm(values, scaling):
    centered = values - lax.optimization_barrier(jnp.mean(values, axis=-1, keepdims=True))
    variance = lax.optimization_barrier(jnp.mean(centered * centered, axis=-1, keepdims=True))
    return centered * lax.rsqrt(variance + EPSILON) * scaling

def segment_row(ends_row, positions):
    counted = lax.optimization_barrier(jnp.sum((positions[:, None] >= ends_row[None, :]).astype(jnp.int32), axis=1))
    inside = (positions >= 0) & (positions < SEQ_LEN)
    return jnp.where(inside, counted, -1).astype(jnp.int32)

def attend_block(query_block, key_window, value_window, seg_query, seg_key):
    scores = jnp.einsum('qe,ke->qk', query_block, key_window, precision=HIGHEST_PRECISION) * 0.125
    same_item = seg_query[:, None] == seg_key[None, :]
    scores = jnp.where(same_item, low_back(scores), NEGATIVE)
    softmax_probs = jax.nn.softmax(scores, axis=-1)
    return jnp.einsum('qk,ke->qe', low(softmax_probs), value_window, precision=HIGHEST_PRECISION)

def row_layer(row_input, ends_row, fitted_row, weights):
    w_qkv, w_out, w_up, w_down, gain_one, gain_two = weights
    margin = LEN_LONG
    block_rows = min(512, SEQ_LEN)
    block_count = SEQ_LEN // block_rows
    window_len = block_rows + 2 * margin
    seg_padded = segment_row(ends_row, jnp.arange(-margin, SEQ_LEN + margin, dtype=jnp.int32))
    seg_row = seg_padded[margin:margin + SEQ_LEN]
    normed_one = low(layer_norm(row_input, gain_one))
    projected = low_back(low(jnp.dot(normed_one, w_qkv, precision=HIGHEST_PRECISION)))
    split_heads = projected.reshape(SEQ_LEN, 3, H, E).transpose(1, 2, 0, 3)
    padding_spec = ((0, 0), (margin, margin), (0, 0))
    keys_padded = jnp.pad(split_heads[1], padding_spec)
    values_padded = jnp.pad(split_heads[2], padding_spec)
    block_step = jax.checkpoint(attend_block)

    def head_work(inputs):
        head_queries, head_keys, head_values = inputs

        def block_work(block_index):
            begin_at = block_index * block_rows
            query_block = lax.dynamic_slice_in_dim(head_queries, begin_at, block_rows, 0)
            key_window = lax.dynamic_slice_in_dim(head_keys, begin_at, window_len, 0)
            value_window = lax.dynamic_slice_in_dim(head_values, begin_at, window_len, 0)
            seg_query = lax.dynamic_slice_in_dim(seg_row, begin_at, block_rows, 0)
            seg_key = lax.dynamic_slice_in_dim(seg_padded, begin_at, window_len, 0)
            return block_step(query_block, key_window, value_window, seg_query, seg_key)
        blocks = lax.map(block_work, jnp.arange(block_count, dtype=jnp.int32))
        return blocks.reshape(SEQ_LEN, E)
    head_out = lax.map(head_work, (split_heads[0], keys_padded, values_padded))
    mixed = low_back(low(head_out.transpose(1, 0, 2).reshape(SEQ_LEN, D)))
    valid_mask = (seg_row < fitted_row).astype(jnp.float32)[:, None]
    resid_one = row_input + valid_mask * low_back(jnp.dot(mixed, w_out, precision=HIGHEST_PRECISION))
    normed_two = low(layer_norm(resid_one, gain_two))
    hidden = low_back(jnp.dot(normed_two, w_up, precision=HIGHEST_PRECISION))
    activated = low(jax.nn.gelu(hidden))
    return resid_one + low_back(jnp.dot(activated, w_down, precision=HIGHEST_PRECISION))

def reference(tokens, item_lengths, w_qkv, w_out, w_up, w_down, gain_one, gain_two, cotangent):
    item_ends = jnp.cumsum(item_lengths, axis=1).astype(jnp.int32)
    fitted = lax.optimization_barrier(jnp.sum((item_ends <= SEQ_LEN).astype(jnp.int32), axis=1)).astype(jnp.int32)
    row_step = jax.checkpoint(row_layer)

    def forward(inputs_full, qkv_full, out_full, up_full, down_full, first_gain, second_gain):
        weights = (qkv_full, out_full, up_full, down_full, first_gain, second_gain)
        return lax.map(lambda inputs: row_step(inputs[0], inputs[1], inputs[2], weights), (inputs_full, item_ends, fitted))
    output, pullback = jax.vjp(forward, tokens.astype(jnp.float32), w_qkv.astype(jnp.float32), w_out.astype(jnp.float32), w_up.astype(jnp.float32), w_down.astype(jnp.float32), gain_one.astype(jnp.float32), gain_two.astype(jnp.float32))
    grads = pullback(cotangent.astype(jnp.float32))
    return (output.astype(jnp.bfloat16), grads[0].astype(jnp.bfloat16), grads[1], grads[2], grads[3], grads[4], grads[5], grads[6])
```

```python
import functools

import jax
import jax.numpy as jnp
from jax import lax
from jax.experimental import pallas as pl
from jax.experimental.pallas import tpu as pltpu
from jax.sharding import PartitionSpec as P

H = 8
E = 64
SEQ_LEN = 4096
LEN_LONG = 250
HALO = 256
TILE = 256
ENTRIES = 8

EPSILON = 1e-05
NEGATIVE = -1e30
SCALE2 = 0.125 * 1.4426950408889634
MIB = 2**20
F32 = jnp.float32
BF16 = jnp.bfloat16
NT = (((1,), (1,)), ((), ()))
TN = (((0,), (0,)), ((), ()))


def layer_norm(values, scaling):
    centered = values - jnp.mean(values, axis=-1, keepdims=True)
    variance = jnp.mean(centered * centered, axis=-1, keepdims=True)
    return centered * lax.rsqrt(variance + EPSILON) * scaling


def max_tiles(local_len):
    return 2 * ((local_len + LEN_LONG - 1) // (TILE + 1)) + 3


def plan_tiles(lengths, table, row, tiles):
    slots = lengths.shape[1]
    local_len = tiles[1]
    low = lax.axis_index("seq") * local_len
    high = low + local_len
    base = row * (tiles[0] + 1) * ENTRIES

    def step(k, carry):
        begin, count, tile_begin, in_tile, fitted_end = carry
        true_end = begin + lengths[row, k]
        end = jnp.minimum(true_end, SEQ_LEN)
        touches = (end > low) & (begin < high) & (end > begin)
        fresh = touches & ((count == 0) | (end - tile_begin > TILE))
        count = jnp.where(fresh, count + 1, count)
        tile_begin = jnp.where(fresh, begin, tile_begin)
        in_tile = jnp.where(fresh, 0, in_tile + 1)

        @pl.when(touches)
        def _():
            spot = base + (count - 1) * ENTRIES
            table[spot] = tile_begin - low + HALO
            for j in range(4):

                @pl.when(j >= in_tile)
                def _():
                    table[spot + 1 + j] = end - tile_begin

        fitted_end = jnp.where(true_end <= SEQ_LEN, true_end, fitted_end)
        return (end, count, tile_begin, in_tile, fitted_end)

    zero = jnp.int32(0)
    _, count, _, _, fitted_end = lax.fori_loop(0, slots, step, (zero, zero, zero, zero, zero))
    table[base + tiles[0] * ENTRIES] = count
    table[base + tiles[0] * ENTRIES + 1] = fitted_end
    return count


def write_bias(table, spot, bias):
    def segments(positions):
        return sum((positions >= table[spot + 1 + j]).astype(jnp.int32) for j in range(4))

    seg_key = segments(lax.broadcasted_iota(jnp.int32, (TILE, 128), 0))
    for half in range(TILE // 128):
        seg_query = segments(lax.broadcasted_iota(jnp.int32, (1, 128), 1) + half * 128)
        bias[:, half * 128 : (half + 1) * 128] = jnp.where(seg_key == seg_query, 0.0, NEGATIVE)


def head_mask(side):
    lane = lax.broadcasted_iota(jnp.int32, (1, 128), 1)
    return jnp.where((lane // E) == side, 1.0, 0.0)


def attend_forward_kernel(
    tiles, lengths, local, left, right, w_qkv, gain, mixed, stats, halo_qkv, table, spread, out, bias
):
    row = pl.program_id(0)
    local_len = local.shape[1]
    count = plan_tiles(lengths, table, row, tiles)
    for side, tokens in enumerate((left, right)):
        normed = layer_norm(tokens[0].astype(F32), gain[...]).astype(BF16)
        made = jnp.dot(normed, w_qkv[...], preferred_element_type=F32).astype(BF16)
        halo_qkv[0, side * HALO : (side + 1) * HALO, :] = made
        start = side * (HALO + local_len)
        for c in range(12):
            spread[c, start : start + HALO, :] = made[:, c * 128 : (c + 1) * 128].astype(F32)
    for c in range(12):
        spread[c, HALO : HALO + local_len, :] = local[0, :, c * 128 : (c + 1) * 128].astype(F32)
    masks = [head_mask(0), head_mask(1)]

    def one_tile(b, _):
        spot = (row * (tiles[0] + 1) + b) * ENTRIES
        begin = table[spot]
        write_bias(table, spot, bias)
        for pair in range(4):
            q2 = spread[pair, pl.ds(begin, TILE), :]
            k2 = spread[4 + pair, pl.ds(begin, TILE), :].astype(BF16)
            v2 = spread[8 + pair, pl.ds(begin, TILE), :].T.astype(BF16)
            parts = []
            for side in range(2):
                masked = (q2 * masks[side]).astype(BF16)
                scores = lax.dot_general(k2, masked, NT, preferred_element_type=F32) + bias[...]
                peak = jnp.max(scores, axis=0, keepdims=True)
                weights = jnp.exp2((scores - peak) * SCALE2)
                total = jnp.sum(weights, axis=0, keepdims=True)
                values = v2[side * E : (side + 1) * E]
                made = jnp.dot(values, weights.astype(BF16), preferred_element_type=F32)
                parts.append(made * (1.0 / total))
                h = 2 * pair + side
                stats[0, b, h : h + 1, :] = peak * SCALE2 + jnp.log2(total)
            out[pair, pl.ds(begin, TILE), :] = jnp.concatenate(parts, axis=0).T
        return 0

    lax.fori_loop(0, count, one_tile, 0)
    for c in range(4):
        mixed[0, :, c * 128 : (c + 1) * 128] = out[c, HALO : HALO + local_len, :].astype(BF16)


def attend_backward_kernel(
    tiles, table, local, halo_qkv, grad, left, right, stats, d_projected, spread, d_out, made, bias
):
    row = pl.program_id(0)
    local_len = local.shape[1]
    for c in range(12):
        columns = slice(c * 128, (c + 1) * 128)
        spread[c, HALO : HALO + local_len, :] = local[0, :, columns].astype(F32)
        for side in range(2):
            start = side * (HALO + local_len)
            piece = halo_qkv[0, side * HALO : (side + 1) * HALO, columns]
            spread[c, start : start + HALO, :] = piece.astype(F32)
    for c in range(4):
        columns = slice(c * 128, (c + 1) * 128)
        d_out[c, :HALO, :] = left[0, :, columns].astype(F32)
        d_out[c, HALO : HALO + local_len, :] = grad[0, :, columns].astype(F32)
        d_out[c, HALO + local_len :, :] = right[0, :, columns].astype(F32)
    masks = [head_mask(0), head_mask(1)]
    count = table[(row * (tiles[0] + 1) + tiles[0]) * ENTRIES]

    def one_tile(b, _):
        spot = (row * (tiles[0] + 1) + b) * ENTRIES
        begin = table[spot]
        write_bias(table, spot, bias)
        for pair in range(4):
            q2 = spread[pair, pl.ds(begin, TILE), :]
            k2 = spread[4 + pair, pl.ds(begin, TILE), :]
            v2 = spread[8 + pair, pl.ds(begin, TILE), :].astype(BF16)
            o2 = d_out[pair, pl.ds(begin, TILE), :]
            k2t = k2.T.astype(BF16)
            k2 = k2.astype(BF16)
            probs, grads, q_parts, o_parts, dq_parts = [], [], [], [], []
            for side in range(2):
                h = 2 * pair + side
                masked_q = (q2 * masks[side]).astype(BF16)
                masked_o = (o2 * masks[side]).astype(BF16)
                scores = lax.dot_general(k2, masked_q, NT, preferred_element_type=F32)
                p = jnp.exp2(scores * SCALE2 + bias[...] - stats[0, b, h : h + 1, :])
                dp = lax.dot_general(v2, masked_o, NT, preferred_element_type=F32)
                weighted = p * dp
                inner = jnp.sum(weighted, axis=0, keepdims=True)
                ds = (weighted - p * inner).astype(BF16)
                dq_parts.append(
                    jnp.dot(k2t[side * E : (side + 1) * E], ds, preferred_element_type=F32)
                )
                probs.append(p.astype(BF16))
                grads.append(ds)
                q_parts.append(masked_q)
                o_parts.append(masked_o)
            made[pair, pl.ds(begin, TILE), :] = jnp.concatenate(dq_parts, axis=0).T * 0.125
            dk = jnp.dot(grads[0], q_parts[0], preferred_element_type=F32)
            dk += jnp.dot(grads[1], q_parts[1], preferred_element_type=F32)
            made[4 + pair, pl.ds(begin, TILE), :] = dk * 0.125
            dv = jnp.dot(probs[0], o_parts[0], preferred_element_type=F32)
            dv += jnp.dot(probs[1], o_parts[1], preferred_element_type=F32)
            made[8 + pair, pl.ds(begin, TILE), :] = dv
        return 0

    lax.fori_loop(0, count, one_tile, 0)
    for c in range(12):
        d_projected[0, :, c * 128 : (c + 1) * 128] = made[c, HALO : HALO + local_len, :].astype(BF16)


def row_spec(*shape):
    return pl.BlockSpec((1,) + shape, lambda r: (r,) + (0,) * len(shape))


def whole_spec(*shape):
    return pl.BlockSpec(shape, lambda r: (0,) * len(shape))


def smem_spec():
    return pl.BlockSpec(memory_space=pltpu.SMEM)


def attend_forward(lengths, local, left, right, w_qkv, gain):
    rows, local_len, _ = local.shape
    width = left.shape[2]
    most = max_tiles(local_len)
    held = local_len + 2 * HALO
    return pl.pallas_call(
        functools.partial(attend_forward_kernel, (most, local_len)),
        grid=(rows,),
        out_shape=(
            jax.ShapeDtypeStruct((rows, local_len, width), BF16),
            jax.ShapeDtypeStruct((rows, most, H, TILE), F32),
            jax.ShapeDtypeStruct((rows, 2 * HALO, 3 * width), BF16),
            jax.ShapeDtypeStruct((rows * (most + 1) * ENTRIES,), jnp.int32),
        ),
        in_specs=[
            smem_spec(),
            row_spec(local_len, 3 * width),
            row_spec(HALO, width),
            row_spec(HALO, width),
            whole_spec(width, 3 * width),
            whole_spec(1, width),
        ],
        out_specs=(
            row_spec(local_len, width),
            row_spec(most, H, TILE),
            row_spec(2 * HALO, 3 * width),
            smem_spec(),
        ),
        scratch_shapes=[
            pltpu.VMEM((12, held, 128), F32),
            pltpu.VMEM((4, held, 128), F32),
            pltpu.VMEM((TILE, TILE), F32),
        ],
        compiler_params=pltpu.CompilerParams(vmem_limit_bytes=56 * MIB),
        name="attend_forward",
    )(lengths, local, left, right, w_qkv, gain.reshape(1, width))


def attend_backward(table, local, halo_qkv, grad, left, right, stats):
    rows, local_len, width = grad.shape
    most = max_tiles(local_len)
    held = local_len + 2 * HALO
    return pl.pallas_call(
        functools.partial(attend_backward_kernel, (most, local_len)),
        grid=(rows,),
        out_shape=jax.ShapeDtypeStruct((rows, local_len, 3 * width), BF16),
        in_specs=[
            smem_spec(),
            row_spec(local_len, 3 * width),
            row_spec(2 * HALO, 3 * width),
            row_spec(local_len, width),
            row_spec(HALO, width),
            row_spec(HALO, width),
            row_spec(most, H, TILE),
        ],
        out_specs=row_spec(local_len, 3 * width),
        scratch_shapes=[
            pltpu.VMEM((12, held, 128), F32),
            pltpu.VMEM((4, held, 128), F32),
            pltpu.VMEM((12, held, 128), F32),
            pltpu.VMEM((TILE, TILE), F32),
        ],
        compiler_params=pltpu.CompilerParams(vmem_limit_bytes=60 * MIB),
        name="attend_backward",
    )(table, local, halo_qkv, grad, left, right, stats)


def exchange(values, devices):
    before = lax.ppermute(values[:, -HALO:], "seq", [(i, i + 1) for i in range(devices - 1)])
    after = lax.ppermute(values[:, :HALO], "seq", [(i + 1, i) for i in range(devices - 1)])
    return before, after


def body(
    devices, tokens, item_lengths, w_qkv, w_out, w_up, w_down, gain_one, gain_two, cotangent
):
    row_count, local_len, width = tokens.shape
    token_count = row_count * local_len
    left, right = exchange(tokens, devices)
    inputs_flat = tokens.astype(F32).reshape(token_count, width)
    normed_one, norm_one_back = jax.vjp(layer_norm, inputs_flat, gain_one)
    normed_one_low = normed_one.astype(BF16)
    projected = jnp.dot(normed_one_low, w_qkv, preferred_element_type=F32)
    projected = projected.astype(BF16).reshape(row_count, local_len, 3 * width)
    mixed, stats, halo_qkv, table = attend_forward(
        item_lengths, projected, left, right, w_qkv, gain_one
    )
    most = max_tiles(local_len)
    fitted_end = table.reshape(row_count, most + 1, ENTRIES)[:, most, 1]
    positions = lax.axis_index("seq") * local_len + jnp.arange(local_len, dtype=jnp.int32)
    valid_mask = (positions[None] < fitted_end[:, None]).astype(F32).reshape(token_count, 1)
    mixed_local = mixed.reshape(token_count, width)
    attn_result = jnp.dot(mixed_local, w_out, preferred_element_type=F32)
    resid_one = inputs_flat + valid_mask * attn_result
    normed_two, norm_two_back = jax.vjp(layer_norm, resid_one, gain_two)
    normed_two_low = normed_two.astype(BF16)
    hidden = jnp.dot(normed_two_low, w_up, preferred_element_type=F32)
    activated, gelu_back = jax.vjp(jax.nn.gelu, hidden)
    activated_low = activated.astype(BF16)
    dense_out = jnp.dot(activated_low, w_down, preferred_element_type=F32)
    output = (resid_one + dense_out).astype(BF16).reshape(row_count, local_len, width)
    grad_output_low = cotangent.reshape(token_count, width)
    grad_output = grad_output_low.astype(F32)
    grad_activated = jnp.dot(grad_output_low, w_down.T, preferred_element_type=F32)
    grad_hidden = gelu_back(grad_activated)[0].astype(BF16)
    grad_normed_two = jnp.dot(grad_hidden, w_up.T, preferred_element_type=F32)
    grad_resid_norm, grad_gain_two = norm_two_back(grad_normed_two)
    grad_resid = grad_output + grad_resid_norm
    grad_attn = (valid_mask * grad_resid).astype(BF16)
    grad_mixed = jnp.dot(grad_attn, w_out.T, preferred_element_type=F32).astype(BF16)
    grad_mixed = grad_mixed.reshape(row_count, local_len, width)
    grad_left, grad_right = exchange(grad_mixed, devices)
    grad_down = jnp.einsum("tf,td->fd", activated_low, grad_output_low, preferred_element_type=F32)
    grad_up = jnp.einsum("td,tf->df", normed_two_low, grad_hidden, preferred_element_type=F32)
    grad_out = jnp.einsum("td,te->de", mixed_local, grad_attn, preferred_element_type=F32)
    grad_projected = attend_backward(
        table, projected, halo_qkv, grad_mixed, grad_left, grad_right, stats
    ).reshape(token_count, 3 * width)
    grad_qkv = jnp.einsum("td,tf->df", normed_one_low, grad_projected, preferred_element_type=F32)
    grad_normed_one = jnp.dot(grad_projected, w_qkv.T, preferred_element_type=F32)
    grad_input_norm, grad_gain_one = norm_one_back(grad_normed_one)
    grad_tokens = (grad_resid + grad_input_norm).astype(BF16).reshape(row_count, local_len, width)
    grads = lax.psum(
        (grad_qkv, grad_out, grad_up, grad_down, grad_gain_one, grad_gain_two), ("dp", "seq")
    )
    return (output, grad_tokens) + grads


def solution(mesh):
    rows = P("dp", "seq", None)
    placed = (rows, P("dp", None), P(), P(), P(), P(), P(), P(), rows)
    return jax.shard_map(
        functools.partial(body, mesh.shape["seq"]),
        mesh=mesh,
        in_specs=placed,
        out_specs=(rows, rows, P(), P(), P(), P(), P(), P()),
        check_vma=False,
    )
```

```python
import functools

import jax
import jax.numpy as jnp
from jax import lax
from jax.experimental import pallas as pl
from jax.experimental.pallas import tpu as pltpu
from jax.sharding import PartitionSpec as P

H = 8
E = 64
SEQ_LEN = 4096
LEN_LONG = 250
HALO = 256
TILE = 256
ENTRIES = 8

EPSILON = 1e-05
NEGATIVE = -1e30
SCALE2 = 0.125 * 1.4426950408889634
MIB = 2**20
F32 = jnp.float32
BF16 = jnp.bfloat16
NT = (((1,), (1,)), ((), ()))
TN = (((0,), (0,)), ((), ()))
MESH = pl.DeviceIdType.MESH
PIPELINED = 3


def layer_norm(values, scaling):
    centered = values - jnp.mean(values, axis=-1, keepdims=True)
    variance = jnp.mean(centered * centered, axis=-1, keepdims=True)
    return centered * lax.rsqrt(variance + EPSILON) * scaling


def max_tiles(local_len):
    return 2 * ((local_len + LEN_LONG - 1) // (TILE + 1)) + 3


def plan_tiles(lengths, table, row, tiles):
    slots = lengths.shape[1]
    local_len = tiles[1]
    low = lax.axis_index("seq") * local_len
    high = low + local_len
    base = row * (tiles[0] + 1) * ENTRIES

    def step(k, carry):
        begin, count, tile_begin, in_tile, fitted_end = carry
        true_end = begin + lengths[row, k]
        end = jnp.minimum(true_end, SEQ_LEN)
        touches = (end > low) & (begin < high) & (end > begin)
        fresh = touches & ((count == 0) | (end - tile_begin > TILE))
        count = jnp.where(fresh, count + 1, count)
        tile_begin = jnp.where(fresh, begin, tile_begin)
        in_tile = jnp.where(fresh, 0, in_tile + 1)

        @pl.when(touches)
        def _():
            spot = base + (count - 1) * ENTRIES
            table[spot] = tile_begin - low + HALO
            for j in range(4):

                @pl.when(j >= in_tile)
                def _():
                    table[spot + 1 + j] = end - tile_begin

        fitted_end = jnp.where(true_end <= SEQ_LEN, true_end, fitted_end)
        return (end, count, tile_begin, in_tile, fitted_end)

    zero = jnp.int32(0)
    _, count, _, _, fitted_end = lax.fori_loop(0, slots, step, (zero, zero, zero, zero, zero))
    table[base + tiles[0] * ENTRIES] = count
    table[base + tiles[0] * ENTRIES + 1] = fitted_end
    return count


def write_bias(table, spot, bias):
    def segments(positions):
        return sum((positions >= table[spot + 1 + j]).astype(jnp.int32) for j in range(4))

    seg_key = segments(lax.broadcasted_iota(jnp.int32, (TILE, 128), 0))
    for half in range(TILE // 128):
        seg_query = segments(lax.broadcasted_iota(jnp.int32, (1, 128), 1) + half * 128)
        bias[:, half * 128 : (half + 1) * 128] = jnp.where(seg_key == seg_query, 0.0, NEGATIVE)


def head_mask(side):
    lane = lax.broadcasted_iota(jnp.int32, (1, 128), 1)
    return jnp.where((lane // E) == side, 1.0, 0.0)


def attend_forward_kernel(
    tiles, lengths, local, left, right, w_qkv, gain, mixed, stats, halo_qkv, table, spread, out, bias
):
    row = pl.program_id(0)
    local_len = local.shape[1]
    count = plan_tiles(lengths, table, row, tiles)
    for side, tokens in enumerate((left, right)):
        normed = layer_norm(tokens[0].astype(F32), gain[...]).astype(BF16)
        made = jnp.dot(normed, w_qkv[...], preferred_element_type=F32).astype(BF16)
        halo_qkv[0, side * HALO : (side + 1) * HALO, :] = made
        start = side * (HALO + local_len)
        for c in range(12):
            spread[c, start : start + HALO, :] = made[:, c * 128 : (c + 1) * 128].astype(F32)
    for c in range(12):
        spread[c, HALO : HALO + local_len, :] = local[0, :, c * 128 : (c + 1) * 128].astype(F32)
    masks = [head_mask(0), head_mask(1)]

    def one_tile(b, _):
        spot = (row * (tiles[0] + 1) + b) * ENTRIES
        begin = table[spot]
        write_bias(table, spot, bias)
        for pair in range(4):
            q2 = spread[pair, pl.ds(begin, TILE), :]
            k2 = spread[4 + pair, pl.ds(begin, TILE), :].astype(BF16)
            v2 = spread[8 + pair, pl.ds(begin, TILE), :].T.astype(BF16)
            parts = []
            for side in range(2):
                masked = (q2 * masks[side]).astype(BF16)
                scores = lax.dot_general(k2, masked, NT, preferred_element_type=F32) + bias[...]
                peak = jnp.max(scores, axis=0, keepdims=True)
                weights = jnp.exp2((scores - peak) * SCALE2)
                total = jnp.sum(weights, axis=0, keepdims=True)
                values = v2[side * E : (side + 1) * E]
                made = jnp.dot(values, weights.astype(BF16), preferred_element_type=F32)
                parts.append(made * (1.0 / total))
                h = 2 * pair + side
                stats[0, b, h : h + 1, :] = peak * SCALE2 + jnp.log2(total)
            out[pair, pl.ds(begin, TILE), :] = jnp.concatenate(parts, axis=0).T
        return 0

    lax.fori_loop(0, count, one_tile, 0)
    for c in range(4):
        mixed[0, :, c * 128 : (c + 1) * 128] = out[c, HALO : HALO + local_len, :].astype(BF16)


def attend_backward_kernel(
    tiles, table, local, halo_qkv, grad, left, right, stats, d_projected, spread, d_out, made, bias
):
    row = pl.program_id(0)
    local_len = local.shape[1]
    for c in range(12):
        columns = slice(c * 128, (c + 1) * 128)
        spread[c, HALO : HALO + local_len, :] = local[0, :, columns].astype(F32)
        for side in range(2):
            start = side * (HALO + local_len)
            piece = halo_qkv[0, side * HALO : (side + 1) * HALO, columns]
            spread[c, start : start + HALO, :] = piece.astype(F32)
    for c in range(4):
        columns = slice(c * 128, (c + 1) * 128)
        d_out[c, :HALO, :] = left[0, :, columns].astype(F32)
        d_out[c, HALO : HALO + local_len, :] = grad[0, :, columns].astype(F32)
        d_out[c, HALO + local_len :, :] = right[0, :, columns].astype(F32)
    masks = [head_mask(0), head_mask(1)]
    count = table[(row * (tiles[0] + 1) + tiles[0]) * ENTRIES]

    def one_tile(b, _):
        spot = (row * (tiles[0] + 1) + b) * ENTRIES
        begin = table[spot]
        write_bias(table, spot, bias)
        for pair in range(4):
            q2 = spread[pair, pl.ds(begin, TILE), :]
            k2 = spread[4 + pair, pl.ds(begin, TILE), :]
            v2 = spread[8 + pair, pl.ds(begin, TILE), :].astype(BF16)
            o2 = d_out[pair, pl.ds(begin, TILE), :]
            k2t = k2.T.astype(BF16)
            k2 = k2.astype(BF16)
            probs, grads, q_parts, o_parts, dq_parts = [], [], [], [], []
            for side in range(2):
                h = 2 * pair + side
                masked_q = (q2 * masks[side]).astype(BF16)
                masked_o = (o2 * masks[side]).astype(BF16)
                scores = lax.dot_general(k2, masked_q, NT, preferred_element_type=F32)
                p = jnp.exp2(scores * SCALE2 + bias[...] - stats[0, b, h : h + 1, :])
                dp = lax.dot_general(v2, masked_o, NT, preferred_element_type=F32)
                weighted = p * dp
                inner = jnp.sum(weighted, axis=0, keepdims=True)
                ds = (weighted - p * inner).astype(BF16)
                dq_parts.append(
                    jnp.dot(k2t[side * E : (side + 1) * E], ds, preferred_element_type=F32)
                )
                probs.append(p.astype(BF16))
                grads.append(ds)
                q_parts.append(masked_q)
                o_parts.append(masked_o)
            made[pair, pl.ds(begin, TILE), :] = jnp.concatenate(dq_parts, axis=0).T * 0.125
            dk = jnp.dot(grads[0], q_parts[0], preferred_element_type=F32)
            dk += jnp.dot(grads[1], q_parts[1], preferred_element_type=F32)
            made[4 + pair, pl.ds(begin, TILE), :] = dk * 0.125
            dv = jnp.dot(probs[0], o_parts[0], preferred_element_type=F32)
            dv += jnp.dot(probs[1], o_parts[1], preferred_element_type=F32)
            made[8 + pair, pl.ds(begin, TILE), :] = dv
        return 0

    lax.fori_loop(0, count, one_tile, 0)
    for c in range(12):
        d_projected[0, :, c * 128 : (c + 1) * 128] = made[c, HALO : HALO + local_len, :].astype(BF16)


def row_spec(*shape):
    return pl.BlockSpec((1,) + shape, lambda r: (r,) + (0,) * len(shape))


def whole_spec(*shape):
    return pl.BlockSpec(shape, lambda r: (0,) * len(shape))


def smem_spec():
    return pl.BlockSpec(memory_space=pltpu.SMEM)


def attend_forward(lengths, local, left, right, w_qkv, gain):
    rows, local_len, _ = local.shape
    width = left.shape[2]
    most = max_tiles(local_len)
    held = local_len + 2 * HALO
    return pl.pallas_call(
        functools.partial(attend_forward_kernel, (most, local_len)),
        grid=(rows,),
        out_shape=(
            jax.ShapeDtypeStruct((rows, local_len, width), BF16),
            jax.ShapeDtypeStruct((rows, most, H, TILE), F32),
            jax.ShapeDtypeStruct((rows, 2 * HALO, 3 * width), BF16),
            jax.ShapeDtypeStruct((rows * (most + 1) * ENTRIES,), jnp.int32),
        ),
        in_specs=[
            smem_spec(),
            row_spec(local_len, 3 * width),
            row_spec(HALO, width),
            row_spec(HALO, width),
            whole_spec(width, 3 * width),
            whole_spec(1, width),
        ],
        out_specs=(
            row_spec(local_len, width),
            row_spec(most, H, TILE),
            row_spec(2 * HALO, 3 * width),
            smem_spec(),
        ),
        scratch_shapes=[
            pltpu.VMEM((12, held, 128), F32),
            pltpu.VMEM((4, held, 128), F32),
            pltpu.VMEM((TILE, TILE), F32),
        ],
        compiler_params=pltpu.CompilerParams(vmem_limit_bytes=56 * MIB),
        name="attend_forward",
    )(lengths, local, left, right, w_qkv, gain.reshape(1, width))


def attend_backward(table, local, halo_qkv, grad, left, right, stats):
    rows, local_len, width = grad.shape
    most = max_tiles(local_len)
    held = local_len + 2 * HALO
    return pl.pallas_call(
        functools.partial(attend_backward_kernel, (most, local_len)),
        grid=(rows,),
        out_shape=jax.ShapeDtypeStruct((rows, local_len, 3 * width), BF16),
        in_specs=[
            smem_spec(),
            row_spec(local_len, 3 * width),
            row_spec(2 * HALO, 3 * width),
            row_spec(local_len, width),
            row_spec(HALO, width),
            row_spec(HALO, width),
            row_spec(most, H, TILE),
        ],
        out_specs=row_spec(local_len, 3 * width),
        scratch_shapes=[
            pltpu.VMEM((12, held, 128), F32),
            pltpu.VMEM((4, held, 128), F32),
            pltpu.VMEM((12, held, 128), F32),
            pltpu.VMEM((TILE, TILE), F32),
        ],
        compiler_params=pltpu.CompilerParams(vmem_limit_bytes=60 * MIB),
        name="attend_backward",
    )(table, local, halo_qkv, grad, left, right, stats)


def exchange(values, devices):
    before = lax.ppermute(values[:, -HALO:], "seq", [(i, i + 1) for i in range(devices - 1)])
    after = lax.ppermute(values[:, :HALO], "seq", [(i + 1, i) for i in range(devices - 1)])
    return before, after


def sum_plan(devices):
    dp, seq = devices
    chip = [("dp", 1 << b) for b in range(1, dp.bit_length() - 1)]
    core = [("dp", 1)]
    along = [("seq", 1 << b) for b in range(seq.bit_length() - 1)]
    return [core + chip + along, core + chip[::-1] + along]


def sum_kernel(devices, grads, gains, outs, gains_out, work, slots, done, gain_slots, sems):
    load_sem, store_sem, send_sem, recv_sem, gain_send, gain_recv = sems
    plans = sum_plan(devices)
    steps = len(plans[0])
    chunks = 2 * PIPELINED
    size = work.shape[0] // chunks
    here = {"dp": lax.axis_index("dp"), "seq": lax.axis_index("seq")}

    def other(axis, bit):
        mine = (here[axis] // bit) % 2
        return mine, {axis: here[axis] + bit - 2 * bit * mine}

    barrier = pltpu.get_barrier_semaphore()
    for axis, bit in plans[0]:
        pl.semaphore_signal(barrier, inc=1, device_id=other(axis, bit)[1], device_id_type=MESH)

    pieces = []
    for k, ref in enumerate(grads):
        for c in range(ref.shape[1] // 128):
            pieces.append((k, c, ref.shape[0]))
    loads, stores, at = [[] for _ in range(chunks)], [[] for _ in range(chunks)], 0
    for k, c, rows in pieces:
        inside, summed = work.at[at : at + rows], done.at[at : at + rows]
        chunk = at // size
        loads[chunk].append(
            pltpu.make_async_copy(grads[k].at[:, c * 128 : (c + 1) * 128], inside, load_sem.at[len(loads[chunk]), chunk])
        )
        stores[chunk].append(
            pltpu.make_async_copy(summed, outs[k].at[:, c * 128 : (c + 1) * 128], store_sem.at[len(stores[chunk]), chunk])
        )
        at += rows
    for chunk in range(chunks):
        for copy in loads[chunk]:
            copy.start()
    pl.semaphore_wait(barrier, steps)

    def place(offset, rows):
        return pl.ds(pl.multiple_of(offset, rows), rows)

    def add(offset, slot, rows, into):
        block = min(rows, 256)

        @pl.loop(0, rows // block)
        def _(i):
            mine = work[pl.ds(pl.multiple_of(offset + i * block, block), block), :].astype(F32)
            theirs = slots[pl.ds(pl.multiple_of(slot + i * block, block), block), :].astype(F32)
            into[pl.ds(pl.multiple_of(offset + i * block, block), block), :] = (mine + theirs).astype(BF16)

    def chunk_events(chunk):
        plan = plans[chunk % 2]
        state = {"offset": chunk * size, "rows": size, "slot": chunk * size, "path": []}

        def halve_start(s):
            mine, target = other(*plan[s])
            half = state["rows"] // 2
            keep = state["offset"] + mine * half
            give = state["offset"] + (1 - mine) * half
            copy = pltpu.make_async_remote_copy(
                src_ref=work.at[place(give, half)],
                dst_ref=slots.at[place(state["slot"], half)],
                send_sem=send_sem.at[chunk, s],
                recv_sem=recv_sem.at[chunk, s],
                device_id=target,
                device_id_type=MESH,
            )
            copy.start()
            state["path"].append((keep, give, half))
            state["copy"] = copy

        def halve_end(s):
            keep, _, half = state["path"][s]
            state["copy"].wait()
            add(keep, state["slot"], half, done if s + 1 == steps else work)
            state.update(offset=keep, rows=half, slot=state["slot"] + half)

        def double_start(s):
            _, target = other(*plan[s])
            keep, give, half = state["path"][s]

            def copy_of(offset):
                return pltpu.make_async_remote_copy(
                    src_ref=done.at[place(offset, half)],
                    dst_ref=done.at[place(offset, half)],
                    send_sem=send_sem.at[chunk, steps + s],
                    recv_sem=recv_sem.at[chunk, steps + s],
                    device_id=target,
                    device_id_type=MESH,
                )

            copy_of(keep).start()
            state["copies"] = (copy_of(keep), copy_of(give))

        def double_end(s):
            state["copies"][0].wait_send()
            state["copies"][1].wait_recv()

        def first():
            for copy in loads[chunk]:
                copy.wait()
            halve_start(0)

        def turn(t):
            if t < steps:
                halve_end(t)
            else:
                double_end(2 * steps - 1 - t)
            if t + 1 < steps:
                halve_start(t + 1)
            elif t + 1 < 2 * steps:
                double_start(2 * steps - 2 - t)
            else:
                for copy in stores[chunk]:
                    copy.start()

        return [first] + [functools.partial(turn, t) for t in range(2 * steps)]

    def gain_events():
        plan = plans[0]
        state = {}

        def start(s):
            copy = pltpu.make_async_remote_copy(
                src_ref=gain_slots.at[2 * s],
                dst_ref=gain_slots.at[2 * s + 1],
                send_sem=gain_send.at[s],
                recv_sem=gain_recv.at[s],
                device_id=other(*plan[s])[1],
                device_id_type=MESH,
            )
            copy.start()
            state["copy"] = copy

        def first():
            gain_slots[0] = gains[...]
            start(0)

        def turn(s):
            state["copy"].wait()
            total = gain_slots[2 * s] + gain_slots[2 * s + 1]
            if s + 1 < steps:
                gain_slots[2 * s + 2] = total
                start(s + 1)
            else:
                gains_out[...] = total

        return [first] + [functools.partial(turn, s) for s in range(steps)]

    runs = [(chunk // 2, chunk_events(chunk)) for chunk in range(chunks)]
    runs.append((0, gain_events()))
    last = max(lag + len(events) for lag, events in runs)
    for t in range(last):
        for lag, events in runs:
            if 0 <= t - lag < len(events):
                events[t - lag]()
    for chunk in range(chunks):
        for copy in stores[chunk]:
            copy.wait()


def sum_grads(devices, grads, gains):
    count = len(grads)
    total_rows = sum(g.shape[0] * g.shape[1] // 128 for g in grads)
    steps = len(sum_plan(devices)[0])
    chunks = 2 * PIPELINED

    def kernel(*refs):
        ins, rest = refs[:count], refs[count:]
        gain_ref, outs, rest = rest[0], rest[1 : 1 + count], rest[1 + count :]
        sum_kernel(devices, ins, gain_ref, outs, *rest[:5], rest[5:])

    any_spec = pl.BlockSpec(memory_space=pl.ANY)
    vmem = pl.BlockSpec(memory_space=pltpu.VMEM)
    made = pl.pallas_call(
        kernel,
        out_shape=[jax.ShapeDtypeStruct(g.shape, BF16) for g in grads]
        + [jax.ShapeDtypeStruct(gains.shape, F32)],
        in_specs=[any_spec] * count + [vmem],
        out_specs=[any_spec] * count + [vmem],
        scratch_shapes=[
            pltpu.VMEM((total_rows, 128), BF16),
            pltpu.VMEM((total_rows, 128), BF16),
            pltpu.VMEM((total_rows, 128), BF16),
            pltpu.VMEM((2 * steps,) + gains.shape, F32),
            pltpu.SemaphoreType.DMA((8, chunks)),
            pltpu.SemaphoreType.DMA((8, chunks)),
            pltpu.SemaphoreType.DMA((chunks, 2 * steps)),
            pltpu.SemaphoreType.DMA((chunks, 2 * steps)),
            pltpu.SemaphoreType.DMA((steps,)),
            pltpu.SemaphoreType.DMA((steps,)),
        ],
        compiler_params=pltpu.CompilerParams(
            collective_id=0, has_side_effects=True, vmem_limit_bytes=40 * MIB
        ),
        name="sum_grads",
    )(*grads, gains)
    return made[:count], made[count]


def body(
    devices, tokens, item_lengths, w_qkv, w_out, w_up, w_down, gain_one, gain_two, cotangent
):
    row_count, local_len, width = tokens.shape
    token_count = row_count * local_len
    left, right = exchange(tokens, devices[1])
    inputs_flat = tokens.astype(F32).reshape(token_count, width)
    normed_one, norm_one_back = jax.vjp(layer_norm, inputs_flat, gain_one)
    normed_one_low = normed_one.astype(BF16)
    projected = jnp.dot(normed_one_low, w_qkv, preferred_element_type=F32)
    projected = projected.astype(BF16).reshape(row_count, local_len, 3 * width)
    mixed, stats, halo_qkv, table = attend_forward(
        item_lengths, projected, left, right, w_qkv, gain_one
    )
    most = max_tiles(local_len)
    fitted_end = table.reshape(row_count, most + 1, ENTRIES)[:, most, 1]
    positions = lax.axis_index("seq") * local_len + jnp.arange(local_len, dtype=jnp.int32)
    valid_mask = (positions[None] < fitted_end[:, None]).astype(F32).reshape(token_count, 1)
    mixed_local = mixed.reshape(token_count, width)
    attn_result = jnp.dot(mixed_local, w_out, preferred_element_type=F32)
    resid_one = inputs_flat + valid_mask * attn_result
    normed_two, norm_two_back = jax.vjp(layer_norm, resid_one, gain_two)
    normed_two_low = normed_two.astype(BF16)
    hidden = jnp.dot(normed_two_low, w_up, preferred_element_type=F32)
    activated, gelu_back = jax.vjp(jax.nn.gelu, hidden)
    activated_low = activated.astype(BF16)
    dense_out = jnp.dot(activated_low, w_down, preferred_element_type=F32)
    output = (resid_one + dense_out).astype(BF16).reshape(row_count, local_len, width)
    grad_output_low = cotangent.reshape(token_count, width)
    grad_output = grad_output_low.astype(F32)
    grad_activated = jnp.dot(grad_output_low, w_down.T, preferred_element_type=F32)
    grad_hidden = gelu_back(grad_activated)[0].astype(BF16)
    grad_normed_two = jnp.dot(grad_hidden, w_up.T, preferred_element_type=F32)
    grad_resid_norm, grad_gain_two = norm_two_back(grad_normed_two)
    grad_resid = grad_output + grad_resid_norm
    grad_attn = (valid_mask * grad_resid).astype(BF16)
    grad_mixed = jnp.dot(grad_attn, w_out.T, preferred_element_type=F32).astype(BF16)
    grad_mixed = grad_mixed.reshape(row_count, local_len, width)
    grad_left, grad_right = exchange(grad_mixed, devices[1])
    grad_down = jnp.einsum("tf,td->fd", activated_low, grad_output_low, preferred_element_type=F32)
    grad_up = jnp.einsum("td,tf->df", normed_two_low, grad_hidden, preferred_element_type=F32)
    grad_out = jnp.einsum("td,te->de", mixed_local, grad_attn, preferred_element_type=F32)
    grad_projected = attend_backward(
        table, projected, halo_qkv, grad_mixed, grad_left, grad_right, stats
    ).reshape(token_count, 3 * width)
    grad_qkv = jnp.einsum("td,tf->df", normed_one_low, grad_projected, preferred_element_type=F32)
    grad_normed_one = jnp.dot(grad_projected, w_qkv.T, preferred_element_type=F32)
    grad_input_norm, grad_gain_one = norm_one_back(grad_normed_one)
    grad_tokens = (grad_resid + grad_input_norm).astype(BF16).reshape(row_count, local_len, width)
    gains = jnp.zeros((8, width), F32).at[0].set(grad_gain_one).at[1].set(grad_gain_two)
    local = [g.astype(BF16) for g in (grad_qkv, grad_out, grad_up, grad_down)]
    summed, gains = sum_grads(devices, local, gains)
    grads = tuple(g.astype(F32) for g in summed) + (gains[0], gains[1])
    return (output, grad_tokens) + grads


def solution(mesh):
    rows = P("dp", "seq", None)
    placed = (rows, P("dp", None), P(), P(), P(), P(), P(), P(), rows)
    return jax.shard_map(
        functools.partial(body, (mesh.shape["dp"], mesh.shape["seq"])),
        mesh=mesh,
        in_specs=placed,
        out_specs=(rows, rows, P(), P(), P(), P(), P(), P()),
        check_vma=False,
    )
```

```python
import functools

import jax
import jax.numpy as jnp
from jax import lax
from jax.experimental import pallas as pl
from jax.experimental.pallas import tpu as pltpu
from jax.sharding import PartitionSpec as P

H = 8
E = 64
SEQ_LEN = 4096
LEN_LONG = 250
HALO = 256
TILE = 256
ENTRIES = 8
BLOCK = 256

EPSILON = 1e-05
NEGATIVE = -1e30
SCALE2 = 0.125 * 1.4426950408889634
GELU_A = 0.7978845608028654
GELU_B = 0.044715
MIB = 2**20
F32 = jnp.float32
BF16 = jnp.bfloat16
NT = (((1,), (1,)), ((), ()))
TN = (((0,), (0,)), ((), ()))
MESH = pl.DeviceIdType.MESH
PIPELINED = 3


def layer_norm(values, scaling):
    centered = values - jnp.mean(values, axis=-1, keepdims=True)
    variance = jnp.mean(centered * centered, axis=-1, keepdims=True)
    return centered * lax.rsqrt(variance + EPSILON) * scaling


def normalize(values):
    centered = values - jnp.mean(values, axis=-1, keepdims=True)
    scale = lax.rsqrt(jnp.mean(centered * centered, axis=-1, keepdims=True) + EPSILON)
    return centered * scale, scale


def normalize_back(upstream, normed, scale):
    mean = jnp.mean(upstream, axis=-1, keepdims=True)
    along = jnp.mean(upstream * normed, axis=-1, keepdims=True)
    return scale * (upstream - mean - normed * along)


def max_tiles(local_len):
    count = 1
    while (count // 2) * 314 + (count % 2) * 64 <= local_len + LEN_LONG - 2:
        count += 1
    return count


def fold_rows(values):
    return jnp.sum(values.reshape(values.shape[0] // 8, 8, values.shape[1]), axis=0)


def plan_tiles(lengths, table, row, tiles):
    slots = lengths.shape[1]
    local_len = tiles[1]
    low = lax.axis_index("seq") * local_len
    high = low + local_len
    base = row * (tiles[0] + 1) * ENTRIES

    def step(k, carry):
        begin, count, tile_begin, in_tile, fitted_end = carry
        true_end = begin + lengths[row, k]
        end = jnp.minimum(true_end, SEQ_LEN)
        touches = (end > low) & (begin < high) & (end > begin)
        fresh = touches & ((count == 0) | (end - tile_begin > TILE))
        count = jnp.where(fresh, count + 1, count)
        tile_begin = jnp.where(fresh, begin, tile_begin)
        in_tile = jnp.where(fresh, 0, in_tile + 1)

        @pl.when(touches)
        def _():
            spot = base + (count - 1) * ENTRIES
            table[spot] = tile_begin - low + HALO
            for j in range(4):

                @pl.when(j >= in_tile)
                def _():
                    table[spot + 1 + j] = end - tile_begin

        fitted_end = jnp.where(true_end <= SEQ_LEN, true_end, fitted_end)
        return (end, count, tile_begin, in_tile, fitted_end)

    zero = jnp.int32(0)
    for b in range(tiles[0]):
        table[base + b * ENTRIES] = 0
    _, count, _, _, fitted_end = lax.fori_loop(0, slots, step, (zero, zero, zero, zero, zero))
    table[base + tiles[0] * ENTRIES] = count
    table[base + tiles[0] * ENTRIES + 1] = fitted_end
    return count


def tile_fills(table, spot):
    def segments(positions):
        return sum((positions >= table[spot + 1 + j]).astype(jnp.int32) for j in range(4))

    seg = segments(lax.broadcasted_iota(jnp.int32, (TILE, 128), 0))
    lane = lax.broadcasted_iota(jnp.int32, (TILE, 128), 1) % E
    same = seg == lane
    one_hot = jnp.where(same, 1.0, 0.0)
    across = jnp.where(same, 0.0, NEGATIVE)
    keys = jnp.where(lane < 5, across, jnp.where(lane < 8, 1.0, 0.0))
    return one_hot, keys


def project_kernel(tokens, w_qkv, gain, projected, normed_t):
    normed, _ = normalize(tokens[...].astype(F32))
    low = (normed * gain[...]).astype(BF16)
    normed_t[...] = low.T
    projected[...] = jnp.dot(low, w_qkv[...], preferred_element_type=F32).astype(BF16)


def project(tokens, w_qkv, gain):
    count, width = tokens.shape
    wide = w_qkv.shape[1]
    block = 2 * BLOCK
    return pl.pallas_call(
        project_kernel,
        grid=(count // block,),
        out_shape=(
            jax.ShapeDtypeStruct((count, wide), BF16),
            jax.ShapeDtypeStruct((width, count), BF16),
        ),
        in_specs=[
            pl.BlockSpec((block, width), lambda i: (i, 0)),
            whole_spec(width, wide),
            whole_spec(1, width),
        ],
        out_specs=(
            pl.BlockSpec((block, wide), lambda i: (i, 0)),
            pl.BlockSpec((width, block), lambda i: (0, i)),
        ),
        compiler_params=pltpu.CompilerParams(vmem_limit_bytes=40 * MIB),
        name="project",
    )(tokens, w_qkv, gain)


def attend_forward_kernel(
    tiles, lengths, local, left, right, w_qkv, gain, mixed, packed, fills, table,
    spread, out, hot, stage, stage_fill, sems,
):
    row = pl.program_id(0)
    local_len = local.shape[0]
    count = plan_tiles(lengths, table, row, tiles)
    for side, tokens in enumerate((left, right)):
        normed = layer_norm(tokens[0].astype(F32), gain[...]).astype(BF16)
        made = jnp.dot(normed, w_qkv[...], preferred_element_type=F32).astype(BF16)
        start = side * (HALO + local_len)
        for c in range(12):
            spread[c, start : start + HALO, :] = made[:, c * 128 : (c + 1) * 128].astype(F32)
    for c in range(12):
        spread[c, HALO : HALO + local_len, :] = local[:, c * 128 : (c + 1) * 128].astype(F32)
    low = lax.broadcasted_iota(jnp.int32, (TILE, 128), 1) < E
    place = lax.broadcasted_iota(jnp.int32, (TILE, 128), 1) % E

    def stores(slot, at):
        return (
            pltpu.make_async_copy(stage.at[slot], packed.at[at], sems.at[0, slot]),
            pltpu.make_async_copy(stage_fill.at[slot], fills.at[at], sems.at[1, slot]),
        )

    def one_tile(b, _):
        spot = (row * (tiles[0] + 1) + b) * ENTRIES
        begin = table[spot]
        slot = lax.rem(b, 2)
        at = row * tiles[0] + b

        @pl.when(b >= 2)
        def _():
            for copy in stores(slot, at - 2):
                copy.wait()

        one_hot, key_fill = tile_fills(table, spot)
        hot[...] = one_hot
        stage_fill[slot, 4] = key_fill.astype(BF16)
        for pair in range(4):
            q = spread[pair, pl.ds(begin, TILE), :].astype(BF16)
            k = spread[4 + pair, pl.ds(begin, TILE), :].astype(BF16)
            v = spread[8 + pair, pl.ds(begin, TILE), :].astype(BF16)
            stage[slot, pair] = q
            stage[slot, 4 + pair] = k
            stage[slot, 8 + pair] = v
            fill_q, fill_k = hot[...].astype(BF16), stage_fill[slot, 4]
            zero = jnp.zeros_like(v)
            made, peaks = 0.0, []
            for side in range(2):
                own = low if side == 0 else ~low
                scores = lax.dot_general(
                    jnp.where(own, q, fill_q),
                    jnp.where(own, k, fill_k),
                    NT,
                    preferred_element_type=F32,
                )
                peak = jnp.max(scores, axis=1, keepdims=True)
                weights = jnp.exp2((scores - peak) * SCALE2).astype(BF16)
                both = jnp.concatenate([jnp.where(own, v, zero), jnp.where(own, zero + 1, zero)], axis=1)
                made += jnp.dot(weights, both, preferred_element_type=F32)
                peaks.append(peak)
            total = made[:, 128:]
            out[pair, pl.ds(begin, TILE), :] = made[:, :128] / total
            total = pltpu.roll(total, E, 1)
            log_sum = jnp.where(low, peaks[1], peaks[0]) + jnp.log2(total) * (1.0 / SCALE2)
            first = log_sum.astype(BF16).astype(F32)
            rest = log_sum - first
            second = rest.astype(BF16).astype(F32)
            fill = jnp.where(place == 7, second - rest, hot[...])
            fill = jnp.where(place == 6, -second, fill)
            stage_fill[slot, pair] = jnp.where(place == 5, -first, fill).astype(BF16)
        for copy in stores(slot, at):
            copy.start()
        return 0

    lax.fori_loop(0, count, one_tile, 0)
    for c in range(4):
        mixed[:, c * 128 : (c + 1) * 128] = out[c, HALO : HALO + local_len, :].astype(BF16)

    @pl.when(count >= 2)
    def _():
        for copy in stores(lax.rem(count, 2), row * tiles[0] + count - 2):
            copy.wait()

    for copy in stores(lax.rem(count + 1, 2), row * tiles[0] + count - 1):
        copy.wait()


def attend_forward(lengths, local, left, right, w_qkv, gain):
    rows = lengths.shape[0]
    width = left.shape[2]
    local_len = local.shape[0] // rows
    most = max_tiles(local_len)
    held = local_len + 2 * HALO
    return pl.pallas_call(
        functools.partial(attend_forward_kernel, (most, local_len)),
        grid=(rows,),
        out_shape=(
            jax.ShapeDtypeStruct((rows * local_len, width), BF16),
            jax.ShapeDtypeStruct((rows * most, 12, TILE, 128), BF16),
            jax.ShapeDtypeStruct((rows * most, 5, TILE, 128), BF16),
            jax.ShapeDtypeStruct((rows * (most + 1) * ENTRIES,), jnp.int32),
        ),
        in_specs=[
            smem_spec(),
            pl.BlockSpec((local_len, 3 * width), lambda r: (r, 0)),
            row_spec(HALO, width),
            row_spec(HALO, width),
            whole_spec(width, 3 * width),
            whole_spec(1, width),
        ],
        out_specs=(
            pl.BlockSpec((local_len, width), lambda r: (r, 0)),
            pl.BlockSpec(memory_space=pl.ANY),
            pl.BlockSpec(memory_space=pl.ANY),
            smem_spec(),
        ),
        scratch_shapes=[
            pltpu.VMEM((12, held, 128), F32),
            pltpu.VMEM((4, held, 128), F32),
            pltpu.VMEM((TILE, 128), F32),
            pltpu.VMEM((2, 12, TILE, 128), BF16),
            pltpu.VMEM((2, 5, TILE, 128), BF16),
            pltpu.SemaphoreType.DMA((2, 2)),
        ],
        compiler_params=pltpu.CompilerParams(vmem_limit_bytes=56 * MIB),
        name="attend_forward",
    )(lengths, local, left, right, w_qkv, gain)


def mlp_kernel(
    tiles, table, tokens, mixed, cotangent, w_out, w_up, w_down, gain,
    output, activated, d_hidden, d_resid, d_attn, d_mixed, normed_t, mixed_t, cotangent_t, grad_gain,
):
    step = pl.program_id(0)
    most, local_len = tiles
    block = tokens.shape[0]
    per_row = local_len // block
    row = step // per_row
    begin = lax.axis_index("seq") * local_len + (step % per_row) * block
    positions = begin + lax.broadcasted_iota(jnp.int32, (block, 1), 0)
    valid = positions < table[(row * (most + 1) + most) * ENTRIES + 1]
    attn = jnp.dot(mixed[...], w_out[...], preferred_element_type=F32)
    resid = tokens[...].astype(F32) + jnp.where(valid, attn, 0.0)
    normed, scale = normalize(resid)
    low = (normed * gain[...]).astype(BF16)
    normed_t[...] = low.T
    mixed_t[...] = mixed[...].T
    dy = cotangent[...]
    cotangent_t[...] = dy.T
    piece = 512
    dense, d_normed = resid, 0.0
    for j in range(w_up.shape[1] // piece):
        columns = slice(j * piece, (j + 1) * piece)
        hidden = jnp.dot(low, w_up[:, columns], preferred_element_type=F32)
        square = hidden * hidden
        bent = jnp.tanh(hidden * (GELU_A + (GELU_A * GELU_B) * square))
        half = 0.5 + 0.5 * bent
        act = (hidden * half).astype(BF16)
        slope = half + (0.5 - 0.5 * bent * bent) * hidden * (GELU_A + (3.0 * GELU_A * GELU_B) * square)
        d_act = lax.dot_general(dy, w_down[columns, :], NT, preferred_element_type=F32)
        grad = (d_act * slope).astype(BF16)
        activated[:, columns] = act
        d_hidden[:, columns] = grad
        dense += jnp.dot(act, w_down[columns, :], preferred_element_type=F32)
        d_normed += lax.dot_general(grad, w_up[:, columns], NT, preferred_element_type=F32)
    output[...] = dense.astype(BF16)

    @pl.when(step == 0)
    def _():
        grad_gain[...] = jnp.zeros_like(grad_gain)

    grad_gain[...] += fold_rows(d_normed * normed)
    made = dy.astype(F32) + normalize_back(d_normed * gain[...], normed, scale)
    d_resid[...] = made
    attn_low = jnp.where(valid, made, 0.0).astype(BF16)
    d_attn[...] = attn_low
    d_mixed[...] = lax.dot_general(attn_low, w_out[...], NT, preferred_element_type=F32).astype(BF16)


def mlp(local_len, table, tokens, mixed, cotangent, w_out, w_up, w_down, gain):
    count, width = tokens.shape
    hidden = w_up.shape[1]
    rows_of = lambda w: pl.BlockSpec((BLOCK, w), lambda i: (i, 0))
    turned = pl.BlockSpec((width, BLOCK), lambda i: (0, i))
    shape = jax.ShapeDtypeStruct
    return pl.pallas_call(
        functools.partial(mlp_kernel, (max_tiles(local_len), local_len)),
        grid=(count // BLOCK,),
        out_shape=(
            shape((count, width), BF16),
            shape((count, hidden), BF16),
            shape((count, hidden), BF16),
            shape((count, width), F32),
            shape((count, width), BF16),
            shape((count, width), BF16),
            shape((width, count), BF16),
            shape((width, count), BF16),
            shape((width, count), BF16),
            shape((8, width), F32),
        ),
        in_specs=[
            smem_spec(),
            rows_of(width),
            rows_of(width),
            rows_of(width),
            whole_spec(width, width),
            whole_spec(width, hidden),
            whole_spec(hidden, width),
            whole_spec(1, width),
        ],
        out_specs=(
            rows_of(width),
            rows_of(hidden),
            rows_of(hidden),
            rows_of(width),
            rows_of(width),
            rows_of(width),
            turned,
            turned,
            turned,
            whole_spec(8, width),
        ),
        compiler_params=pltpu.CompilerParams(vmem_limit_bytes=56 * MIB),
        name="mlp",
    )(table, tokens, mixed, cotangent, w_out, w_up, w_down, gain)


def tile_backward(packed, fills, grad_of, put):
    low = lax.broadcasted_iota(jnp.int32, (TILE, 128), 1) < E
    for pair in range(4):
        q, k, v, o = packed(pair), packed(4 + pair), packed(8 + pair), grad_of(pair)
        fill_q, fill_k = fills(pair), fills(4)
        zero = jnp.zeros_like(q)
        dq, dk, dv = 0.0, 0.0, 0.0
        for side in range(2):
            own = low if side == 0 else ~low
            own_o = jnp.where(own, o, zero)
            scores = lax.dot_general(
                jnp.where(own, k, fill_k), jnp.where(own, q, fill_q), NT, preferred_element_type=F32
            )
            probs = jnp.exp2(scores * SCALE2)
            d_probs = lax.dot_general(v, own_o, NT, preferred_element_type=F32)
            weighted = probs * d_probs
            inner = jnp.sum(weighted, axis=0, keepdims=True)
            d_scores = (weighted - probs * inner).astype(BF16)
            dq += lax.dot_general(d_scores, jnp.where(own, k, zero), TN, preferred_element_type=F32)
            dk += jnp.dot(d_scores, jnp.where(own, q, zero), preferred_element_type=F32)
            dv += jnp.dot(probs.astype(BF16), own_o, preferred_element_type=F32)
        put(pair, (dq * 0.125).astype(BF16))
        put(4 + pair, (dk * 0.125).astype(BF16))
        put(8 + pair, dv.astype(BF16))


def attend_backward_kernel(tiles, table, packed, fills, grad, left, right, made, d_out):
    row, b = pl.program_id(0), pl.program_id(1)
    local_len = tiles[1]

    @pl.when(b == 0)
    def _():
        for c in range(4):
            columns = slice(c * 128, (c + 1) * 128)
            d_out[c, :HALO, :] = left[0, :, columns].astype(F32)
            d_out[c, HALO : HALO + local_len, :] = grad[:, columns].astype(F32)
            d_out[c, HALO + local_len :, :] = right[0, :, columns].astype(F32)

    begin = table[(row * (tiles[0] + 1) + b) * ENTRIES]
    count = table[(row * (tiles[0] + 1) + tiles[0]) * ENTRIES]

    @pl.when(b < count)
    def _():
        def put(c, values):
            made[0, c] = values

        tile_backward(
            lambda c: packed[0, c],
            lambda c: fills[0, c],
            lambda c: d_out[c, pl.ds(begin, TILE), :].astype(BF16),
            put,
        )


def attend_backward(rows, table, packed, fills, grad, left, right):
    local_len, width = grad.shape[0] // rows, grad.shape[1]
    most = max_tiles(local_len)
    held = local_len + 2 * HALO
    tile = lambda n: pl.BlockSpec((1, n, TILE, 128), lambda r, b: (r * most + b, 0, 0, 0))
    halo = pl.BlockSpec((1, HALO, width), lambda r, b: (r, 0, 0))
    return pl.pallas_call(
        functools.partial(attend_backward_kernel, (most, local_len)),
        grid=(rows, most),
        out_shape=jax.ShapeDtypeStruct(packed.shape, BF16),
        in_specs=[
            smem_spec(),
            tile(12),
            tile(5),
            pl.BlockSpec((local_len, width), lambda r, b: (r, 0)),
            halo,
            halo,
        ],
        out_specs=tile(12),
        scratch_shapes=[pltpu.VMEM((4, held, 128), F32)],
        compiler_params=pltpu.CompilerParams(vmem_limit_bytes=56 * MIB),
        name="attend_backward",
    )(table, packed, fills, grad, left, right)


def input_back_kernel(
    tiles, table, tokens, made, d_resid, normed_t, w_qkv, gain, grad_tokens, grad_qkv, grad_gain, spread, total
):
    row = pl.program_id(0)
    most, local_len = tiles
    count = table[(row * (most + 1) + most) * ENTRIES]

    def place(b, _):
        begin = table[(row * (most + 1) + b) * ENTRIES]
        for c in range(12):
            spread[c, pl.ds(begin, TILE), :] = made[b, c].astype(F32)
        return 0

    lax.fori_loop(0, count, place, 0)
    piece = BLOCK
    gain_sum = jnp.zeros(grad_gain.shape, F32)
    for i in range(local_len // piece):
        at = slice(i * piece, (i + 1) * piece)
        d_projected = jnp.concatenate(
            [spread[c, HALO + i * piece : HALO + (i + 1) * piece, :].astype(BF16) for c in range(12)], axis=1
        )
        d_normed = lax.dot_general(d_projected, w_qkv[...], NT, preferred_element_type=F32)
        normed, scale = normalize(tokens[at, :].astype(F32))
        gain_sum += fold_rows(d_normed * normed)
        back = normalize_back(d_normed * gain[...], normed, scale)
        grad_tokens[at, :] = (d_resid[at, :] + back).astype(BF16)

    @pl.when(row == 0)
    def _():
        grad_gain[...] = gain_sum

    @pl.when(row > 0)
    def _():
        grad_gain[...] += gain_sum

    last = row == pl.num_programs(0) - 1
    for c in range(6):
        both = jnp.concatenate(
            [spread[2 * c + i, HALO : HALO + local_len, :].astype(BF16) for i in range(2)], axis=1
        )
        part = jnp.dot(normed_t[...], both, preferred_element_type=F32)
        columns = slice(c * 256, (c + 1) * 256)

        @pl.when(row == 0)
        def _():
            total[:, columns] = part

        @pl.when(row > 0)
        def _():
            total[:, columns] += part

    @pl.when(last)
    def _():
        grad_qkv[...] = total[...].astype(BF16)


def input_back(rows, table, tokens, made, d_resid, normed_t, w_qkv, gain):
    local_len, width = tokens.shape[0] // rows, tokens.shape[1]
    most = max_tiles(local_len)
    held = local_len + 2 * HALO
    wide = w_qkv.shape[1]
    row_block = pl.BlockSpec((local_len, width), lambda r: (r, 0))
    return pl.pallas_call(
        functools.partial(input_back_kernel, (most, local_len)),
        grid=(rows,),
        out_shape=(
            jax.ShapeDtypeStruct(tokens.shape, BF16),
            jax.ShapeDtypeStruct((width, wide), BF16),
            jax.ShapeDtypeStruct((8, width), F32),
        ),
        in_specs=[
            smem_spec(),
            row_block,
            pl.BlockSpec((most, 12, TILE, 128), lambda r: (r, 0, 0, 0)),
            row_block,
            pl.BlockSpec((width, local_len), lambda r: (0, r)),
            whole_spec(width, wide),
            whole_spec(1, width),
        ],
        out_specs=(row_block, whole_spec(width, wide), whole_spec(8, width)),
        scratch_shapes=[pltpu.VMEM((12, held, 128), F32), pltpu.VMEM((width, wide), F32)],
        compiler_params=pltpu.CompilerParams(vmem_limit_bytes=60 * MIB),
        name="input_back",
    )(table, tokens, made, d_resid, normed_t, w_qkv, gain)


def row_spec(*shape):
    return pl.BlockSpec((1,) + shape, lambda r: (r,) + (0,) * len(shape))


def whole_spec(*shape):
    return pl.BlockSpec(shape, lambda r: (0,) * len(shape))


def smem_spec():
    return pl.BlockSpec(memory_space=pltpu.SMEM)


def exchange(values, devices):
    before = lax.ppermute(values[:, -HALO:], "seq", [(i, i + 1) for i in range(devices - 1)])
    after = lax.ppermute(values[:, :HALO], "seq", [(i + 1, i) for i in range(devices - 1)])
    return before, after


def sum_plan(devices):
    dp, seq = devices
    chip = [("dp", 1 << b) for b in range(1, dp.bit_length() - 1)]
    core = [("dp", 1)]
    along = [("seq", 1 << b) for b in range(seq.bit_length() - 1)]
    return [core + chip + along, core + chip[::-1] + along]


def sum_kernel(devices, grads, gains, outs, gains_out, work, slots, done, gain_slots, sems):
    load_sem, store_sem, send_sem, recv_sem, gain_send, gain_recv = sems
    plans = sum_plan(devices)
    steps = len(plans[0])
    chunks = 2 * PIPELINED
    size = work.shape[0] // chunks
    here = {"dp": lax.axis_index("dp"), "seq": lax.axis_index("seq")}

    def other(axis, bit):
        mine = (here[axis] // bit) % 2
        return mine, {axis: here[axis] + bit - 2 * bit * mine}

    barrier = pltpu.get_barrier_semaphore()
    for axis, bit in plans[0]:
        pl.semaphore_signal(barrier, inc=1, device_id=other(axis, bit)[1], device_id_type=MESH)

    pieces = []
    for k, ref in enumerate(grads):
        for c in range(ref.shape[1] // 128):
            pieces.append((k, c, ref.shape[0]))
    loads, stores, at = [[] for _ in range(chunks)], [[] for _ in range(chunks)], 0
    for k, c, rows in pieces:
        inside, summed = work.at[at : at + rows], done.at[at : at + rows]
        chunk = at // size
        loads[chunk].append(
            pltpu.make_async_copy(grads[k].at[:, c * 128 : (c + 1) * 128], inside, load_sem.at[len(loads[chunk]), chunk])
        )
        stores[chunk].append(
            pltpu.make_async_copy(summed, outs[k].at[:, c * 128 : (c + 1) * 128], store_sem.at[len(stores[chunk]), chunk])
        )
        at += rows
    for chunk in range(chunks):
        for copy in loads[chunk]:
            copy.start()
    pl.semaphore_wait(barrier, steps)

    def place(offset, rows):
        return pl.ds(pl.multiple_of(offset, rows), rows)

    def add(offset, slot, rows, into):
        block = min(rows, 256)

        @pl.loop(0, rows // block)
        def _(i):
            mine = work[pl.ds(pl.multiple_of(offset + i * block, block), block), :].astype(F32)
            theirs = slots[pl.ds(pl.multiple_of(slot + i * block, block), block), :].astype(F32)
            into[pl.ds(pl.multiple_of(offset + i * block, block), block), :] = (mine + theirs).astype(BF16)

    def chunk_events(chunk):
        plan = plans[chunk % 2]
        state = {"offset": chunk * size, "rows": size, "slot": chunk * size, "path": []}

        def halve_start(s):
            mine, target = other(*plan[s])
            half = state["rows"] // 2
            keep = state["offset"] + mine * half
            give = state["offset"] + (1 - mine) * half
            copy = pltpu.make_async_remote_copy(
                src_ref=work.at[place(give, half)],
                dst_ref=slots.at[place(state["slot"], half)],
                send_sem=send_sem.at[chunk, s],
                recv_sem=recv_sem.at[chunk, s],
                device_id=target,
                device_id_type=MESH,
            )
            copy.start()
            state["path"].append((keep, give, half))
            state["copy"] = copy

        def halve_end(s):
            keep, _, half = state["path"][s]
            state["copy"].wait()
            add(keep, state["slot"], half, done if s + 1 == steps else work)
            state.update(offset=keep, rows=half, slot=state["slot"] + half)

        def double_start(s):
            _, target = other(*plan[s])
            keep, give, half = state["path"][s]

            def copy_of(offset):
                return pltpu.make_async_remote_copy(
                    src_ref=done.at[place(offset, half)],
                    dst_ref=done.at[place(offset, half)],
                    send_sem=send_sem.at[chunk, steps + s],
                    recv_sem=recv_sem.at[chunk, steps + s],
                    device_id=target,
                    device_id_type=MESH,
                )

            copy_of(keep).start()
            state["copies"] = (copy_of(keep), copy_of(give))

        def double_end(s):
            state["copies"][0].wait_send()
            state["copies"][1].wait_recv()

        def first():
            for copy in loads[chunk]:
                copy.wait()
            halve_start(0)

        def turn(t):
            if t < steps:
                halve_end(t)
            else:
                double_end(2 * steps - 1 - t)
            if t + 1 < steps:
                halve_start(t + 1)
            elif t + 1 < 2 * steps:
                double_start(2 * steps - 2 - t)
            else:
                for copy in stores[chunk]:
                    copy.start()

        return [first] + [functools.partial(turn, t) for t in range(2 * steps)]

    def gain_events():
        plan = plans[0]
        state = {}

        def start(s):
            copy = pltpu.make_async_remote_copy(
                src_ref=gain_slots.at[2 * s],
                dst_ref=gain_slots.at[2 * s + 1],
                send_sem=gain_send.at[s],
                recv_sem=gain_recv.at[s],
                device_id=other(*plan[s])[1],
                device_id_type=MESH,
            )
            copy.start()
            state["copy"] = copy

        def first():
            gain_slots[0] = gains[...]
            start(0)

        def turn(s):
            state["copy"].wait()
            total = gain_slots[2 * s] + gain_slots[2 * s + 1]
            if s + 1 < steps:
                gain_slots[2 * s + 2] = total
                start(s + 1)
            else:
                gains_out[...] = total

        return [first] + [functools.partial(turn, s) for s in range(steps)]

    runs = [(chunk // 2, chunk_events(chunk)) for chunk in range(chunks)]
    runs.append((0, gain_events()))
    last = max(lag + len(events) for lag, events in runs)
    for t in range(last):
        for lag, events in runs:
            if 0 <= t - lag < len(events):
                events[t - lag]()
    for chunk in range(chunks):
        for copy in stores[chunk]:
            copy.wait()


def sum_grads(devices, grads, gains):
    count = len(grads)
    total_rows = sum(g.shape[0] * g.shape[1] // 128 for g in grads)
    steps = len(sum_plan(devices)[0])
    chunks = 2 * PIPELINED

    def kernel(*refs):
        ins, rest = refs[:count], refs[count:]
        gain_ref, outs, rest = rest[0], rest[1 : 1 + count], rest[1 + count :]
        sum_kernel(devices, ins, gain_ref, outs, *rest[:5], rest[5:])

    any_spec = pl.BlockSpec(memory_space=pl.ANY)
    vmem = pl.BlockSpec(memory_space=pltpu.VMEM)
    made = pl.pallas_call(
        kernel,
        out_shape=[jax.ShapeDtypeStruct(g.shape, BF16) for g in grads]
        + [jax.ShapeDtypeStruct(gains.shape, F32)],
        in_specs=[any_spec] * count + [vmem],
        out_specs=[any_spec] * count + [vmem],
        scratch_shapes=[
            pltpu.VMEM((total_rows, 128), BF16),
            pltpu.VMEM((total_rows, 128), BF16),
            pltpu.VMEM((total_rows, 128), BF16),
            pltpu.VMEM((2 * steps,) + gains.shape, F32),
            pltpu.SemaphoreType.DMA((8, chunks)),
            pltpu.SemaphoreType.DMA((8, chunks)),
            pltpu.SemaphoreType.DMA((chunks, 2 * steps)),
            pltpu.SemaphoreType.DMA((chunks, 2 * steps)),
            pltpu.SemaphoreType.DMA((steps,)),
            pltpu.SemaphoreType.DMA((steps,)),
        ],
        compiler_params=pltpu.CompilerParams(
            collective_id=0, has_side_effects=True, vmem_limit_bytes=40 * MIB
        ),
        name="sum_grads",
    )(*grads, gains)
    return made[:count], made[count]


def body(
    devices, tokens, item_lengths, w_qkv, w_out, w_up, w_down, gain_one, gain_two, cotangent
):
    rows, local_len, width = tokens.shape
    count = rows * local_len
    gain_one, gain_two = gain_one.reshape(1, width), gain_two.reshape(1, width)
    flat = tokens.reshape(count, width)
    left, right = exchange(tokens, devices[1])
    projected, normed_one_t = project(flat, w_qkv, gain_one)
    mixed, packed, fills, table = attend_forward(item_lengths, projected, left, right, w_qkv, gain_one)
    (
        output, activated, d_hidden, d_resid, d_attn, d_mixed, normed_two_t, mixed_t, cotangent_t, grad_gain_two
    ) = mlp(local_len, table, flat, mixed, cotangent.reshape(count, width), w_out, w_up, w_down, gain_two)
    d_left, d_right = exchange(d_mixed.reshape(rows, local_len, width), devices[1])
    grad_down = jnp.dot(cotangent_t, activated, preferred_element_type=F32).astype(BF16).T
    grad_up = jnp.dot(normed_two_t, d_hidden, preferred_element_type=F32).astype(BF16)
    grad_out = jnp.dot(mixed_t, d_attn, preferred_element_type=F32).astype(BF16)
    made = attend_backward(rows, table, packed, fills, d_mixed, d_left, d_right)
    grad_tokens, grad_qkv, grad_gain_one = input_back(
        rows, table, flat, made, d_resid, normed_one_t, w_qkv, gain_one
    )
    gains = jnp.concatenate([grad_gain_one, grad_gain_two])
    summed, gains = sum_grads(devices, [grad_qkv, grad_out, grad_up, grad_down], gains)
    grads = tuple(g.astype(F32) for g in summed)
    gains = jnp.sum(gains.reshape(2, 8, width), axis=1)
    placed = (output.reshape(tokens.shape), grad_tokens.reshape(tokens.shape))
    return placed + grads + (gains[0], gains[1])


def solution(mesh):
    rows = P("dp", "seq", None)
    placed = (rows, P("dp", None), P(), P(), P(), P(), P(), P(), rows)
    return jax.shard_map(
        functools.partial(body, (mesh.shape["dp"], mesh.shape["seq"])),
        mesh=mesh,
        in_specs=placed,
        out_specs=(rows, rows, P(), P(), P(), P(), P(), P()),
        check_vma=False,
    )
```

```python
import functools

import jax
import jax.numpy as jnp
from jax import lax
from jax.experimental import pallas as pl
from jax.experimental.pallas import tpu as pltpu
from jax.sharding import PartitionSpec as P

H = 8
E = 64
SEQ_LEN = 4096
LEN_LONG = 250
HALO = 256
TILE = 256
ENTRIES = 8
BLOCK = 256
PIECE = 512
WINDOW = 64
GROUPS = 2
EVERY = 4

EPSILON = 1e-05
NEGATIVE = -1e30
SCALE2 = 0.125 * 1.4426950408889634
GELU_A = 0.7978845608028654
GELU_B = 0.044715
MIB = 2**20
F32 = jnp.float32
BF16 = jnp.bfloat16
NT = (((1,), (1,)), ((), ()))
TN = (((0,), (0,)), ((), ()))
MESH = pl.DeviceIdType.MESH


def layer_norm(values, scaling):
    centered = values - jnp.mean(values, axis=-1, keepdims=True)
    variance = jnp.mean(centered * centered, axis=-1, keepdims=True)
    return centered * lax.rsqrt(variance + EPSILON) * scaling


def normalize(values):
    centered = values - jnp.mean(values, axis=-1, keepdims=True)
    scale = lax.rsqrt(jnp.mean(centered * centered, axis=-1, keepdims=True) + EPSILON)
    return centered * scale, scale


def normalize_back(upstream, normed, scale):
    mean = jnp.mean(upstream, axis=-1, keepdims=True)
    along = jnp.mean(upstream * normed, axis=-1, keepdims=True)
    return scale * (upstream - mean - normed * along)


def max_tiles(local_len):
    count = 1
    while (count // 2) * 314 + (count % 2) * 64 <= local_len + LEN_LONG - 2:
        count += 1
    return count


def fold_rows(values):
    return jnp.sum(values.reshape(values.shape[0] // 8, 8, values.shape[1]), axis=0)


def plan_tiles(lengths, table, row, tiles):
    slots = lengths.shape[1]
    local_len = tiles[1]
    low = lax.axis_index("seq") * local_len
    high = low + local_len
    base = row * (tiles[0] + 1) * ENTRIES

    def step(k, carry):
        begin, count, tile_begin, in_tile, fitted_end = carry
        true_end = begin + lengths[row, k]
        end = jnp.minimum(true_end, SEQ_LEN)
        touches = (end > low) & (begin < high) & (end > begin)
        fresh = touches & ((count == 0) | (end - tile_begin > TILE))
        count = jnp.where(fresh, count + 1, count)
        tile_begin = jnp.where(fresh, begin, tile_begin)
        in_tile = jnp.where(fresh, 0, in_tile + 1)

        @pl.when(touches)
        def _():
            spot = base + (count - 1) * ENTRIES
            table[spot] = tile_begin - low + HALO
            for j in range(4):

                @pl.when(j >= in_tile)
                def _():
                    table[spot + 1 + j] = end - tile_begin

        fitted_end = jnp.where(true_end <= SEQ_LEN, true_end, fitted_end)
        return (end, count, tile_begin, in_tile, fitted_end)

    zero = jnp.int32(0)
    for b in range(tiles[0]):
        table[base + b * ENTRIES] = 0
    _, count, _, _, fitted_end = lax.fori_loop(0, slots, step, (zero, zero, zero, zero, zero))
    table[base + tiles[0] * ENTRIES] = count
    table[base + tiles[0] * ENTRIES + 1] = fitted_end
    windows = local_len // WINDOW
    unpack_from = tiles[2] * (tiles[0] + 1) * ENTRIES + row * windows * 4

    def window(w, b):
        at = HALO + w * WINDOW

        def end_of(n):
            return table[base + n * ENTRIES] + table[base + n * ENTRIES + 4]

        b = jnp.where(end_of(b) <= at, b + 1, b)
        cut = end_of(b) - at
        table[unpack_from + w * 4] = b * TILE + at - table[base + b * ENTRIES]
        table[unpack_from + w * 4 + 1] = (b + 1) * TILE - cut
        table[unpack_from + w * 4 + 2] = cut
        return b

    lax.fori_loop(0, windows, window, zero)
    return count


def tile_fills(table, spot):
    def segments(positions):
        return sum((positions >= table[spot + 1 + j]).astype(jnp.int32) for j in range(4))

    seg = segments(lax.broadcasted_iota(jnp.int32, (TILE, 128), 0))
    lane = lax.broadcasted_iota(jnp.int32, (TILE, 128), 1) % E
    same = seg == lane
    one_hot = jnp.where(same, 1.0, 0.0)
    across = jnp.where(same, 0.0, NEGATIVE)
    keys = jnp.where(lane < 5, across, jnp.where(lane < 8, 1.0, 0.0))
    return one_hot, keys


def project_kernel(tokens, w_qkv, gain, projected, normed_t):
    normed, _ = normalize(tokens[...].astype(F32))
    low = (normed * gain[...]).astype(BF16)
    normed_t[...] = low.T
    projected[...] = jnp.dot(low, w_qkv[...], preferred_element_type=F32).astype(BF16)


def project(tokens, w_qkv, gain):
    count, width = tokens.shape
    wide = w_qkv.shape[1]
    block = 2 * BLOCK
    return pl.pallas_call(
        project_kernel,
        grid=(count // block,),
        out_shape=(
            jax.ShapeDtypeStruct((count, wide), BF16),
            jax.ShapeDtypeStruct((width, count), BF16),
        ),
        in_specs=[
            pl.BlockSpec((block, width), lambda i: (i, 0)),
            whole_spec(width, wide),
            whole_spec(1, width),
        ],
        out_specs=(
            pl.BlockSpec((block, wide), lambda i: (i, 0)),
            pl.BlockSpec((width, block), lambda i: (0, i)),
        ),
        compiler_params=pltpu.CompilerParams(vmem_limit_bytes=40 * MIB),
        name="project",
    )(tokens, w_qkv, gain)


def attend_forward_kernel(
    tiles, lengths, local, left, right, w_qkv, gain, mixed, packed, table,
    spread, out, hot, stage, sems,
):
    row = pl.program_id(0)
    local_len = local.shape[0]
    count = plan_tiles(lengths, table, row, tiles)
    for side, tokens in enumerate((left, right)):
        normed = layer_norm(tokens[0].astype(F32), gain[...]).astype(BF16)
        made = jnp.dot(normed, w_qkv[...], preferred_element_type=F32).astype(BF16)
        start = side * (HALO + local_len)
        for c in range(12):
            spread[c, start : start + HALO, :] = made[:, c * 128 : (c + 1) * 128].astype(F32)
    for c in range(12):
        spread[c, HALO : HALO + local_len, :] = local[:, c * 128 : (c + 1) * 128].astype(F32)
    low = lax.broadcasted_iota(jnp.int32, (TILE, 128), 1) < E
    place = lax.broadcasted_iota(jnp.int32, (TILE, 128), 1) % E

    def store(slot, at):
        return pltpu.make_async_copy(stage.at[slot], packed.at[at], sems.at[slot])

    def one_tile(b, _):
        spot = (row * (tiles[0] + 1) + b) * ENTRIES
        begin = table[spot]
        slot = lax.rem(b, 2)
        at = row * tiles[0] + b

        @pl.when(b >= 2)
        def _():
            store(slot, at - 2).wait()

        one_hot, key_fill = tile_fills(table, spot)
        hot[...] = one_hot
        for group in range(GROUPS):
            stage[slot, group, 8] = key_fill.astype(BF16)
        for pair in range(4):
            q = spread[pair, pl.ds(begin, TILE), :].astype(BF16)
            k = spread[4 + pair, pl.ds(begin, TILE), :].astype(BF16)
            v = spread[8 + pair, pl.ds(begin, TILE), :].astype(BF16)
            group, i = pair // 2, pair % 2
            stage[slot, group, i] = q
            stage[slot, group, 2 + i] = k
            stage[slot, group, 4 + i] = v
            fill_q, fill_k = hot[...].astype(BF16), stage[slot, group, 8]
            zero = jnp.zeros_like(v)
            made, peaks = 0.0, []
            for side in range(2):
                own = low if side == 0 else ~low
                scores = lax.dot_general(
                    jnp.where(own, q, fill_q),
                    jnp.where(own, k, fill_k),
                    NT,
                    preferred_element_type=F32,
                )
                peak = jnp.max(scores, axis=1, keepdims=True)
                weights = jnp.exp2((scores - peak) * SCALE2).astype(BF16)
                both = jnp.concatenate([jnp.where(own, v, zero), jnp.where(own, zero + 1, zero)], axis=1)
                made += jnp.dot(weights, both, preferred_element_type=F32)
                peaks.append(peak)
            total = made[:, 128:]
            out[pair, pl.ds(begin, TILE), :] = made[:, :128] / total
            total = pltpu.roll(total, E, 1)
            log_sum = jnp.where(low, peaks[1], peaks[0]) + jnp.log2(total) * (1.0 / SCALE2)
            first = log_sum.astype(BF16).astype(F32)
            rest = log_sum - first
            second = rest.astype(BF16).astype(F32)
            fill = jnp.where(place == 7, second - rest, hot[...])
            fill = jnp.where(place == 6, -second, fill)
            stage[slot, group, 6 + i] = jnp.where(place == 5, -first, fill).astype(BF16)
        store(slot, at).start()
        return 0

    lax.fori_loop(0, count, one_tile, 0)
    for c in range(4):
        mixed[:, c * 128 : (c + 1) * 128] = out[c, HALO : HALO + local_len, :].astype(BF16)

    @pl.when(count >= 2)
    def _():
        store(lax.rem(count, 2), row * tiles[0] + count - 2).wait()

    store(lax.rem(count + 1, 2), row * tiles[0] + count - 1).wait()


def attend_forward(lengths, local, left, right, w_qkv, gain):
    rows = lengths.shape[0]
    width = left.shape[2]
    local_len = local.shape[0] // rows
    most = max_tiles(local_len)
    held = local_len + 2 * HALO
    return pl.pallas_call(
        functools.partial(attend_forward_kernel, (most, local_len, rows)),
        grid=(rows,),
        out_shape=(
            jax.ShapeDtypeStruct((rows * local_len, width), BF16),
            jax.ShapeDtypeStruct((rows * most, GROUPS, 9, TILE, 128), BF16),
            jax.ShapeDtypeStruct(
                (rows * (most + 1) * ENTRIES + rows * (local_len // WINDOW) * 4,), jnp.int32
            ),
        ),
        in_specs=[
            smem_spec(),
            pl.BlockSpec((local_len, 3 * width), lambda r: (r, 0)),
            row_spec(HALO, width),
            row_spec(HALO, width),
            whole_spec(width, 3 * width),
            whole_spec(1, width),
        ],
        out_specs=(
            pl.BlockSpec((local_len, width), lambda r: (r, 0)),
            pl.BlockSpec(memory_space=pl.ANY),
            smem_spec(),
        ),
        scratch_shapes=[
            pltpu.VMEM((12, held, 128), F32),
            pltpu.VMEM((4, held, 128), F32),
            pltpu.VMEM((TILE, 128), F32),
            pltpu.VMEM((2, GROUPS, 9, TILE, 128), BF16),
            pltpu.SemaphoreType.DMA((2,)),
        ],
        compiler_params=pltpu.CompilerParams(vmem_limit_bytes=56 * MIB),
        name="attend_forward",
    )(lengths, local, left, right, w_qkv, gain)


def mlp_kernel(
    tiles, table, tokens, mixed, cotangent, w_out, w_up, w_down, gain,
    output, activated, d_hidden, d_resid, d_attn, d_mixed, normed_t, mixed_t, cotangent_t, grad_gain,
):
    step = pl.program_id(0)
    most, local_len = tiles
    block = tokens.shape[0]
    per_row = local_len // block
    row = step // per_row
    begin = lax.axis_index("seq") * local_len + (step % per_row) * block
    positions = begin + lax.broadcasted_iota(jnp.int32, (block, 1), 0)
    valid = positions < table[(row * (most + 1) + most) * ENTRIES + 1]
    attn = jnp.dot(mixed[...], w_out[...], preferred_element_type=F32)
    resid = tokens[...].astype(F32) + jnp.where(valid, attn, 0.0)
    normed, scale = normalize(resid)
    low = (normed * gain[...]).astype(BF16)
    normed_t[...] = low.T
    mixed_t[...] = mixed[...].T
    dy = cotangent[...]
    cotangent_t[...] = dy.T
    piece = 512
    dense, d_normed = resid, 0.0
    for j in range(w_up.shape[1] // piece):
        columns = slice(j * piece, (j + 1) * piece)
        hidden = jnp.dot(low, w_up[:, columns], preferred_element_type=F32)
        square = hidden * hidden
        bent = jnp.tanh(hidden * (GELU_A + (GELU_A * GELU_B) * square))
        half = 0.5 + 0.5 * bent
        act = (hidden * half).astype(BF16)
        slope = half + (0.5 - 0.5 * bent * bent) * hidden * (GELU_A + (3.0 * GELU_A * GELU_B) * square)
        d_act = lax.dot_general(dy, w_down[columns, :], NT, preferred_element_type=F32)
        grad = (d_act * slope).astype(BF16)
        for part in range(piece // 256):
            activated[j * (piece // 256) + part] = act[:, part * 256 : (part + 1) * 256]
            d_hidden[j * (piece // 256) + part] = grad[:, part * 256 : (part + 1) * 256]
        dense += jnp.dot(act, w_down[columns, :], preferred_element_type=F32)
        d_normed += lax.dot_general(grad, w_up[:, columns], NT, preferred_element_type=F32)
    output[...] = dense.astype(BF16)

    @pl.when(step == 0)
    def _():
        grad_gain[...] = jnp.zeros_like(grad_gain)

    grad_gain[...] += fold_rows(d_normed * normed)
    made = dy.astype(F32) + normalize_back(d_normed * gain[...], normed, scale)
    d_resid[...] = made
    attn_low = jnp.where(valid, made, 0.0).astype(BF16)
    for part in range(attn_low.shape[1] // 256):
        d_attn[part] = attn_low[:, part * 256 : (part + 1) * 256]
    d_mixed[...] = lax.dot_general(attn_low, w_out[...], NT, preferred_element_type=F32).astype(BF16)


def mlp(local_len, table, tokens, mixed, cotangent, w_out, w_up, w_down, gain):
    count, width = tokens.shape
    hidden = w_up.shape[1]
    rows_of = lambda w: pl.BlockSpec((BLOCK, w), lambda i: (i, 0))
    blocks_of = lambda w: pl.BlockSpec((w // 256, BLOCK, 256), lambda i: (0, i, 0))
    turned = pl.BlockSpec((width, BLOCK), lambda i: (0, i))
    shape = jax.ShapeDtypeStruct
    return pl.pallas_call(
        functools.partial(mlp_kernel, (max_tiles(local_len), local_len)),
        grid=(count // BLOCK,),
        out_shape=(
            shape((count, width), BF16),
            shape((hidden // 256, count, 256), BF16),
            shape((hidden // 256, count, 256), BF16),
            shape((count, width), F32),
            shape((width // 256, count, 256), BF16),
            shape((count, width), BF16),
            shape((width, count), BF16),
            shape((width, count), BF16),
            shape((width, count), BF16),
            shape((8, width), F32),
        ),
        in_specs=[
            smem_spec(),
            rows_of(width),
            rows_of(width),
            rows_of(width),
            whole_spec(width, width),
            whole_spec(width, hidden),
            whole_spec(hidden, width),
            whole_spec(1, width),
        ],
        out_specs=(
            rows_of(width),
            blocks_of(hidden),
            blocks_of(hidden),
            rows_of(width),
            blocks_of(width),
            rows_of(width),
            turned,
            turned,
            turned,
            whole_spec(8, width),
        ),
        compiler_params=pltpu.CompilerParams(vmem_limit_bytes=56 * MIB),
        name="mlp",
    )(table, tokens, mixed, cotangent, w_out, w_up, w_down, gain)


def tile_backward(pairs, packed, fills, grad_of, put):
    low = lax.broadcasted_iota(jnp.int32, (TILE, 128), 1) < E
    for pair in range(pairs):
        q, k, v, o = packed(pair), packed(pairs + pair), packed(2 * pairs + pair), grad_of(pair)
        fill_q, fill_k = fills(pair), fills(pairs)
        zero = jnp.zeros_like(q)
        dq, dk, dv = 0.0, 0.0, 0.0
        for side in range(2):
            own = low if side == 0 else ~low
            own_o = jnp.where(own, o, zero)
            scores = lax.dot_general(
                jnp.where(own, k, fill_k), jnp.where(own, q, fill_q), NT, preferred_element_type=F32
            )
            probs = jnp.exp2(scores * SCALE2)
            d_probs = lax.dot_general(v, own_o, NT, preferred_element_type=F32)
            weighted = probs * d_probs
            inner = jnp.sum(weighted, axis=0, keepdims=True)
            d_scores = (weighted - probs * inner).astype(BF16)
            dq += lax.dot_general(d_scores, jnp.where(own, k, zero), TN, preferred_element_type=F32)
            dk += jnp.dot(d_scores, jnp.where(own, q, zero), preferred_element_type=F32)
            dv += jnp.dot(probs.astype(BF16), own_o, preferred_element_type=F32)
        put(pair, dq * 0.125)
        put(pairs + pair, dk * 0.125)
        put(2 * pairs + pair, dv)


def row_spec(*shape):
    return pl.BlockSpec((1,) + shape, lambda r: (r,) + (0,) * len(shape))


def whole_spec(*shape):
    return pl.BlockSpec(shape, lambda r: (0,) * len(shape))


def smem_spec():
    return pl.BlockSpec(memory_space=pltpu.SMEM)


def exchange(values, devices):
    before = lax.ppermute(values[:, -HALO:], "seq", [(i, i + 1) for i in range(devices - 1)])
    after = lax.ppermute(values[:, :HALO], "seq", [(i + 1, i) for i in range(devices - 1)])
    return before, after


def sum_plan(devices):
    dp, seq = devices
    chip = [("dp", 1 << b) for b in range(1, dp.bit_length() - 1)]
    core = [("dp", 1)]
    along = [("seq", 1 << b) for b in range(seq.bit_length() - 1)]
    return [core + chip + along, core + chip[::-1] + along]


def chunk_pieces(devices):
    unit = max(1, 16 * devices[0] * devices[1] // PIECE)
    if unit == 1:
        return [4] * 8 + [5, 5, 3, 3]
    return [unit] * (48 // unit)


class GradSum:
    def __init__(self, devices, work, slots, done, send_sem, recv_sem):
        self.plans = sum_plan(devices)
        self.steps = len(self.plans[0])
        self.work, self.slots, self.done = work, slots, done
        self.send_sem, self.recv_sem = send_sem, recv_sem
        self.here = {"dp": lax.axis_index("dp"), "seq": lax.axis_index("seq")}
        self.sizes = chunk_pieces(devices)
        self.paths, self.active = [], []
        base = 0
        for chunk, pieces in enumerate(self.sizes):
            offset, rows, slot, path = base, pieces * PIECE, base, []
            for axis, bit in self.plan(chunk):
                mine, _ = self.other(axis, bit)
                rows //= 2
                keep, give = offset + mine * rows, offset + (1 - mine) * rows
                path.append((keep, give, slot, rows))
                offset, slot = keep, slot + rows
            self.paths.append(path)
            base += pieces * PIECE

    def plan(self, chunk):
        return self.plans[chunk % 2]

    def other(self, axis, bit):
        mine = (self.here[axis] // bit) % 2
        return mine, {axis: self.here[axis] + bit - 2 * bit * mine}

    def copy(self, chunk, t, source, target, to):
        return pltpu.make_async_remote_copy(
            src_ref=source,
            dst_ref=target,
            send_sem=self.send_sem.at[chunk, t],
            recv_sem=self.recv_sem.at[chunk, t],
            device_id=self.other(*to)[1],
            device_id_type=MESH,
        )

    def halving(self, chunk, s):
        _, give, slot, rows = self.paths[chunk][s]
        source = self.work.at[pl.ds(pl.multiple_of(give, 16), rows)]
        return self.copy(chunk, s, source, self.slots.at[slot : slot + rows], self.plan(chunk)[s])

    def doubling(self, chunk, s, received):
        keep, give, _, rows = self.paths[chunk][s]
        part = self.done.at[pl.ds(pl.multiple_of(give if received else keep, 16), rows)]
        return self.copy(chunk, self.steps + s, part, part, self.plan(chunk)[s])

    def add(self, chunk, s):
        keep, _, slot, rows = self.paths[chunk][s]
        into = self.done if s + 1 == self.steps else self.work
        count = next(n for n in range(1, rows) if rows % (16 * n) == 0 and rows // n <= 512)
        block = rows // count

        @pl.loop(0, count)
        def _(i):
            at = pl.ds(pl.multiple_of(keep + i * block, 16), block)
            theirs = self.slots[pl.ds(pl.multiple_of(slot + i * block, 16), block), :]
            into[at, :] = (self.work[at, :].astype(F32) + theirs.astype(F32)).astype(BF16)

    def event(self, chunk, t):
        steps = self.steps
        if 0 < t <= steps:
            self.halving(chunk, t - 1).wait()
            self.add(chunk, t - 1)
        elif t > steps:
            self.doubling(chunk, 2 * steps - t, False).wait_send()
            self.doubling(chunk, 2 * steps - t, True).wait_recv()
        if t < steps:
            self.halving(chunk, t).start()
        elif t < 2 * steps:
            self.doubling(chunk, 2 * steps - 1 - t, False).start()
        return t == 2 * steps

    def begin(self, chunks):
        for chunk in chunks:
            self.event(chunk, 0)
            self.active.append([chunk, 1])

    def advance(self, finish):
        for entry in list(self.active):
            if self.event(*entry):
                finish(entry[0])
                self.active.remove(entry)
            entry[1] += 1


def backward_kernel(
    devices, tiles, table, gains, w_qkv, gain_one,
    normed_two_t, cotangent_t, mixed_t, normed_one_t, d_hidden, activated, d_attn, d_mixed, tokens, d_resid,
    packed,
    grad_tokens, grad_qkv, grad_out, grad_up, grad_down, gains_out,
    work, slots, done, left_a, left_b, right_block, halo, d_mix, tok, resid, made_tok, d_proj, bins, d_out,
    tile_in, gain_slots, gain_one_sum,
    send_sem, recv_sem, gain_send, gain_recv, halo_sem, load_sem, block_sem, tile_sem, store_sem, out_sem,
):
    most, local_len = tiles
    count = tok.shape[0]
    rows = count // local_len
    seq = lax.axis_index("seq")
    sums = GradSum(devices, work, slots, done, send_sem, recv_sem)
    steps = sums.steps

    barrier = pltpu.get_barrier_semaphore()
    after, before = seq < devices[1] - 1, seq > 0
    peers = [sums.other(axis, bit)[1] for axis, bit in sums.plans[0] if axis == "dp"]
    peers += [{"seq": lax.rem(seq + d, devices[1])} for d in range(1, devices[1])]
    for peer in peers:
        pl.semaphore_signal(barrier, inc=1, device_id=peer, device_id_type=MESH)

    load_a = lambda ref, k: pltpu.make_async_copy(ref, left_a, load_sem.at[k])
    load_b = lambda ref, k: pltpu.make_async_copy(ref, left_b, load_sem.at[k])
    load_block = lambda ref, block, slot: pltpu.make_async_copy(
        ref.at[block], right_block.at[slot], block_sem.at[slot]
    )
    load_mix = pltpu.make_async_copy(d_mixed, d_mix, load_sem.at[4])
    load_tok = pltpu.make_async_copy(tokens, tok, load_sem.at[5])
    load_resid = pltpu.make_async_copy(d_resid, resid, load_sem.at[6])
    load_a(normed_two_t, 0).start()
    load_block(d_hidden, 0, 0).start()
    load_block(d_hidden, 1, 1).start()
    load_b(cotangent_t, 1).start()
    load_mix.start()

    pl.semaphore_wait(barrier, len(peers))

    def halo_copy(side, row):
        start = row * local_len + (local_len - HALO if side == 0 else 0)
        return pltpu.make_async_remote_copy(
            src_ref=d_mixed.at[start : start + HALO],
            dst_ref=halo.at[side, row],
            send_sem=halo_sem.at[0, side, row],
            recv_sem=halo_sem.at[1, side, row],
            device_id={"seq": seq + 1 if side == 0 else seq - 1},
            device_id_type=MESH,
        )

    for side, sends, receives in ((0, after, before), (1, before, after)):

        @pl.when(sends)
        def _():
            for row in range(rows):
                halo_copy(side, row).start()

        @pl.when(jnp.logical_not(receives))
        def _():
            for row in range(rows):
                halo[side, row] = jnp.zeros(halo.shape[2:], BF16)

    homes = [(grad_up, 0, c) for c in range(16)]
    homes += [(grad_down, i * PIECE, c) for i in range(4) for c in range(4)]
    homes += [(grad_out, 0, c) for c in range(4)]
    homes += [(grad_qkv, 0, kind * 4 + 2 * g + i) for g in range(GROUPS) for kind in range(3) for i in range(2)]
    stored = []

    def store(piece):
        ref, row, c = homes[piece]
        return pltpu.make_async_copy(
            done.at[piece * PIECE : (piece + 1) * PIECE],
            ref.at[row : row + PIECE, c * 128 : (c + 1) * 128],
            out_sem.at[piece],
        )

    def finish(chunk):
        first = sum(sums.sizes[:chunk])
        for piece in range(first, first + sums.sizes[chunk]):
            store(piece).start()
            stored.append(piece)

    begun = [0]

    def ready(pieces):
        chunks = []
        while begun[0] < len(sums.sizes) and sum(sums.sizes[: begun[0] + 1]) <= pieces:
            chunks.append(begun[0])
            begun[0] += 1
        sums.begin(chunks)

    def put_columns(base, block, product):
        low = product.astype(BF16)
        for i in range(2):
            at = pl.multiple_of((base + 2 * block + i) * PIECE, PIECE)
            work[pl.ds(at, PIECE), :] = low[:, i * 128 : (i + 1) * 128]

    def put_rows(base, block, product):
        low = product.T.astype(BF16)
        for c in range(4):
            at = (base + (block // 2) * 4 + c) * PIECE + (block % 2) * 256
            work[pl.ds(pl.multiple_of(at, 256), 256), :] = low[:, c * 128 : (c + 1) * 128]

    half = d_hidden.shape[0] // 2
    runs = [
        (left_a, d_hidden, 0, half, 0, put_columns),
        (left_a, d_hidden, half, half, 0, put_columns),
        (left_b, activated, 0, half, 16, put_rows),
        (left_b, activated, half, half, 16, put_rows),
        (left_a, d_attn, 0, 2, 32, put_columns),
    ]
    waits = {0: load_a(normed_two_t, 0), 2: load_b(cotangent_t, 1), 4: load_a(mixed_t, 2)}
    at = 0
    for n, (lhs, ref, first, blocks, base, put) in enumerate(runs):
        if n in waits:
            waits[n].wait()

        def one_block(j, _, n=n, lhs=lhs, ref=ref, first=first, blocks=blocks, base=base, put=put, at=at):
            slot, later = lax.rem(at + j, 3), lax.rem(at + j + 2, 3)
            load_block(ref, first + j, slot).wait()

            @pl.when(j + 2 < blocks)
            def _():
                load_block(ref, first + j + 2, later).start()

            if n + 1 < len(runs):

                @pl.when(j + 2 >= blocks)
                def _():
                    load_block(runs[n + 1][1], runs[n + 1][2] + j + 2 - blocks, later).start()

            put(base, first + j, jnp.dot(lhs[...], right_block[slot], preferred_element_type=F32))
            return 0

        lax.fori_loop(0, blocks, one_block, 0)
        at += blocks
        if n == 1:
            load_a(mixed_t, 2).start()
        if n == 3:
            load_b(normed_one_t, 3).start()
            load_tok.start()
            load_resid.start()
        if n > 0:
            sums.advance(finish)
        if n < 4:
            ready(8 * (n + 1))

    per_group = rows * most
    total = GROUPS * per_group
    unpack_from = rows * (most + 1) * ENTRIES
    windows = local_len // WINDOW

    def load_tile(step, slot):
        group, spot = step // per_group, lax.rem(step, per_group)
        return pltpu.make_async_copy(packed.at[spot, group], tile_in.at[slot], tile_sem.at[slot])

    load_tile(0, 0).start()
    load_mix.wait()
    for side, sends, receives in ((0, after, before), (1, before, after)):

        @pl.when(sends)
        def _():
            for row in range(rows):
                halo_copy(side, row).wait_send()

        @pl.when(receives)
        def _():
            for row in range(rows):
                halo_copy(side, row).wait_recv()

    def one_tile(step, _):
        slot = lax.rem(step, 2)
        group, spot = step // per_group, lax.rem(step, per_group)
        row, b = spot // most, lax.rem(spot, most)
        load_tile(step, slot).wait()

        @pl.when(step + 1 < total)
        def _():
            load_tile(step + 1, 1 - slot).start()

        @pl.when(b == 0)
        def _():
            start = pl.multiple_of(row * local_len, local_len)
            for i in range(2):
                columns = pl.ds(pl.multiple_of((2 * group + i) * 128, 128), 128)
                d_out[i, :HALO, :] = halo[0, row, :, columns].astype(F32)
                d_out[i, HALO : HALO + local_len, :] = d_mix[pl.ds(start, local_len), columns].astype(F32)
                d_out[i, HALO + local_len :, :] = halo[1, row, :, columns].astype(F32)

        begin = table[(row * (most + 1) + b) * ENTRIES]

        def put(c, values):
            bins[c, pl.ds(pl.multiple_of(b * TILE, TILE), TILE), :] = values

        tile_backward(
            2,
            lambda c: tile_in[slot, c],
            lambda c: tile_in[slot, 6 + c],
            lambda c: d_out[c, pl.ds(begin, TILE), :].astype(BF16),
            put,
        )

        @pl.when(b == most - 1)
        def _():
            @pl.loop(0, windows)
            def _(w):
                entry = unpack_from + (row * windows + w) * 4
                one, two, cut = table[entry], table[entry + 1], table[entry + 2]
                in_one = lax.broadcasted_iota(jnp.int32, (WINDOW, 128), 0) < cut
                to = pl.multiple_of(row * local_len + w * WINDOW, WINDOW)
                for c in range(6):
                    values = jnp.where(
                        in_one, bins[c, pl.ds(one, WINDOW), :], bins[c, pl.ds(two, WINDOW), :]
                    )
                    d_proj[group * 6 + c, pl.ds(to, WINDOW), :] = values.astype(BF16)

        def qkv_gradient(g):
            for kind in range(3):
                both = jnp.concatenate([d_proj[g * 6 + 2 * kind + i] for i in range(2)], axis=1)
                product = jnp.dot(left_b[...], both, preferred_element_type=F32).astype(BF16)
                for i in range(2):
                    piece = 36 + 6 * g + 2 * kind + i
                    work[piece * PIECE : (piece + 1) * PIECE, :] = product[:, i * 128 : (i + 1) * 128]

        for k in range(total):
            ends_group = (k + 1) % per_group == 0
            moves = k % EVERY == EVERY - 1 and sums.active
            if not (ends_group or moves):
                continue

            @pl.when(step == k)
            def _():
                if moves:
                    sums.advance(finish)
                if ends_group:
                    g = k // per_group
                    if g == 0:
                        load_b(normed_one_t, 3).wait()
                    qkv_gradient(g)
                    ready(42 + 6 * g)

        return 0

    lax.fori_loop(0, total, one_tile, 0)

    load_tok.wait()
    load_resid.wait()
    gain_one_sum[...] = jnp.zeros_like(gain_one_sum)
    blocks = count // BLOCK

    def store_tok(i):
        part = pl.ds(pl.multiple_of(i * BLOCK, BLOCK), BLOCK)
        return pltpu.make_async_copy(made_tok.at[part], grad_tokens.at[part], store_sem.at[i])

    def input_block(i, _):
        part = pl.ds(pl.multiple_of(i * BLOCK, BLOCK), BLOCK)
        order = [6 * (pair // 2) + 2 * kind + pair % 2 for kind in range(3) for pair in range(4)]
        d_projected = jnp.concatenate([d_proj[c, part, :] for c in order], axis=1)
        d_normed = lax.dot_general(d_projected, w_qkv[...], NT, preferred_element_type=F32)
        normed, scale = normalize(tok[part, :].astype(F32))
        gain_one_sum[...] += fold_rows(d_normed * normed)
        back = normalize_back(d_normed * gain_one[...], normed, scale)
        made_tok[part, :] = (resid[part, :] + back).astype(BF16)
        store_tok(i).start()
        for k in range(1, blocks, 2):

            @pl.when(i == k)
            def _():
                sums.advance(finish)

        return 0

    lax.fori_loop(0, blocks, input_block, 0)

    def gain_copy(s):
        return pltpu.make_async_remote_copy(
            src_ref=gain_slots.at[2 * s],
            dst_ref=gain_slots.at[2 * s + 1],
            send_sem=gain_send.at[s],
            recv_sem=gain_recv.at[s],
            device_id=sums.other(*sums.plans[0][s])[1],
            device_id_type=MESH,
        )

    gain_slots[0, :8] = gain_one_sum[...]
    gain_slots[0, 8:] = gains[...]
    gain_copy(0).start()
    for s in range(steps):
        if sums.active:
            sums.advance(finish)
        gain_copy(s).wait()
        joined = gain_slots[2 * s] + gain_slots[2 * s + 1]
        if s + 1 < steps:
            gain_slots[2 * s + 2] = joined
            gain_copy(s + 1).start()
        else:
            gains_out[...] = joined
    while sums.active:
        sums.advance(finish)
    for i in range(blocks):
        store_tok(i).wait()
    for piece in stored:
        store(piece).wait()


def backward(
    devices, rows, table, gains, w_qkv, gain_one, normed_two_t, cotangent_t, mixed_t, normed_one_t,
    d_hidden, activated, d_attn, d_mixed, tokens, d_resid, packed,
):
    count, width = tokens.shape
    local_len = count // rows
    most = max_tiles(local_len)
    held = local_len + 2 * HALO
    hidden, wide = d_hidden.shape[0] * d_hidden.shape[2], w_qkv.shape[1]
    steps = len(sum_plan(devices)[0])
    chunks = len(chunk_pieces(devices))
    shape = jax.ShapeDtypeStruct
    anywhere = pl.BlockSpec(memory_space=pl.ANY)
    vmem = pl.BlockSpec(memory_space=pltpu.VMEM)
    dma = pltpu.SemaphoreType.DMA
    return pl.pallas_call(
        functools.partial(backward_kernel, devices, (most, local_len)),
        out_shape=(
            shape((count, width), BF16),
            shape((width, wide), BF16),
            shape((width, width), BF16),
            shape((width, hidden), BF16),
            shape((hidden, width), BF16),
            shape((16, width), F32),
        ),
        in_specs=[smem_spec(), vmem, vmem, vmem] + [anywhere] * 11,
        out_specs=(anywhere,) * 5 + (vmem,),
        scratch_shapes=[
            pltpu.VMEM((48 * PIECE, 128), BF16),
            pltpu.VMEM((48 * PIECE, 128), BF16),
            pltpu.VMEM((48 * PIECE, 128), BF16),
            pltpu.VMEM((width, count), BF16),
            pltpu.VMEM((width, count), BF16),
            pltpu.VMEM((3, count, 256), BF16),
            pltpu.VMEM((2, rows, HALO, width), BF16),
            pltpu.VMEM((count, width), BF16),
            pltpu.VMEM((count, width), BF16),
            pltpu.VMEM((count, width), F32),
            pltpu.VMEM((count, width), BF16),
            pltpu.VMEM((12, count, 128), BF16),
            pltpu.VMEM((6, most * TILE + WINDOW, 128), F32),
            pltpu.VMEM((2, held, 128), F32),
            pltpu.VMEM((2, 9, TILE, 128), BF16),
            pltpu.VMEM((2 * steps, 16, width), F32),
            pltpu.VMEM((8, width), F32),
            dma((chunks, 2 * steps)),
            dma((chunks, 2 * steps)),
            dma((steps,)),
            dma((steps,)),
            dma((2, 2, rows)),
            dma((7,)),
            dma((3,)),
            dma((2,)),
            dma((count // BLOCK,)),
            dma((48,)),
        ],
        compiler_params=pltpu.CompilerParams(
            collective_id=0, has_side_effects=True, vmem_limit_bytes=60 * MIB
        ),
        name="backward",
    )(
        table, gains, w_qkv, gain_one, normed_two_t, cotangent_t, mixed_t, normed_one_t,
        d_hidden, activated, d_attn, d_mixed, tokens, d_resid, packed,
    )


def body(
    devices, tokens, item_lengths, w_qkv, w_out, w_up, w_down, gain_one, gain_two, cotangent
):
    rows, local_len, width = tokens.shape
    count = rows * local_len
    gain_one, gain_two = gain_one.reshape(1, width), gain_two.reshape(1, width)
    flat = tokens.reshape(count, width)
    left, right = exchange(tokens, devices[1])
    projected, normed_one_t = project(flat, w_qkv, gain_one)
    mixed, packed, table = attend_forward(item_lengths, projected, left, right, w_qkv, gain_one)
    (
        output, activated, d_hidden, d_resid, d_attn, d_mixed, normed_two_t, mixed_t, cotangent_t, grad_gain_two
    ) = mlp(local_len, table, flat, mixed, cotangent.reshape(count, width), w_out, w_up, w_down, gain_two)
    grad_tokens, grad_qkv, grad_out, grad_up, grad_down, gains = backward(
        devices, rows, table, grad_gain_two, w_qkv, gain_one, normed_two_t, cotangent_t, mixed_t, normed_one_t,
        d_hidden, activated, d_attn, d_mixed, flat, d_resid, packed,
    )
    summed = (grad_qkv, grad_out, grad_up, grad_down)
    grads = tuple(g.astype(F32) for g in summed)
    gains = jnp.sum(gains.reshape(2, 8, width), axis=1)
    placed = (output.reshape(tokens.shape), grad_tokens.reshape(tokens.shape))
    return placed + grads + (gains[0], gains[1])


def solution(mesh):
    rows = P("dp", "seq", None)
    placed = (rows, P("dp", None), P(), P(), P(), P(), P(), P(), rows)
    return jax.shard_map(
        functools.partial(body, (mesh.shape["dp"], mesh.shape["seq"])),
        mesh=mesh,
        in_specs=placed,
        out_specs=(rows, rows, P(), P(), P(), P(), P(), P()),
        check_vma=False,
    )
```

```python
import functools

import jax
import jax.numpy as jnp
from jax import lax
from jax.experimental import pallas as pl
from jax.experimental.pallas import tpu as pltpu
from jax.sharding import PartitionSpec as P

H = 8
E = 64
SEQ_LEN = 4096
LEN_LONG = 250
HALO = 256
TILE = 256
ENTRIES = 8
BLOCK = 256
MLP_BLOCK = 512
PIECE = 512
WINDOW = 64
GROUPS = 2
MOVES = tuple(range(5, 36, 6))
LATE = 2
APART = 1
AHEAD = 5
BLOCKS_AHEAD = 3

EPSILON = 1e-05
NEGATIVE = -1e30
SCALE2 = 0.125 * 1.4426950408889634
GELU_A = 0.7978845608028654
GELU_B = 0.044715
MIB = 2**20
F32 = jnp.float32
BF16 = jnp.bfloat16
NT = (((1,), (1,)), ((), ()))
TN = (((0,), (0,)), ((), ()))
MESH = pl.DeviceIdType.MESH


def layer_norm(values, scaling):
    centered = values - jnp.mean(values, axis=-1, keepdims=True)
    variance = jnp.mean(centered * centered, axis=-1, keepdims=True)
    return centered * lax.rsqrt(variance + EPSILON) * scaling


def normalize(values):
    centered = values - jnp.mean(values, axis=-1, keepdims=True)
    scale = lax.rsqrt(jnp.mean(centered * centered, axis=-1, keepdims=True) + EPSILON)
    return centered * scale, scale


def normalize_back(upstream, normed, scale):
    mean = jnp.mean(upstream, axis=-1, keepdims=True)
    along = jnp.mean(upstream * normed, axis=-1, keepdims=True)
    return scale * (upstream - mean - normed * along)


def max_tiles(local_len):
    count = 1
    while (count // 2) * 314 + (count % 2) * 64 <= local_len + LEN_LONG - 2:
        count += 1
    return count


def fold_rows(values):
    return jnp.sum(values.reshape(values.shape[0] // 8, 8, values.shape[1]), axis=0)


def plan_tiles(lengths, table, row, tiles):
    slots = lengths.shape[1]
    local_len = tiles[1]
    low = lax.axis_index("seq") * local_len
    high = low + local_len
    base = row * (tiles[0] + 1) * ENTRIES

    def step(k, carry):
        begin, count, tile_begin, in_tile, fitted_end = carry
        true_end = begin + lengths[row, k]
        end = jnp.minimum(true_end, SEQ_LEN)
        touches = (end > low) & (begin < high) & (end > begin)
        fresh = touches & ((count == 0) | (end - tile_begin > TILE))
        count = jnp.where(fresh, count + 1, count)
        tile_begin = jnp.where(fresh, begin, tile_begin)
        in_tile = jnp.where(fresh, 0, in_tile + 1)

        @pl.when(touches)
        def _():
            spot = base + (count - 1) * ENTRIES
            table[spot] = tile_begin - low + HALO
            for j in range(4):

                @pl.when(j >= in_tile)
                def _():
                    table[spot + 1 + j] = end - tile_begin

        fitted_end = jnp.where(true_end <= SEQ_LEN, true_end, fitted_end)
        return (end, count, tile_begin, in_tile, fitted_end)

    zero = jnp.int32(0)
    for b in range(tiles[0]):
        table[base + b * ENTRIES] = 0
    _, count, _, _, fitted_end = lax.fori_loop(0, slots, step, (zero, zero, zero, zero, zero), unroll=5)
    table[base + tiles[0] * ENTRIES] = count
    table[base + tiles[0] * ENTRIES + 1] = fitted_end
    windows = local_len // WINDOW
    unpack_from = tiles[2] * (tiles[0] + 1) * ENTRIES + row * windows * 4

    def window(w, b):
        at = HALO + w * WINDOW

        def end_of(n):
            return table[base + n * ENTRIES] + table[base + n * ENTRIES + 4]

        b = jnp.where(end_of(b) <= at, b + 1, b)
        cut = end_of(b) - at
        table[unpack_from + w * 4] = b * TILE + at - table[base + b * ENTRIES]
        table[unpack_from + w * 4 + 1] = (b + 1) * TILE - cut
        table[unpack_from + w * 4 + 2] = cut
        return b

    lax.fori_loop(0, windows, window, zero)
    return count


def tile_fills(table, spot):
    def segments(positions):
        return sum((positions >= table[spot + 1 + j]).astype(jnp.int32) for j in range(4))

    seg = segments(lax.broadcasted_iota(jnp.int32, (TILE, 128), 0))
    lane = lax.broadcasted_iota(jnp.int32, (TILE, 128), 1) % E
    same = seg == lane
    one_hot = jnp.where(same, 1.0, 0.0)
    across = jnp.where(same, 0.0, NEGATIVE)
    keys = jnp.where(lane < 5, across, jnp.where(lane < 8, 1.0, 0.0))
    return one_hot, keys


def project_kernel(
    devices, local_len, tokens, w_qkv, gain, source, projected, normed_t, halo, zero, halo_sem, zero_sem
):
    step = pl.program_id(0)
    rows = halo.shape[1]
    seq = lax.axis_index("seq")
    after, before = seq < devices[1] - 1, seq > 0

    def halo_copy(side, row):
        start = row * local_len + (local_len - HALO if side == 0 else 0)
        return pltpu.make_async_remote_copy(
            src_ref=source.at[start : start + HALO],
            dst_ref=halo.at[side, row],
            send_sem=halo_sem.at[0, side, row],
            recv_sem=halo_sem.at[1, side, row],
            device_id={"seq": seq + 1 if side == 0 else seq - 1},
            device_id_type=MESH,
        )

    def fill(side, row):
        return pltpu.make_async_copy(zero, halo.at[side, row], zero_sem.at[side, row])

    sides = ((0, after, before), (1, before, after))

    @pl.when(step == 0)
    def _():
        barrier = pltpu.get_barrier_semaphore()
        for d in range(1, devices[1]):
            peer = {"seq": lax.rem(seq + d, devices[1])}
            pl.semaphore_signal(barrier, inc=1, device_id=peer, device_id_type=MESH)
        zero[...] = jnp.zeros_like(zero)
        pl.semaphore_wait(barrier, devices[1] - 1)
        for side, sends, receives in sides:

            @pl.when(sends)
            def _():
                for row in range(rows):
                    halo_copy(side, row).start()

            @pl.when(jnp.logical_not(receives))
            def _():
                for row in range(rows):
                    fill(side, row).start()

    normed, _ = normalize(tokens[...].astype(F32))
    low = (normed * gain[...]).astype(BF16)
    normed_t[...] = low.T
    projected[...] = jnp.dot(low, w_qkv[...], preferred_element_type=F32).astype(BF16)

    @pl.when(step == pl.num_programs(0) - 1)
    def _():
        for side, sends, receives in sides:

            @pl.when(sends)
            def _():
                for row in range(rows):
                    halo_copy(side, row).wait_send()

            @pl.when(receives)
            def _():
                for row in range(rows):
                    halo_copy(side, row).wait_recv()

            @pl.when(jnp.logical_not(receives))
            def _():
                for row in range(rows):
                    fill(side, row).wait()


def project(devices, rows, tokens, w_qkv, gain):
    count, width = tokens.shape
    wide = w_qkv.shape[1]
    block = BLOCK
    dma = pltpu.SemaphoreType.DMA
    return pl.pallas_call(
        functools.partial(project_kernel, devices, count // rows),
        grid=(count // block,),
        out_shape=(
            jax.ShapeDtypeStruct((count, wide), BF16),
            jax.ShapeDtypeStruct((width, count), BF16),
            jax.ShapeDtypeStruct((2, rows, HALO, width), BF16),
        ),
        in_specs=[
            pl.BlockSpec((block, width), lambda i: (i, 0)),
            whole_spec(width, wide),
            whole_spec(1, width),
            pl.BlockSpec(memory_space=pl.ANY),
        ],
        out_specs=(
            pl.BlockSpec((block, wide), lambda i: (i, 0)),
            pl.BlockSpec((width, block), lambda i: (0, i)),
            pl.BlockSpec(memory_space=pl.ANY),
        ),
        scratch_shapes=[pltpu.VMEM((HALO, width), BF16), dma((2, 2, rows)), dma((2, rows))],
        compiler_params=pltpu.CompilerParams(
            collective_id=1, has_side_effects=True, vmem_limit_bytes=60 * MIB
        ),
        name="project",
    )(tokens, w_qkv, gain, tokens)


def attend_forward_kernel(
    tiles, lengths, local, left, right, w_qkv, gain, mixed, packed, table,
    spread, out, hot, stage, sems,
):
    row = pl.program_id(0)
    local_len = local.shape[0]
    count = plan_tiles(lengths, table, row, tiles)
    for side, tokens in enumerate((left, right)):
        normed = layer_norm(tokens[0, 0].astype(F32), gain[...]).astype(BF16)
        made = jnp.dot(normed, w_qkv[...], preferred_element_type=F32).astype(BF16)
        start = side * (HALO + local_len)
        for c in range(12):
            spread[c, start : start + HALO, :] = made[:, c * 128 : (c + 1) * 128].astype(F32)
    for c in range(12):
        spread[c, HALO : HALO + local_len, :] = local[:, c * 128 : (c + 1) * 128].astype(F32)
    low = lax.broadcasted_iota(jnp.int32, (TILE, 128), 1) < E
    place = lax.broadcasted_iota(jnp.int32, (TILE, 128), 1) % E

    def store(slot, at):
        return pltpu.make_async_copy(stage.at[slot], packed.at[at], sems.at[slot])

    def one_tile(b, _):
        spot = (row * (tiles[0] + 1) + b) * ENTRIES
        begin = table[spot]
        slot = lax.rem(b, 2)
        at = row * tiles[0] + b

        @pl.when(b >= 2)
        def _():
            store(slot, at - 2).wait()

        one_hot, key_fill = tile_fills(table, spot)
        hot[...] = one_hot
        for group in range(GROUPS):
            stage[slot, group, 8] = key_fill.astype(BF16)
        loaded, held = {}, {}
        key_fill = key_fill.astype(BF16)

        def front(h):
            pair, side = h // 2, h % 2
            group, i = pair // 2, pair % 2
            if side == 0:
                loaded[pair] = tuple(spread[4 * n + pair, pl.ds(begin, TILE), :].astype(BF16) for n in range(3))
                for n in range(3):
                    stage[slot, group, 2 * n + i] = loaded[pair][n]
            q, k, _ = loaded[pair]
            own = low if side == 0 else ~low
            return lax.dot_general(
                jnp.where(own, q, hot[...].astype(BF16)),
                jnp.where(own, k, key_fill),
                NT,
                preferred_element_type=F32,
            )

        def back(h, scores):
            pair, side = h // 2, h % 2
            v = loaded[pair][2]
            zero = jnp.zeros_like(v)
            own = low if side == 0 else ~low
            peak = jnp.max(scores, axis=1, keepdims=True)
            weights = jnp.exp2((scores - peak) * SCALE2).astype(BF16)
            both = jnp.concatenate([jnp.where(own, v, zero), jnp.where(own, zero + 1, zero)], axis=1)
            made = jnp.dot(weights, both, preferred_element_type=F32)
            if side == 0:
                held[pair] = (made, peak)
                return
            made += held[pair][0]
            total = made[:, 128:]
            out[pair, pl.ds(begin, TILE), :] = made[:, :128] / total
            total = pltpu.roll(total, E, 1)
            log_sum = jnp.where(low, peak, held[pair][1]) + jnp.log2(total) * (1.0 / SCALE2)
            first = log_sum.astype(BF16).astype(F32)
            rest = log_sum - first
            second = rest.astype(BF16).astype(F32)
            fill = jnp.where(place == 7, second - rest, hot[...])
            fill = jnp.where(place == 6, -second, fill)
            stage[slot, pair // 2, 6 + pair % 2] = jnp.where(place == 5, -first, fill).astype(BF16)

        ahead = front(0)
        for h in range(8):
            now = ahead
            if h < 7:
                ahead = front(h + 1)
            back(h, now)
        store(slot, at).start()
        return 0

    lax.fori_loop(0, count, one_tile, 0)
    for c in range(4):
        mixed[:, c * 128 : (c + 1) * 128] = out[c, HALO : HALO + local_len, :].astype(BF16)

    @pl.when(count >= 2)
    def _():
        store(lax.rem(count, 2), row * tiles[0] + count - 2).wait()

    store(lax.rem(count + 1, 2), row * tiles[0] + count - 1).wait()


def attend_forward(lengths, local, halo, w_qkv, gain):
    rows = lengths.shape[0]
    width = halo.shape[3]
    local_len = local.shape[0] // rows
    most = max_tiles(local_len)
    held = local_len + 2 * HALO
    return pl.pallas_call(
        functools.partial(attend_forward_kernel, (most, local_len, rows)),
        grid=(rows,),
        out_shape=(
            jax.ShapeDtypeStruct((rows * local_len, width), BF16),
            jax.ShapeDtypeStruct((rows * most, GROUPS, 9, TILE, 128), BF16),
            jax.ShapeDtypeStruct(
                (rows * (most + 1) * ENTRIES + rows * (local_len // WINDOW) * 4,), jnp.int32
            ),
        ),
        in_specs=[
            smem_spec(),
            pl.BlockSpec((local_len, 3 * width), lambda r: (r, 0)),
            pl.BlockSpec((1, 1, HALO, width), lambda r: (0, r, 0, 0)),
            pl.BlockSpec((1, 1, HALO, width), lambda r: (1, r, 0, 0)),
            whole_spec(width, 3 * width),
            whole_spec(1, width),
        ],
        out_specs=(
            pl.BlockSpec((local_len, width), lambda r: (r, 0)),
            pl.BlockSpec(memory_space=pl.ANY),
            smem_spec(),
        ),
        scratch_shapes=[
            pltpu.VMEM((12, held, 128), F32),
            pltpu.VMEM((4, held, 128), F32),
            pltpu.VMEM((TILE, 128), F32),
            pltpu.VMEM((2, GROUPS, 9, TILE, 128), BF16),
            pltpu.SemaphoreType.DMA((2,)),
        ],
        compiler_params=pltpu.CompilerParams(vmem_limit_bytes=60 * MIB),
        name="attend_forward",
    )(lengths, local, halo, halo, w_qkv, gain)


def interleave(chains, lag):
    live = {n: chain for n, chain in enumerate(chains)}
    turn = 0
    while live:
        for n in list(live):
            if turn >= n * lag and next(live[n], None) is None:
                del live[n]
        turn += 1


def mlp_kernel(
    tiles, table, tokens, mixed, cotangent, w_out, w_up, w_down, gain,
    output, activated, d_hidden, d_resid, d_attn, d_mixed, normed_t, mixed_t, cotangent_t, grad_gain,
):
    step = pl.program_id(0)
    most, local_len = tiles
    block = tokens.shape[0]
    per_row = local_len // block
    row = step // per_row
    begin = lax.axis_index("seq") * local_len + (step % per_row) * block
    fitted_end = table[(row * (most + 1) + most) * ENTRIES + 1]
    piece = 256
    pieces = w_up.shape[1] // piece

    @pl.when(step == 0)
    def _():
        grad_gain[...] = jnp.zeros_like(grad_gain)

    def chain(first):
        part = slice(first, first + BLOCK)
        positions = begin + first + lax.broadcasted_iota(jnp.int32, (BLOCK, 1), 0)
        valid = positions < fitted_end
        attn = jnp.dot(mixed[part, :], w_out[...], preferred_element_type=F32)
        dy = cotangent[part, :]
        yield True
        resid = tokens[part, :].astype(F32) + jnp.where(valid, attn, 0.0)
        normed, scale = normalize(resid)
        low = (normed * gain[...]).astype(BF16)
        yield True

        def front(j):
            columns = slice(j * piece, (j + 1) * piece)
            hidden = jnp.dot(low, w_up[:, columns], preferred_element_type=F32)
            return hidden, lax.dot_general(dy, w_down[columns, :], NT, preferred_element_type=F32)

        dense, d_normed = resid, 0.0
        ahead = front(0)
        for j in range(pieces):
            columns = slice(j * piece, (j + 1) * piece)
            hidden, d_act = ahead
            if j + 1 < pieces:
                ahead = front(j + 1)
            square = hidden * hidden
            bent = jnp.tanh(hidden * (GELU_A + (GELU_A * GELU_B) * square))
            half = 0.5 + 0.5 * bent
            act = (hidden * half).astype(BF16)
            slope = half + (0.5 - 0.5 * bent * bent) * hidden * (GELU_A + (3.0 * GELU_A * GELU_B) * square)
            grad = (d_act * slope).astype(BF16)
            activated[j, part, :] = act
            d_hidden[j, part, :] = grad
            dense += jnp.dot(act, w_down[columns, :], preferred_element_type=F32)
            d_normed += lax.dot_general(grad, w_up[:, columns], NT, preferred_element_type=F32)
            if j == 1:
                normed_t[:, part] = low.T
            if j == 2:
                mixed_t[:, part] = mixed[part, :].T
            if j == 3:
                cotangent_t[:, part] = dy.T
            yield True
        output[part, :] = dense.astype(BF16)
        grad_gain[...] += fold_rows(d_normed * normed)
        made = dy.astype(F32) + normalize_back(d_normed * gain[...], normed, scale)
        yield True
        d_resid[part, :] = made
        attn_low = jnp.where(valid, made, 0.0).astype(BF16)
        for n in range(attn_low.shape[1] // 256):
            d_attn[n, part, :] = attn_low[:, n * 256 : (n + 1) * 256]
        d_mixed[part, :] = lax.dot_general(attn_low, w_out[...], NT, preferred_element_type=F32).astype(BF16)

    interleave([chain(first) for first in range(0, block, BLOCK)], 3)


def mlp(local_len, table, tokens, mixed, cotangent, w_out, w_up, w_down, gain):
    count, width = tokens.shape
    hidden = w_up.shape[1]
    rows_of = lambda w: pl.BlockSpec((MLP_BLOCK, w), lambda i: (i, 0))
    blocks_of = lambda w: pl.BlockSpec((w // 256, MLP_BLOCK, 256), lambda i: (0, i, 0))
    turned = pl.BlockSpec((width, MLP_BLOCK), lambda i: (0, i))
    shape = jax.ShapeDtypeStruct
    return pl.pallas_call(
        functools.partial(mlp_kernel, (max_tiles(local_len), local_len)),
        grid=(count // MLP_BLOCK,),
        out_shape=(
            shape((count, width), BF16),
            shape((hidden // 256, count, 256), BF16),
            shape((hidden // 256, count, 256), BF16),
            shape((count, width), F32),
            shape((width // 256, count, 256), BF16),
            shape((count, width), BF16),
            shape((width, count), BF16),
            shape((width, count), BF16),
            shape((width, count), BF16),
            shape((8, width), F32),
        ),
        in_specs=[
            smem_spec(),
            rows_of(width),
            rows_of(width),
            rows_of(width),
            whole_spec(width, width),
            whole_spec(width, hidden),
            whole_spec(hidden, width),
            whole_spec(1, width),
        ],
        out_specs=(
            rows_of(width),
            blocks_of(hidden),
            blocks_of(hidden),
            rows_of(width),
            blocks_of(width),
            rows_of(width),
            turned,
            turned,
            turned,
            whole_spec(8, width),
        ),
        compiler_params=pltpu.CompilerParams(vmem_limit_bytes=60 * MIB),
        name="mlp",
    )(table, tokens, mixed, cotangent, w_out, w_up, w_down, gain)


def tile_backward(pairs, packed, fills, grad_of, put):
    low = lax.broadcasted_iota(jnp.int32, (TILE, 128), 1) < E
    key_fill = fills(pairs)
    loaded = {}

    def front(h):
        pair, side = h // 2, h % 2
        if side == 0:
            loaded[pair] = (packed(pair), packed(pairs + pair), packed(2 * pairs + pair), grad_of(pair), fills(pair))
        q, k, v, o, fill = loaded[pair]
        own = low if side == 0 else ~low
        own_o = jnp.where(own, o, jnp.zeros_like(o))
        scores = lax.dot_general(
            jnp.where(own, k, key_fill), jnp.where(own, q, fill), NT, preferred_element_type=F32
        )
        d_probs = lax.dot_general(v, own_o, NT, preferred_element_type=F32)
        return scores, d_probs, own_o

    made = {}

    def back(h, scores, d_probs, own_o):
        pair, side = h // 2, h % 2
        q, k, _, _, _ = loaded[pair]
        own = low if side == 0 else ~low
        zero = jnp.zeros_like(q)
        probs = jnp.exp2(scores * SCALE2)
        weighted = probs * d_probs
        inner = jnp.sum(weighted, axis=0, keepdims=True)
        d_scores = (weighted - probs * inner).astype(BF16)
        dv = jnp.dot(probs.astype(BF16), own_o, preferred_element_type=F32)
        dk = jnp.dot(d_scores, jnp.where(own, q, zero), preferred_element_type=F32)
        dq = lax.dot_general(d_scores, jnp.where(own, k, zero), TN, preferred_element_type=F32)
        if side == 0:
            made[pair] = (dq, dk, dv)
        else:
            first = made[pair]
            put(pair, (first[0] + dq) * 0.125)
            put(pairs + pair, (first[1] + dk) * 0.125)
            put(2 * pairs + pair, first[2] + dv)

    ahead = front(0)
    for h in range(2 * pairs):
        now = ahead
        if h + 1 < 2 * pairs:
            ahead = front(h + 1)
        back(h, *now)


def whole_spec(*shape):
    return pl.BlockSpec(shape, lambda r: (0,) * len(shape))


def smem_spec():
    return pl.BlockSpec(memory_space=pltpu.SMEM)


def sum_plan(devices):
    dp, seq = devices
    chip = [1 << b for b in range(1, dp.bit_length() - 1)]
    along = [1 << b for b in range(seq.bit_length() - 1)]

    def paired(axis, bits):
        return [(axis, tuple(bits[n : n + 2])) for n in range(0, len(bits), 2)]

    core, z = [("dp", (1,))], paired("seq", along)
    one = [("dp", (bit,)) for bit in chip]
    return [core + one + z, core + one[::-1] + z, core + paired("dp", chip) + z]


def chunk_pieces(devices):
    unit = max(1, 16 * devices[0] * devices[1] // PIECE)
    if unit == 1:
        return [4] * 8 + [5, 5, 3, 3]
    return [unit] * (48 // unit)


class GradSum:
    def __init__(self, devices, work, slots, done, send_sem, recv_sem):
        self.plans = sum_plan(devices)
        self.work, self.slots, self.done = work, slots, done
        self.send_sem, self.recv_sem = send_sem, recv_sem
        self.here = {"dp": lax.axis_index("dp"), "seq": lax.axis_index("seq")}
        self.sizes = chunk_pieces(devices)
        self.paths, self.active = [], []
        self.queue, self.clock, self.free_at = [], 0, 0
        base = 0
        for chunk, pieces in enumerate(self.sizes):
            offset, rows, slot, path = base, pieces * PIECE, base, []
            for axis, bits in self.plan(chunk):
                mine, others = self.peers(axis, bits)
                rows //= 1 << len(bits)
                keep = offset + mine * rows
                path.append((keep, [offset + n * rows for n, _ in others], slot, rows))
                offset, slot = keep, slot + rows * len(others)
            self.paths.append(path)
            base += pieces * PIECE

    def plan(self, chunk):
        return self.plans[2 if chunk >= len(self.sizes) - LATE else chunk % 2]

    def peers(self, axis, bits):
        index = self.here[axis]
        own = [(index // bit) % 2 for bit in bits]
        others = []
        for mask in range(1, 1 << len(bits)):
            number, to = 0, index
            for i, bit in enumerate(bits):
                flip = (mask >> i) % 2
                number = number + (1 - own[i] if flip else own[i]) * (1 << i)
                to = to + flip * (bit - 2 * bit * own[i])
            others.append((number, {axis: to}))
        return sum(own[i] * (1 << i) for i in range(len(bits))), others

    def copies(self, chunk, t, pairs):
        axis, bits = self.plan(chunk)[min(t, 2 * len(self.plan(chunk)) - 1 - t)]
        return [
            pltpu.make_async_remote_copy(
                src_ref=source,
                dst_ref=target,
                send_sem=self.send_sem.at[chunk, t, n],
                recv_sem=self.recv_sem.at[chunk, t, n],
                device_id=to,
                device_id_type=MESH,
            )
            for n, ((source, target), (_, to)) in enumerate(zip(pairs, self.peers(axis, bits)[1]))
        ]

    def spreading(self, chunk, s):
        _, gives, slot, rows = self.paths[chunk][s]
        return self.copies(
            chunk,
            s,
            [
                (
                    self.work.at[pl.ds(pl.multiple_of(give, 16), rows)],
                    self.slots.at[slot + n * rows : slot + (n + 1) * rows],
                )
                for n, give in enumerate(gives)
            ],
        )

    def gathering(self, chunk, s, received):
        keep, gives, _, rows = self.paths[chunk][s]
        parts = [
            self.done.at[pl.ds(pl.multiple_of(give if received else keep, 16), rows)] for give in gives
        ]
        return self.copies(chunk, 2 * len(self.plan(chunk)) - 1 - s, [(part, part) for part in parts])

    def add(self, chunk, s):
        keep, gives, slot, rows = self.paths[chunk][s]
        into = self.done if s + 1 == len(self.plan(chunk)) else self.work
        count = next(n for n in range(1, rows) if rows % (16 * n) == 0 and rows // n <= 512)
        block = rows // count

        @pl.loop(0, count)
        def _(i):
            at = pl.ds(pl.multiple_of(keep + i * block, 16), block)
            total = self.work[at, :].astype(F32)
            for n in range(len(gives)):
                from_at = pl.ds(pl.multiple_of(slot + n * rows + i * block, 16), block)
                total += self.slots[from_at, :].astype(F32)
            into[at, :] = total.astype(BF16)

    def event(self, chunk, t):
        steps = len(self.plan(chunk))
        if 0 < t <= steps:
            for copy in self.spreading(chunk, t - 1):
                copy.wait()
            self.add(chunk, t - 1)
        elif t > steps:
            for copy in self.gathering(chunk, 2 * steps - t, False):
                copy.wait_send()
            for copy in self.gathering(chunk, 2 * steps - t, True):
                copy.wait_recv()
        if t < steps:
            for copy in self.spreading(chunk, t):
                copy.start()
        elif t < 2 * steps:
            for copy in self.gathering(chunk, 2 * steps - 1 - t, False):
                copy.start()
        return t == 2 * steps

    def begin(self, chunks, now=False):
        self.queue += chunks
        while self.queue and (now or self.clock >= self.free_at):
            for chunk in self.queue[:2]:
                self.event(chunk, 0)
                self.active.append([chunk, 1])
            self.queue = self.queue[2:]
            self.free_at = self.clock + APART

    def advance(self, finish):
        self.clock += 1
        for entry in list(self.active):
            if self.event(*entry):
                finish(entry[0])
                self.active.remove(entry)
            entry[1] += 1
        self.begin([])


def backward_kernel(
    devices, tiles, table, gains, w_qkv, gain_one,
    normed_two_t, cotangent_t, mixed_t, normed_one_t, d_hidden, activated, d_attn, d_mixed, tokens, d_resid,
    packed,
    grad_tokens, summed, gains_out,
    work, slots, done, left_a, left_b, right_block, halo, d_mix, tok, resid, made_tok, d_proj, bins, d_out,
    tile_in, gain_slots, gain_one_sum,
    send_sem, recv_sem, gain_send, gain_recv, halo_sem, load_sem, block_sem, tile_sem, store_sem, out_sem,
):
    most, local_len = tiles
    count = tok.shape[0]
    rows = count // local_len
    seq = lax.axis_index("seq")
    sums = GradSum(devices, work, slots, done, send_sem, recv_sem)

    barrier = pltpu.get_barrier_semaphore()
    after, before = seq < devices[1] - 1, seq > 0
    peers = [to for axis, bits in sums.plans[2] if axis == "dp" for _, to in sums.peers(axis, bits)[1]]
    peers += [{"seq": lax.rem(seq + d, devices[1])} for d in range(1, devices[1])]
    for peer in peers:
        pl.semaphore_signal(barrier, inc=1, device_id=peer, device_id_type=MESH)

    load_a = lambda ref, k: pltpu.make_async_copy(ref, left_a, load_sem.at[k])
    load_b = lambda ref, k: pltpu.make_async_copy(ref, left_b, load_sem.at[k])
    load_block = lambda ref, block, slot: pltpu.make_async_copy(
        ref.at[block], right_block.at[slot], block_sem.at[slot]
    )
    load_mix = pltpu.make_async_copy(d_mixed, d_mix, load_sem.at[4])
    load_tok = pltpu.make_async_copy(tokens, tok, load_sem.at[5])
    load_resid = pltpu.make_async_copy(d_resid, resid, load_sem.at[6])
    load_a(normed_two_t, 0).start()
    for n in range(BLOCKS_AHEAD):
        load_block(d_hidden, n, n).start()
    load_b(cotangent_t, 1).start()
    load_mix.start()

    pl.semaphore_wait(barrier, len(peers))

    def halo_copy(side, row):
        start = row * local_len + (local_len - HALO if side == 0 else 0)
        return pltpu.make_async_remote_copy(
            src_ref=d_mixed.at[start : start + HALO],
            dst_ref=halo.at[side, row],
            send_sem=halo_sem.at[0, side, row],
            recv_sem=halo_sem.at[1, side, row],
            device_id={"seq": seq + 1 if side == 0 else seq - 1},
            device_id_type=MESH,
        )

    for side, sends, receives in ((0, after, before), (1, before, after)):

        @pl.when(sends)
        def _():
            for row in range(rows):
                halo_copy(side, row).start()

        @pl.when(jnp.logical_not(receives))
        def _():
            for row in range(rows):
                halo[side, row] = jnp.zeros(halo.shape[2:], BF16)

    stored = []

    def store(chunk):
        part = pl.ds(sum(sums.sizes[:chunk]) * PIECE, sums.sizes[chunk] * PIECE)
        return pltpu.make_async_copy(done.at[part], summed.at[part], out_sem.at[chunk])

    def finish(chunk):
        store(chunk).start()
        stored.append(chunk)

    begun = [0]

    def ready(pieces):
        chunks = []
        while begun[0] < len(sums.sizes) and sum(sums.sizes[: begun[0] + 1]) <= pieces:
            chunks.append(begun[0])
            begun[0] += 1
        sums.begin(chunks, pieces >= 48)

    def put_columns(base, block, product):
        low = product.astype(BF16)
        for i in range(2):
            at = pl.multiple_of((base + 2 * block + i) * PIECE, PIECE)
            work[pl.ds(at, PIECE), :] = low[:, i * 128 : (i + 1) * 128]

    def put_rows(base, block, product):
        low = product.T.astype(BF16)
        for c in range(4):
            at = (base + (block // 2) * 4 + c) * PIECE + (block % 2) * 256
            work[pl.ds(pl.multiple_of(at, 256), 256), :] = low[:, c * 128 : (c + 1) * 128]

    half = d_hidden.shape[0] // 2
    runs = [
        (left_a, d_hidden, 0, half, 0, put_columns),
        (left_a, d_hidden, half, half, 0, put_columns),
        (left_b, activated, 0, half, 16, put_rows),
        (left_b, activated, half, half, 16, put_rows),
        (left_a, d_attn, 0, 2, 32, put_columns),
    ]
    waits = {0: load_a(normed_two_t, 0), 2: load_b(cotangent_t, 1), 4: load_a(mixed_t, 2)}
    at = 0
    for n, (lhs, ref, first, blocks, base, put) in enumerate(runs):
        if n in waits:
            waits[n].wait()

        upcoming = [(run[1], run[2], run[3]) for run in runs[n:]][:3]

        def one_block(j, _, n=n, upcoming=upcoming, lhs=lhs, ref=ref, first=first, blocks=blocks, base=base, put=put, at=at):
            slot, later = lax.rem(at + j, BLOCKS_AHEAD + 1), lax.rem(at + j + BLOCKS_AHEAD, BLOCKS_AHEAD + 1)
            load_block(ref, first + j, slot).wait()
            until = 0
            for next_ref, next_first, next_blocks in upcoming:
                since, until = until, until + next_blocks

                @pl.when((j + BLOCKS_AHEAD >= since) & (j + BLOCKS_AHEAD < until))
                def _():
                    load_block(next_ref, next_first + j + BLOCKS_AHEAD - since, later).start()

            put(base, first + j, jnp.dot(lhs[...], right_block[slot], preferred_element_type=F32))
            return 0

        lax.fori_loop(0, blocks, one_block, 0)
        at += blocks
        if n == 1:
            load_a(mixed_t, 2).start()
        if n == 3:
            load_b(normed_one_t, 3).start()
            load_tok.start()
            load_resid.start()
        if n > 0:
            sums.advance(finish)
        if n < 4:
            ready(8 * (n + 1))

    per_group = rows * most
    total = GROUPS * per_group
    unpack_from = rows * (most + 1) * ENTRIES
    windows = local_len // WINDOW

    def load_tile(step, slot):
        group, spot = step // per_group, lax.rem(step, per_group)
        return pltpu.make_async_copy(packed.at[spot, group], tile_in.at[slot], tile_sem.at[slot])

    for n in range(AHEAD):
        load_tile(n, n).start()
    load_mix.wait()
    for side, sends, receives in ((0, after, before), (1, before, after)):

        @pl.when(sends)
        def _():
            for row in range(rows):
                halo_copy(side, row).wait_send()

        @pl.when(receives)
        def _():
            for row in range(rows):
                halo_copy(side, row).wait_recv()

    def one_tile(step, _):
        slot = lax.rem(step, AHEAD + 1)
        group, spot = step // per_group, lax.rem(step, per_group)
        row, b = spot // most, lax.rem(spot, most)
        load_tile(step, slot).wait()

        @pl.when(step + AHEAD < total)
        def _():
            load_tile(step + AHEAD, lax.rem(step + AHEAD, AHEAD + 1)).start()

        @pl.when(b == 0)
        def _():
            start = pl.multiple_of(row * local_len, local_len)
            for i in range(2):
                columns = pl.ds(pl.multiple_of((2 * group + i) * 128, 128), 128)
                d_out[i, :HALO, :] = halo[0, row, :, columns].astype(F32)
                d_out[i, HALO : HALO + local_len, :] = d_mix[pl.ds(start, local_len), columns].astype(F32)
                d_out[i, HALO + local_len :, :] = halo[1, row, :, columns].astype(F32)

        begin = table[(row * (most + 1) + b) * ENTRIES]

        def put(c, values):
            bins[c, pl.ds(pl.multiple_of(b * TILE, TILE), TILE), :] = values

        tile_backward(
            2,
            lambda c: tile_in[slot, c],
            lambda c: tile_in[slot, 6 + c],
            lambda c: d_out[c, pl.ds(begin, TILE), :].astype(BF16),
            put,
        )

        @pl.when(b == most - 1)
        def _():
            @pl.loop(0, windows)
            def _(w):
                entry = unpack_from + (row * windows + w) * 4
                one, two, cut = table[entry], table[entry + 1], table[entry + 2]
                in_one = lax.broadcasted_iota(jnp.int32, (WINDOW, 128), 0) < cut
                to = pl.multiple_of(row * local_len + w * WINDOW, WINDOW)
                for c in range(6):
                    values = jnp.where(
                        in_one, bins[c, pl.ds(one, WINDOW), :], bins[c, pl.ds(two, WINDOW), :]
                    )
                    d_proj[group * 6 + c, pl.ds(to, WINDOW), :] = values.astype(BF16)

        def qkv_gradient(g):
            for kind in range(3):
                both = jnp.concatenate([d_proj[g * 6 + 2 * kind + i] for i in range(2)], axis=1)
                product = jnp.dot(left_b[...], both, preferred_element_type=F32).astype(BF16)
                for i in range(2):
                    piece = 36 + 6 * g + 2 * kind + i
                    work[piece * PIECE : (piece + 1) * PIECE, :] = product[:, i * 128 : (i + 1) * 128]

        for k in range(total):
            ends_group = (k + 1) % per_group == 0
            moves = k in MOVES and sums.active
            if not (ends_group or moves):
                continue

            @pl.when(step == k)
            def _():
                if moves:
                    sums.advance(finish)
                if ends_group:
                    g = k // per_group
                    if g == 0:
                        load_b(normed_one_t, 3).wait()
                    qkv_gradient(g)
                    ready(42 + 6 * g)

        return 0

    lax.fori_loop(0, total, one_tile, 0)

    load_tok.wait()
    load_resid.wait()
    gain_one_sum[...] = jnp.zeros_like(gain_one_sum)
    blocks = count // BLOCK

    def store_tok(i):
        part = pl.ds(pl.multiple_of(i * BLOCK, BLOCK), BLOCK)
        return pltpu.make_async_copy(made_tok.at[part], grad_tokens.at[part], store_sem.at[i])

    def input_block(i, _):
        part = pl.ds(pl.multiple_of(i * BLOCK, BLOCK), BLOCK)
        order = [6 * (pair // 2) + 2 * kind + pair % 2 for kind in range(3) for pair in range(4)]
        d_projected = jnp.concatenate([d_proj[c, part, :] for c in order], axis=1)
        d_normed = lax.dot_general(d_projected, w_qkv[...], NT, preferred_element_type=F32)
        normed, scale = normalize(tok[part, :].astype(F32))
        gain_one_sum[...] += fold_rows(d_normed * normed)
        back = normalize_back(d_normed * gain_one[...], normed, scale)
        made_tok[part, :] = (resid[part, :] + back).astype(BF16)
        store_tok(i).start()
        for k in range(1, blocks, 2):

            @pl.when(i == k)
            def _():
                sums.advance(finish)

        return 0

    lax.fori_loop(0, blocks, input_block, 0)

    gain_plan = sums.plans[2]

    def gain_copies(s):
        return [
            pltpu.make_async_remote_copy(
                src_ref=gain_slots.at[s, 0],
                dst_ref=gain_slots.at[s, n + 1],
                send_sem=gain_send.at[s, n],
                recv_sem=gain_recv.at[s, n],
                device_id=to,
                device_id_type=MESH,
            )
            for n, (_, to) in enumerate(sums.peers(*gain_plan[s])[1])
        ]

    gain_slots[0, 0, :8] = gain_one_sum[...]
    gain_slots[0, 0, 8:] = gains[...]
    for copy in gain_copies(0):
        copy.start()
    for s in range(len(gain_plan)):
        if sums.active:
            sums.advance(finish)
        joined = gain_slots[s, 0]
        for n, copy in enumerate(gain_copies(s)):
            copy.wait()
            joined += gain_slots[s, n + 1]
        if s + 1 < len(gain_plan):
            gain_slots[s + 1, 0] = joined
            for copy in gain_copies(s + 1):
                copy.start()
        else:
            gains_out[...] = joined
    while sums.active:
        sums.advance(finish)
    for i in range(blocks):
        store_tok(i).wait()
    for chunk in stored:
        store(chunk).wait()


def backward(
    devices, rows, table, gains, w_qkv, gain_one, normed_two_t, cotangent_t, mixed_t, normed_one_t,
    d_hidden, activated, d_attn, d_mixed, tokens, d_resid, packed,
):
    count, width = tokens.shape
    local_len = count // rows
    most = max_tiles(local_len)
    held = local_len + 2 * HALO
    steps = max(len(plan) for plan in sum_plan(devices))
    chunks = len(chunk_pieces(devices))
    shape = jax.ShapeDtypeStruct
    anywhere = pl.BlockSpec(memory_space=pl.ANY)
    vmem = pl.BlockSpec(memory_space=pltpu.VMEM)
    dma = pltpu.SemaphoreType.DMA
    return pl.pallas_call(
        functools.partial(backward_kernel, devices, (most, local_len)),
        out_shape=(
            shape((count, width), BF16),
            shape((48 * PIECE, 128), BF16),
            shape((16, width), F32),
        ),
        in_specs=[smem_spec(), vmem, vmem, vmem] + [anywhere] * 11,
        out_specs=(anywhere, anywhere, vmem),
        scratch_shapes=[
            pltpu.VMEM((48 * PIECE, 128), BF16),
            pltpu.VMEM((48 * PIECE, 128), BF16),
            pltpu.VMEM((48 * PIECE, 128), BF16),
            pltpu.VMEM((width, count), BF16),
            pltpu.VMEM((width, count), BF16),
            pltpu.VMEM((BLOCKS_AHEAD + 1, count, 256), BF16),
            pltpu.VMEM((2, rows, HALO, width), BF16),
            pltpu.VMEM((count, width), BF16),
            pltpu.VMEM((count, width), BF16),
            pltpu.VMEM((count, width), F32),
            pltpu.VMEM((count, width), BF16),
            pltpu.VMEM((12, count, 128), BF16),
            pltpu.VMEM((6, most * TILE + WINDOW, 128), F32),
            pltpu.VMEM((2, held, 128), F32),
            pltpu.VMEM((AHEAD + 1, 9, TILE, 128), BF16),
            pltpu.VMEM((steps, 4, 16, width), F32),
            pltpu.VMEM((8, width), F32),
            dma((chunks, 2 * steps, 3)),
            dma((chunks, 2 * steps, 3)),
            dma((steps, 3)),
            dma((steps, 3)),
            dma((2, 2, rows)),
            dma((7,)),
            dma((BLOCKS_AHEAD + 1,)),
            dma((AHEAD + 1,)),
            dma((count // BLOCK,)),
            dma((chunks,)),
        ],
        compiler_params=pltpu.CompilerParams(
            collective_id=0, has_side_effects=True, vmem_limit_bytes=60 * MIB
        ),
        name="backward",
    )(
        table, gains, w_qkv, gain_one, normed_two_t, cotangent_t, mixed_t, normed_one_t,
        d_hidden, activated, d_attn, d_mixed, tokens, d_resid, packed,
    )


def unpack_kernel(up, down, out, *refs):
    grad_qkv, grad_out, grad_up, grad_down = refs[3:]
    for c in range(4):
        columns = slice(c * 128, (c + 1) * 128)
        grad_up[:, columns] = up[c].astype(F32)
        grad_down[:, columns] = down[c].astype(F32)
    grad_out[...] = out[0].astype(F32)
    for n in range(3):
        grad_qkv[:, n * 128 : (n + 1) * 128] = refs[n][0].astype(F32)


def unpack(summed, width, hidden, wide):
    pieces = summed.reshape(48, PIECE, 128)

    def qkv_piece(n):
        def place(i, k):
            block = 3 * i + n
            kind, pair = block // 4, block % 4
            return (36 + 6 * (pair // 2) + 2 * kind + pair % 2, k, 0)

        return pl.BlockSpec((1, PIECE // 2, 128), place)

    shape = jax.ShapeDtypeStruct
    return pl.pallas_call(
        unpack_kernel,
        grid=(4, 2),
        out_shape=(
            shape((width, wide), F32),
            shape((width, width), F32),
            shape((width, hidden), F32),
            shape((hidden, width), F32),
        ),
        in_specs=[
            pl.BlockSpec((4, PIECE // 2, 128), lambda i, k: (i, k, 0)),
            pl.BlockSpec((4, PIECE // 2, 128), lambda i, k: (4 + i, k, 0)),
            pl.BlockSpec((1, PIECE // 2, 128), lambda i, k: (32 + i, k, 0)),
        ]
        + [qkv_piece(n) for n in range(3)],
        out_specs=(
            pl.BlockSpec((width // 2, wide // 4), lambda i, k: (k, i)),
            pl.BlockSpec((width // 2, width // 4), lambda i, k: (k, i)),
            pl.BlockSpec((width // 2, hidden // 4), lambda i, k: (k, i)),
            pl.BlockSpec((hidden // 8, width), lambda i, k: (2 * i + k, 0)),
        ),
        compiler_params=pltpu.CompilerParams(vmem_limit_bytes=60 * MIB),
        name="unpack",
    )(*[pieces] * 6)


def body(
    devices, tokens, item_lengths, w_qkv, w_out, w_up, w_down, gain_one, gain_two, cotangent
):
    rows, local_len, width = tokens.shape
    count = rows * local_len
    gain_one, gain_two = gain_one.reshape(1, width), gain_two.reshape(1, width)
    flat = tokens.reshape(count, width)
    projected, normed_one_t, halo = project(devices, rows, flat, w_qkv, gain_one)
    mixed, packed, table = attend_forward(item_lengths, projected, halo, w_qkv, gain_one)
    (
        output, activated, d_hidden, d_resid, d_attn, d_mixed, normed_two_t, mixed_t, cotangent_t, grad_gain_two
    ) = mlp(local_len, table, flat, mixed, cotangent.reshape(count, width), w_out, w_up, w_down, gain_two)
    grad_tokens, summed, gains = backward(
        devices, rows, table, grad_gain_two, w_qkv, gain_one, normed_two_t, cotangent_t, mixed_t, normed_one_t,
        d_hidden, activated, d_attn, d_mixed, flat, d_resid, packed,
    )
    grads = tuple(unpack(summed, width, w_up.shape[1], w_qkv.shape[1]))
    gains = jnp.sum(gains.reshape(2, 8, width), axis=1)
    placed = (output.reshape(tokens.shape), grad_tokens.reshape(tokens.shape))
    return placed + grads + (gains[0], gains[1])


def solution(mesh):
    rows = P("dp", "seq", None)
    placed = (rows, P("dp", None), P(), P(), P(), P(), P(), P(), rows)
    return jax.shard_map(
        functools.partial(body, (mesh.shape["dp"], mesh.shape["seq"])),
        mesh=mesh,
        in_specs=placed,
        out_specs=(rows, rows, P(), P(), P(), P(), P(), P()),
        check_vma=False,
    )
```

```python
import functools

import jax
import jax.numpy as jnp
from jax import lax
from jax.experimental import pallas as pl
from jax.experimental.pallas import tpu as pltpu
from jax.sharding import PartitionSpec as P

H = 8
E = 64
SEQ_LEN = 4096
LEN_LONG = 250
HALO = 256
TILE = 256
ENTRIES = 8
BLOCK = 256
MLP_BLOCK = 512
PIECE = 512
WINDOW = 64
GROUPS = 2
MOVES = (6, 13, 20, 27, 34)
LATE = 2
APART = 1
AHEAD = 5
BLOCKS_AHEAD = 3

EPSILON = 1e-05
NEGATIVE = -1e30
SCALE2 = 0.125 * 1.4426950408889634
GELU_A = 0.7978845608028654
GELU_B = 0.044715
MIB = 2**20
F32 = jnp.float32
BF16 = jnp.bfloat16
NT = (((1,), (1,)), ((), ()))
TN = (((0,), (0,)), ((), ()))
MESH = pl.DeviceIdType.MESH


def layer_norm(values, scaling):
    centered = values - jnp.mean(values, axis=-1, keepdims=True)
    variance = jnp.mean(centered * centered, axis=-1, keepdims=True)
    return centered * lax.rsqrt(variance + EPSILON) * scaling


def normalize(values):
    centered = values - jnp.mean(values, axis=-1, keepdims=True)
    scale = lax.rsqrt(jnp.mean(centered * centered, axis=-1, keepdims=True) + EPSILON)
    return centered * scale, scale


def normalize_back(upstream, normed, scale):
    mean = jnp.mean(upstream, axis=-1, keepdims=True)
    along = jnp.mean(upstream * normed, axis=-1, keepdims=True)
    return scale * (upstream - mean - normed * along)


def max_tiles(local_len):
    count = 1
    while (count // 2) * 314 + (count % 2) * 64 <= local_len + LEN_LONG - 2:
        count += 1
    return count


def fold_rows(values):
    return jnp.sum(values.reshape(values.shape[0] // 8, 8, values.shape[1]), axis=0)


def plan_tiles(lengths, table, row, tiles):
    slots = lengths.shape[1]
    local_len = tiles[1]
    low = lax.axis_index("seq") * local_len
    high = low + local_len
    base = row * (tiles[0] + 1) * ENTRIES

    def step(k, carry):
        begin, count, tile_begin, in_tile, fitted_end = carry
        true_end = begin + lengths[row, k]
        end = jnp.minimum(true_end, SEQ_LEN)
        touches = (end > low) & (begin < high) & (end > begin)
        fresh = touches & ((count == 0) | (end - tile_begin > TILE))
        count = jnp.where(fresh, count + 1, count)
        tile_begin = jnp.where(fresh, begin, tile_begin)
        in_tile = jnp.where(fresh, 0, in_tile + 1)

        @pl.when(touches)
        def _():
            spot = base + (count - 1) * ENTRIES
            table[spot] = tile_begin - low + HALO
            for j in range(4):

                @pl.when(j >= in_tile)
                def _():
                    table[spot + 1 + j] = end - tile_begin

        fitted_end = jnp.where(true_end <= SEQ_LEN, true_end, fitted_end)
        return (end, count, tile_begin, in_tile, fitted_end)

    zero = jnp.int32(0)
    for b in range(tiles[0]):
        table[base + b * ENTRIES] = 0
    _, count, _, _, fitted_end = lax.fori_loop(0, slots, step, (zero, zero, zero, zero, zero), unroll=5)
    table[base + tiles[0] * ENTRIES] = count
    table[base + tiles[0] * ENTRIES + 1] = fitted_end
    windows = local_len // WINDOW
    unpack_from = tiles[2] * (tiles[0] + 1) * ENTRIES + row * windows * 4

    def window(w, b):
        at = HALO + w * WINDOW

        def end_of(n):
            return table[base + n * ENTRIES] + table[base + n * ENTRIES + 4]

        b = jnp.where(end_of(b) <= at, b + 1, b)
        cut = end_of(b) - at
        table[unpack_from + w * 4] = b * TILE + at - table[base + b * ENTRIES]
        table[unpack_from + w * 4 + 1] = (b + 1) * TILE - cut
        table[unpack_from + w * 4 + 2] = cut
        return b

    lax.fori_loop(0, windows, window, zero)
    return count


def tile_fills(table, spot):
    def segments(positions):
        return sum((positions >= table[spot + 1 + j]).astype(jnp.int32) for j in range(4))

    seg = segments(lax.broadcasted_iota(jnp.int32, (TILE, 128), 0))
    lane = lax.broadcasted_iota(jnp.int32, (TILE, 128), 1) % E
    same = seg == lane
    one_hot = jnp.where(same, 1.0, 0.0)
    across = jnp.where(same, 0.0, NEGATIVE)
    keys = jnp.where(lane < 5, across, jnp.where(lane < 8, 1.0, 0.0))
    return one_hot, keys


def project_kernel(
    devices, local_len, tokens, w_qkv, gain, source, projected, normed_t, halo, zero, halo_sem, zero_sem
):
    step = pl.program_id(0)
    rows = halo.shape[1]
    seq = lax.axis_index("seq")
    after, before = seq < devices[1] - 1, seq > 0

    def halo_copy(side, row):
        start = row * local_len + (local_len - HALO if side == 0 else 0)
        return pltpu.make_async_remote_copy(
            src_ref=source.at[start : start + HALO],
            dst_ref=halo.at[side, row],
            send_sem=halo_sem.at[0, side, row],
            recv_sem=halo_sem.at[1, side, row],
            device_id={"seq": seq + 1 if side == 0 else seq - 1},
            device_id_type=MESH,
        )

    def fill(side, row):
        return pltpu.make_async_copy(zero, halo.at[side, row], zero_sem.at[side, row])

    sides = ((0, after, before), (1, before, after))

    @pl.when(step == 0)
    def _():
        barrier = pltpu.get_barrier_semaphore()
        for d in range(1, devices[1]):
            peer = {"seq": lax.rem(seq + d, devices[1])}
            pl.semaphore_signal(barrier, inc=1, device_id=peer, device_id_type=MESH)
        zero[...] = jnp.zeros_like(zero)
        pl.semaphore_wait(barrier, devices[1] - 1)
        for side, sends, receives in sides:

            @pl.when(sends)
            def _():
                for row in range(rows):
                    halo_copy(side, row).start()

            @pl.when(jnp.logical_not(receives))
            def _():
                for row in range(rows):
                    fill(side, row).start()

    normed, _ = normalize(tokens[...].astype(F32))
    low = (normed * gain[...]).astype(BF16)
    normed_t[...] = low.T
    projected[...] = jnp.dot(low, w_qkv[...], preferred_element_type=F32).astype(BF16)

    @pl.when(step == pl.num_programs(0) - 1)
    def _():
        for side, sends, receives in sides:

            @pl.when(sends)
            def _():
                for row in range(rows):
                    halo_copy(side, row).wait_send()

            @pl.when(receives)
            def _():
                for row in range(rows):
                    halo_copy(side, row).wait_recv()

            @pl.when(jnp.logical_not(receives))
            def _():
                for row in range(rows):
                    fill(side, row).wait()


def project(devices, rows, tokens, w_qkv, gain):
    count, width = tokens.shape
    wide = w_qkv.shape[1]
    block = BLOCK
    dma = pltpu.SemaphoreType.DMA
    return pl.pallas_call(
        functools.partial(project_kernel, devices, count // rows),
        grid=(count // block,),
        out_shape=(
            jax.ShapeDtypeStruct((count, wide), BF16),
            jax.ShapeDtypeStruct((width, count), BF16),
            jax.ShapeDtypeStruct((2, rows, HALO, width), BF16),
        ),
        in_specs=[
            pl.BlockSpec((block, width), lambda i: (i, 0)),
            whole_spec(width, wide),
            whole_spec(1, width),
            pl.BlockSpec(memory_space=pl.ANY),
        ],
        out_specs=(
            pl.BlockSpec((block, wide), lambda i: (i, 0)),
            pl.BlockSpec((width, block), lambda i: (0, i)),
            pl.BlockSpec(memory_space=pl.ANY),
        ),
        scratch_shapes=[pltpu.VMEM((HALO, width), BF16), dma((2, 2, rows)), dma((2, rows))],
        compiler_params=pltpu.CompilerParams(
            collective_id=1, has_side_effects=True, vmem_limit_bytes=60 * MIB
        ),
        name="project",
    )(tokens, w_qkv, gain, tokens)


def attend_forward_kernel(
    tiles, lengths, local, left, right, w_qkv, gain, mixed, packed, table,
    spread, out, hot, stage, sems,
):
    row = pl.program_id(0)
    local_len = local.shape[0]
    count = plan_tiles(lengths, table, row, tiles)
    for side, tokens in enumerate((left, right)):
        normed = layer_norm(tokens[0, 0].astype(F32), gain[...]).astype(BF16)
        made = jnp.dot(normed, w_qkv[...], preferred_element_type=F32).astype(BF16)
        start = side * (HALO + local_len)
        for c in range(12):
            spread[c, start : start + HALO, :] = made[:, c * 128 : (c + 1) * 128].astype(F32)
    for c in range(12):
        spread[c, HALO : HALO + local_len, :] = local[:, c * 128 : (c + 1) * 128].astype(F32)
    low = lax.broadcasted_iota(jnp.int32, (TILE, 128), 1) < E
    place = lax.broadcasted_iota(jnp.int32, (TILE, 128), 1) % E

    def store(slot, at):
        return pltpu.make_async_copy(stage.at[slot], packed.at[at], sems.at[slot])

    def one_tile(b, _):
        spot = (row * (tiles[0] + 1) + b) * ENTRIES
        begin = table[spot]
        slot = lax.rem(b, 2)
        at = row * tiles[0] + b

        @pl.when(b >= 2)
        def _():
            store(slot, at - 2).wait()

        one_hot, key_fill = tile_fills(table, spot)
        hot[...] = one_hot
        for group in range(GROUPS):
            stage[slot, group, 8] = key_fill.astype(BF16)
        loaded, held = {}, {}
        key_fill = key_fill.astype(BF16)

        def front(h):
            pair, side = h // 2, h % 2
            group, i = pair // 2, pair % 2
            if side == 0:
                loaded[pair] = tuple(spread[4 * n + pair, pl.ds(begin, TILE), :].astype(BF16) for n in range(3))
                for n in range(3):
                    stage[slot, group, 2 * n + i] = loaded[pair][n]
            q, k, _ = loaded[pair]
            own = low if side == 0 else ~low
            return lax.dot_general(
                jnp.where(own, q, hot[...].astype(BF16)),
                jnp.where(own, k, key_fill),
                NT,
                preferred_element_type=F32,
            )

        def back(h, scores):
            pair, side = h // 2, h % 2
            v = loaded[pair][2]
            zero = jnp.zeros_like(v)
            own = low if side == 0 else ~low
            peak = jnp.max(scores, axis=1, keepdims=True)
            weights = jnp.exp2((scores - peak) * SCALE2).astype(BF16)
            both = jnp.concatenate([jnp.where(own, v, zero), jnp.where(own, zero + 1, zero)], axis=1)
            if side == 0:
                held[pair] = ((weights, both), peak)
                return
            made = jnp.dot(
                jnp.concatenate([held[pair][0][0], weights], axis=1),
                jnp.concatenate([held[pair][0][1], both], axis=0),
                preferred_element_type=F32,
            )
            total = made[:, 128:]
            out[pair, pl.ds(begin, TILE), :] = made[:, :128] / total
            total = pltpu.roll(total, E, 1)
            log_sum = jnp.where(low, peak, held[pair][1]) + jnp.log2(total) * (1.0 / SCALE2)
            first = log_sum.astype(BF16).astype(F32)
            rest = log_sum - first
            second = rest.astype(BF16).astype(F32)
            fill = jnp.where(place == 7, second - rest, hot[...])
            fill = jnp.where(place == 6, -second, fill)
            stage[slot, pair // 2, 6 + pair % 2] = jnp.where(place == 5, -first, fill).astype(BF16)

        ahead = [front(h) for h in range(2)]
        for h in range(8):
            now = ahead.pop(0)
            if h + 2 < 8:
                ahead.append(front(h + 2))
            back(h, now)
        store(slot, at).start()
        return 0

    lax.fori_loop(0, count, one_tile, 0)
    for c in range(4):
        mixed[:, c * 128 : (c + 1) * 128] = out[c, HALO : HALO + local_len, :].astype(BF16)

    @pl.when(count >= 2)
    def _():
        store(lax.rem(count, 2), row * tiles[0] + count - 2).wait()

    store(lax.rem(count + 1, 2), row * tiles[0] + count - 1).wait()


def attend_forward(lengths, local, halo, w_qkv, gain):
    rows = lengths.shape[0]
    width = halo.shape[3]
    local_len = local.shape[0] // rows
    most = max_tiles(local_len)
    held = local_len + 2 * HALO
    return pl.pallas_call(
        functools.partial(attend_forward_kernel, (most, local_len, rows)),
        grid=(rows,),
        out_shape=(
            jax.ShapeDtypeStruct((rows * local_len, width), BF16),
            jax.ShapeDtypeStruct((rows * most, GROUPS, 9, TILE, 128), BF16),
            jax.ShapeDtypeStruct(
                (rows * (most + 1) * ENTRIES + rows * (local_len // WINDOW) * 4,), jnp.int32
            ),
        ),
        in_specs=[
            smem_spec(),
            pl.BlockSpec((local_len, 3 * width), lambda r: (r, 0)),
            pl.BlockSpec((1, 1, HALO, width), lambda r: (0, r, 0, 0)),
            pl.BlockSpec((1, 1, HALO, width), lambda r: (1, r, 0, 0)),
            whole_spec(width, 3 * width),
            whole_spec(1, width),
        ],
        out_specs=(
            pl.BlockSpec((local_len, width), lambda r: (r, 0)),
            pl.BlockSpec(memory_space=pl.ANY),
            smem_spec(),
        ),
        scratch_shapes=[
            pltpu.VMEM((12, held, 128), F32),
            pltpu.VMEM((4, held, 128), F32),
            pltpu.VMEM((TILE, 128), F32),
            pltpu.VMEM((2, GROUPS, 9, TILE, 128), BF16),
            pltpu.SemaphoreType.DMA((2,)),
        ],
        compiler_params=pltpu.CompilerParams(vmem_limit_bytes=60 * MIB),
        name="attend_forward",
    )(lengths, local, halo, halo, w_qkv, gain)


def interleave(chains, lag):
    live = {n: chain for n, chain in enumerate(chains)}
    turn = 0
    while live:
        for n in list(live):
            if turn >= n * lag and next(live[n], None) is None:
                del live[n]
        turn += 1


def mlp_kernel(
    tiles, table, tokens, mixed, cotangent, w_out, w_up, w_down, gain,
    output, activated, d_hidden, d_resid, d_attn, d_mixed, normed_t, mixed_t, cotangent_t, grad_gain,
):
    step = pl.program_id(0)
    most, local_len = tiles
    block = tokens.shape[0]
    per_row = local_len // block
    row = step // per_row
    begin = lax.axis_index("seq") * local_len + (step % per_row) * block
    fitted_end = table[(row * (most + 1) + most) * ENTRIES + 1]
    piece = 256
    pieces = w_up.shape[1] // piece

    @pl.when(step == 0)
    def _():
        grad_gain[...] = jnp.zeros_like(grad_gain)

    def chain(first):
        part = slice(first, first + BLOCK)
        positions = begin + first + lax.broadcasted_iota(jnp.int32, (BLOCK, 1), 0)
        valid = positions < fitted_end
        attn = jnp.dot(mixed[part, :], w_out[...], preferred_element_type=F32)
        dy = cotangent[part, :]
        yield True
        resid = tokens[part, :].astype(F32) + jnp.where(valid, attn, 0.0)
        normed, scale = normalize(resid)
        low = (normed * gain[...]).astype(BF16)
        yield True

        def front(j):
            columns = slice(j * piece, (j + 1) * piece)
            hidden = jnp.dot(low, w_up[:, columns], preferred_element_type=F32)
            return hidden, lax.dot_general(dy, w_down[columns, :], NT, preferred_element_type=F32)

        dense, d_normed = resid, 0.0
        ahead = front(0)
        for j in range(pieces):
            columns = slice(j * piece, (j + 1) * piece)
            hidden, d_act = ahead
            if j + 1 < pieces:
                ahead = front(j + 1)
            square = hidden * hidden
            bent = jnp.tanh(hidden * (GELU_A + (GELU_A * GELU_B) * square))
            half = 0.5 + 0.5 * bent
            act = (hidden * half).astype(BF16)
            slope = half + (0.5 - 0.5 * bent * bent) * hidden * (GELU_A + (3.0 * GELU_A * GELU_B) * square)
            grad = (d_act * slope).astype(BF16)
            activated[j, part, :] = act
            d_hidden[j, part, :] = grad
            dense += jnp.dot(act, w_down[columns, :], preferred_element_type=F32)
            d_normed += lax.dot_general(grad, w_up[:, columns], NT, preferred_element_type=F32)
            if j == 1:
                normed_t[:, part] = low.T
            if j == 2:
                mixed_t[:, part] = mixed[part, :].T
            if j == 3:
                cotangent_t[:, part] = dy.T
            yield True
        output[part, :] = dense.astype(BF16)
        grad_gain[...] += fold_rows(d_normed * normed)
        made = dy.astype(F32) + normalize_back(d_normed * gain[...], normed, scale)
        yield True
        d_resid[part, :] = made
        attn_low = jnp.where(valid, made, 0.0).astype(BF16)
        for n in range(attn_low.shape[1] // 256):
            d_attn[n, part, :] = attn_low[:, n * 256 : (n + 1) * 256]
        d_mixed[part, :] = lax.dot_general(attn_low, w_out[...], NT, preferred_element_type=F32).astype(BF16)

    interleave([chain(first) for first in range(0, block, BLOCK)], 3)


def mlp(local_len, table, tokens, mixed, cotangent, w_out, w_up, w_down, gain):
    count, width = tokens.shape
    hidden = w_up.shape[1]
    rows_of = lambda w: pl.BlockSpec((MLP_BLOCK, w), lambda i: (i, 0))
    blocks_of = lambda w: pl.BlockSpec((w // 256, MLP_BLOCK, 256), lambda i: (0, i, 0))
    turned = pl.BlockSpec((width, MLP_BLOCK), lambda i: (0, i))
    shape = jax.ShapeDtypeStruct
    return pl.pallas_call(
        functools.partial(mlp_kernel, (max_tiles(local_len), local_len)),
        grid=(count // MLP_BLOCK,),
        out_shape=(
            shape((count, width), BF16),
            shape((hidden // 256, count, 256), BF16),
            shape((hidden // 256, count, 256), BF16),
            shape((count, width), F32),
            shape((width // 256, count, 256), BF16),
            shape((count, width), BF16),
            shape((width, count), BF16),
            shape((width, count), BF16),
            shape((width, count), BF16),
            shape((8, width), F32),
        ),
        in_specs=[
            smem_spec(),
            rows_of(width),
            rows_of(width),
            rows_of(width),
            whole_spec(width, width),
            whole_spec(width, hidden),
            whole_spec(hidden, width),
            whole_spec(1, width),
        ],
        out_specs=(
            rows_of(width),
            blocks_of(hidden),
            blocks_of(hidden),
            rows_of(width),
            blocks_of(width),
            rows_of(width),
            turned,
            turned,
            turned,
            whole_spec(8, width),
        ),
        compiler_params=pltpu.CompilerParams(vmem_limit_bytes=60 * MIB),
        name="mlp",
    )(table, tokens, mixed, cotangent, w_out, w_up, w_down, gain)


def tile_backward(pairs, packed, fills, grad_of, put):
    low = lax.broadcasted_iota(jnp.int32, (TILE, 128), 1) < E
    key_fill = fills(pairs)
    loaded = {}

    def front(h):
        pair, side = h // 2, h % 2
        if side == 0:
            loaded[pair] = (packed(pair), packed(pairs + pair), packed(2 * pairs + pair), grad_of(pair), fills(pair))
        q, k, v, o, fill = loaded[pair]
        own = low if side == 0 else ~low
        own_o = jnp.where(own, o, jnp.zeros_like(o))
        scores = lax.dot_general(
            jnp.where(own, k, key_fill), jnp.where(own, q, fill), NT, preferred_element_type=F32
        )
        d_probs = lax.dot_general(v, own_o, NT, preferred_element_type=F32)
        return scores, d_probs, own_o

    made = {}

    def back(h, scores, d_probs, own_o):
        pair, side = h // 2, h % 2
        q, k, _, _, _ = loaded[pair]
        own = low if side == 0 else ~low
        zero = jnp.zeros_like(q)
        probs = jnp.exp2(scores * SCALE2)
        weighted = probs * d_probs
        inner = jnp.sum(weighted, axis=0, keepdims=True)
        d_scores = (weighted - probs * inner).astype(BF16)
        dv = jnp.dot(probs.astype(BF16), own_o, preferred_element_type=F32)
        dk = jnp.dot(d_scores, jnp.where(own, q, zero), preferred_element_type=F32)
        dq = lax.dot_general(d_scores, jnp.where(own, k, zero), TN, preferred_element_type=F32)
        if side == 0:
            made[pair] = (dq, dk, dv)
        else:
            first = made[pair]
            put(pair, (first[0] + dq) * 0.125)
            put(pairs + pair, (first[1] + dk) * 0.125)
            put(2 * pairs + pair, first[2] + dv)

    ahead = [front(0), front(1)]
    for h in range(2 * pairs):
        now = ahead.pop(0)
        if h + 2 < 2 * pairs:
            ahead.append(front(h + 2))
        back(h, *now)


def whole_spec(*shape):
    return pl.BlockSpec(shape, lambda r: (0,) * len(shape))


def smem_spec():
    return pl.BlockSpec(memory_space=pltpu.SMEM)


def sum_plan(devices):
    dp, seq = devices
    chip = [1 << b for b in range(1, dp.bit_length() - 1)]
    along = [1 << b for b in range(seq.bit_length() - 1)]

    def paired(axis, bits):
        return [(axis, tuple(bits[n : n + 2])) for n in range(0, len(bits), 2)]

    core, z = [("dp", (1,))], paired("seq", along)
    one = [("dp", (bit,)) for bit in chip]
    return [core + one + z, core + one[::-1] + z, core + paired("dp", chip) + z]


def chunk_pieces(devices):
    unit = max(1, 16 * devices[0] * devices[1] // PIECE)
    if unit == 1:
        return [4] * 8 + [5, 5, 3, 3]
    return [unit] * (48 // unit)


class GradSum:
    def __init__(self, devices, work, slots, done, send_sem, recv_sem):
        self.plans = sum_plan(devices)
        self.work, self.slots, self.done = work, slots, done
        self.send_sem, self.recv_sem = send_sem, recv_sem
        self.here = {"dp": lax.axis_index("dp"), "seq": lax.axis_index("seq")}
        self.sizes = chunk_pieces(devices)
        self.paths, self.active = [], []
        self.queue, self.clock, self.free_at = [], 0, 0
        base = 0
        for chunk, pieces in enumerate(self.sizes):
            offset, rows, slot, path = base, pieces * PIECE, base, []
            for axis, bits in self.plan(chunk):
                mine, others = self.peers(axis, bits)
                rows //= 1 << len(bits)
                keep = offset + mine * rows
                path.append((keep, [offset + n * rows for n, _ in others], slot, rows))
                offset, slot = keep, slot + rows * len(others)
            self.paths.append(path)
            base += pieces * PIECE

    def plan(self, chunk):
        return self.plans[2 if chunk >= len(self.sizes) - LATE else chunk % 2]

    def peers(self, axis, bits):
        index = self.here[axis]
        own = [(index // bit) % 2 for bit in bits]
        others = []
        for mask in range(1, 1 << len(bits)):
            number, to = 0, index
            for i, bit in enumerate(bits):
                flip = (mask >> i) % 2
                number = number + (1 - own[i] if flip else own[i]) * (1 << i)
                to = to + flip * (bit - 2 * bit * own[i])
            others.append((number, {axis: to}))
        return sum(own[i] * (1 << i) for i in range(len(bits))), others

    def copies(self, chunk, t, pairs):
        axis, bits = self.plan(chunk)[min(t, 2 * len(self.plan(chunk)) - 1 - t)]
        return [
            pltpu.make_async_remote_copy(
                src_ref=source,
                dst_ref=target,
                send_sem=self.send_sem.at[chunk, t, n],
                recv_sem=self.recv_sem.at[chunk, t, n],
                device_id=to,
                device_id_type=MESH,
            )
            for n, ((source, target), (_, to)) in enumerate(zip(pairs, self.peers(axis, bits)[1]))
        ]

    def spreading(self, chunk, s):
        _, gives, slot, rows = self.paths[chunk][s]
        return self.copies(
            chunk,
            s,
            [
                (
                    self.work.at[pl.ds(pl.multiple_of(give, 16), rows)],
                    self.slots.at[slot + n * rows : slot + (n + 1) * rows],
                )
                for n, give in enumerate(gives)
            ],
        )

    def gathering(self, chunk, s, received):
        keep, gives, _, rows = self.paths[chunk][s]
        parts = [
            self.done.at[pl.ds(pl.multiple_of(give if received else keep, 16), rows)] for give in gives
        ]
        return self.copies(chunk, 2 * len(self.plan(chunk)) - 1 - s, [(part, part) for part in parts])

    def add(self, chunk, s):
        keep, gives, slot, rows = self.paths[chunk][s]
        into = self.done if s + 1 == len(self.plan(chunk)) else self.work
        count = next(n for n in range(1, rows) if rows % (16 * n) == 0 and rows // n <= 512)
        block = rows // count

        @pl.loop(0, count)
        def _(i):
            at = pl.ds(pl.multiple_of(keep + i * block, 16), block)
            total = self.work[at, :].astype(F32)
            for n in range(len(gives)):
                from_at = pl.ds(pl.multiple_of(slot + n * rows + i * block, 16), block)
                total += self.slots[from_at, :].astype(F32)
            into[at, :] = total.astype(BF16)

    def event(self, chunk, t):
        steps = len(self.plan(chunk))
        if 0 < t <= steps:
            for copy in self.spreading(chunk, t - 1):
                copy.wait()
            self.add(chunk, t - 1)
        elif t > steps:
            for copy in self.gathering(chunk, 2 * steps - t, False):
                copy.wait_send()
            for copy in self.gathering(chunk, 2 * steps - t, True):
                copy.wait_recv()
        if t < steps:
            for copy in self.spreading(chunk, t):
                copy.start()
        elif t < 2 * steps:
            for copy in self.gathering(chunk, 2 * steps - 1 - t, False):
                copy.start()
        return t == 2 * steps

    def begin(self, chunks, now=False):
        self.queue += chunks
        while self.queue and (now or self.clock >= self.free_at):
            for chunk in self.queue[:2]:
                self.event(chunk, 0)
                self.active.append([chunk, 1])
            self.queue = self.queue[2:]
            self.free_at = self.clock + APART

    def advance(self, finish):
        self.clock += 1
        for entry in list(self.active):
            if self.event(*entry):
                finish(entry[0])
                self.active.remove(entry)
            entry[1] += 1
        self.begin([])


def backward_kernel(
    devices, tiles, table, gains, w_qkv, gain_one,
    normed_two_t, cotangent_t, mixed_t, normed_one_t, d_hidden, activated, d_attn, d_mixed, tokens, d_resid,
    packed,
    grad_tokens, summed, gains_out,
    work, slots, done, left_a, left_b, right_block, halo, d_mix, tok, resid, made_tok, d_proj, bins, d_out,
    tile_in, gain_slots, gain_one_sum,
    send_sem, recv_sem, gain_send, gain_recv, halo_sem, load_sem, block_sem, tile_sem, store_sem, out_sem,
):
    most, local_len = tiles
    count = tok.shape[0]
    rows = count // local_len
    seq = lax.axis_index("seq")
    sums = GradSum(devices, work, slots, done, send_sem, recv_sem)

    barrier = pltpu.get_barrier_semaphore()
    after, before = seq < devices[1] - 1, seq > 0
    peers = [to for axis, bits in sums.plans[2] if axis == "dp" for _, to in sums.peers(axis, bits)[1]]
    peers += [{"seq": lax.rem(seq + d, devices[1])} for d in range(1, devices[1])]
    for peer in peers:
        pl.semaphore_signal(barrier, inc=1, device_id=peer, device_id_type=MESH)

    load_a = lambda ref, k: pltpu.make_async_copy(ref, left_a, load_sem.at[k])
    load_b = lambda ref, k: pltpu.make_async_copy(ref, left_b, load_sem.at[k])
    load_block = lambda ref, block, slot: pltpu.make_async_copy(
        ref.at[block], right_block.at[slot], block_sem.at[slot]
    )
    load_mix = pltpu.make_async_copy(d_mixed, d_mix, load_sem.at[4])
    load_tok = pltpu.make_async_copy(tokens, tok, load_sem.at[5])
    load_resid = pltpu.make_async_copy(d_resid, resid, load_sem.at[6])
    load_a(normed_two_t, 0).start()
    for n in range(BLOCKS_AHEAD):
        load_block(d_hidden, n, n).start()
    load_b(cotangent_t, 1).start()
    load_mix.start()

    pl.semaphore_wait(barrier, len(peers))

    def halo_copy(side, row):
        start = row * local_len + (local_len - HALO if side == 0 else 0)
        return pltpu.make_async_remote_copy(
            src_ref=d_mixed.at[start : start + HALO],
            dst_ref=halo.at[side, row],
            send_sem=halo_sem.at[0, side, row],
            recv_sem=halo_sem.at[1, side, row],
            device_id={"seq": seq + 1 if side == 0 else seq - 1},
            device_id_type=MESH,
        )

    for side, sends, receives in ((0, after, before), (1, before, after)):

        @pl.when(sends)
        def _():
            for row in range(rows):
                halo_copy(side, row).start()

        @pl.when(jnp.logical_not(receives))
        def _():
            for row in range(rows):
                halo[side, row] = jnp.zeros(halo.shape[2:], BF16)

    stored = []

    def store(chunk):
        part = pl.ds(sum(sums.sizes[:chunk]) * PIECE, sums.sizes[chunk] * PIECE)
        return pltpu.make_async_copy(done.at[part], summed.at[part], out_sem.at[chunk])

    def finish(chunk):
        store(chunk).start()
        stored.append(chunk)

    begun = [0]

    def ready(pieces):
        chunks = []
        while begun[0] < len(sums.sizes) and sum(sums.sizes[: begun[0] + 1]) <= pieces:
            chunks.append(begun[0])
            begun[0] += 1
        sums.begin(chunks, pieces >= 48)

    def put_columns(base, block, product):
        low = product.astype(BF16)
        for i in range(2):
            at = pl.multiple_of((base + 2 * block + i) * PIECE, PIECE)
            work[pl.ds(at, PIECE), :] = low[:, i * 128 : (i + 1) * 128]

    def put_rows(base, block, product):
        low = product.T.astype(BF16)
        for c in range(4):
            at = (base + (block // 2) * 4 + c) * PIECE + (block % 2) * 256
            work[pl.ds(pl.multiple_of(at, 256), 256), :] = low[:, c * 128 : (c + 1) * 128]

    half = d_hidden.shape[0] // 2
    runs = [
        (left_a, d_hidden, 0, half, 0, put_columns),
        (left_a, d_hidden, half, half, 0, put_columns),
        (left_b, activated, 0, half, 16, put_rows),
        (left_b, activated, half, half, 16, put_rows),
        (left_a, d_attn, 0, 2, 32, put_columns),
    ]
    waits = {0: load_a(normed_two_t, 0), 2: load_b(cotangent_t, 1), 4: load_a(mixed_t, 2)}
    at = 0
    for n, (lhs, ref, first, blocks, base, put) in enumerate(runs):
        if n in waits:
            waits[n].wait()

        upcoming = [(run[1], run[2], run[3]) for run in runs[n:]][:3]

        def one_block(j, _, n=n, upcoming=upcoming, lhs=lhs, ref=ref, first=first, blocks=blocks, base=base, put=put, at=at):
            slot, later = lax.rem(at + j, BLOCKS_AHEAD + 1), lax.rem(at + j + BLOCKS_AHEAD, BLOCKS_AHEAD + 1)
            load_block(ref, first + j, slot).wait()
            until = 0
            for next_ref, next_first, next_blocks in upcoming:
                since, until = until, until + next_blocks

                @pl.when((j + BLOCKS_AHEAD >= since) & (j + BLOCKS_AHEAD < until))
                def _():
                    load_block(next_ref, next_first + j + BLOCKS_AHEAD - since, later).start()

            put(base, first + j, jnp.dot(lhs[...], right_block[slot], preferred_element_type=F32))
            return 0

        lax.fori_loop(0, blocks, one_block, 0)
        at += blocks
        if n == 1:
            load_a(mixed_t, 2).start()
        if n == 3:
            load_b(normed_one_t, 3).start()
            load_tok.start()
            load_resid.start()
        if n > 0:
            sums.advance(finish)
        if n < 4:
            ready(8 * (n + 1))

    per_group = rows * most
    total = GROUPS * per_group
    unpack_from = rows * (most + 1) * ENTRIES
    windows = local_len // WINDOW

    def load_tile(step, slot):
        group, spot = step // per_group, lax.rem(step, per_group)
        return pltpu.make_async_copy(packed.at[spot, group], tile_in.at[slot], tile_sem.at[slot])

    for n in range(AHEAD):
        load_tile(n, n).start()
    load_mix.wait()
    for side, sends, receives in ((0, after, before), (1, before, after)):

        @pl.when(sends)
        def _():
            for row in range(rows):
                halo_copy(side, row).wait_send()

        @pl.when(receives)
        def _():
            for row in range(rows):
                halo_copy(side, row).wait_recv()

    def one_tile(step, _):
        slot = lax.rem(step, AHEAD + 1)
        group, spot = step // per_group, lax.rem(step, per_group)
        row, b = spot // most, lax.rem(spot, most)
        load_tile(step, slot).wait()

        @pl.when(step + AHEAD < total)
        def _():
            load_tile(step + AHEAD, lax.rem(step + AHEAD, AHEAD + 1)).start()

        @pl.when(b == 0)
        def _():
            start = pl.multiple_of(row * local_len, local_len)
            for i in range(2):
                columns = pl.ds(pl.multiple_of((2 * group + i) * 128, 128), 128)
                d_out[i, :HALO, :] = halo[0, row, :, columns].astype(F32)
                d_out[i, HALO : HALO + local_len, :] = d_mix[pl.ds(start, local_len), columns].astype(F32)
                d_out[i, HALO + local_len :, :] = halo[1, row, :, columns].astype(F32)

        begin = table[(row * (most + 1) + b) * ENTRIES]

        def put(c, values):
            bins[c, pl.ds(pl.multiple_of(b * TILE, TILE), TILE), :] = values

        tile_backward(
            2,
            lambda c: tile_in[slot, c],
            lambda c: tile_in[slot, 6 + c],
            lambda c: d_out[c, pl.ds(begin, TILE), :].astype(BF16),
            put,
        )

        @pl.when(b == most - 1)
        def _():
            @pl.loop(0, windows)
            def _(w):
                entry = unpack_from + (row * windows + w) * 4
                one, two, cut = table[entry], table[entry + 1], table[entry + 2]
                in_one = lax.broadcasted_iota(jnp.int32, (WINDOW, 128), 0) < cut
                to = pl.multiple_of(row * local_len + w * WINDOW, WINDOW)
                for c in range(6):
                    values = jnp.where(
                        in_one, bins[c, pl.ds(one, WINDOW), :], bins[c, pl.ds(two, WINDOW), :]
                    )
                    d_proj[group * 6 + c, pl.ds(to, WINDOW), :] = values.astype(BF16)

        def qkv_gradient(g):
            for kind in range(3):
                both = jnp.concatenate([d_proj[g * 6 + 2 * kind + i] for i in range(2)], axis=1)
                product = jnp.dot(left_b[...], both, preferred_element_type=F32).astype(BF16)
                for i in range(2):
                    piece = 36 + 6 * g + 2 * kind + i
                    work[piece * PIECE : (piece + 1) * PIECE, :] = product[:, i * 128 : (i + 1) * 128]

        for k in range(total):
            ends_group = (k + 1) % per_group == 0
            moves = k in MOVES and sums.active
            if not (ends_group or moves):
                continue

            @pl.when(step == k)
            def _():
                if moves:
                    sums.advance(finish)
                if ends_group:
                    g = k // per_group
                    if g == 0:
                        load_b(normed_one_t, 3).wait()
                    qkv_gradient(g)
                    ready(42 + 6 * g)

        return 0

    lax.fori_loop(0, total, one_tile, 0)

    load_tok.wait()
    load_resid.wait()
    gain_one_sum[...] = jnp.zeros_like(gain_one_sum)
    blocks = count // BLOCK

    def store_tok(i):
        part = pl.ds(pl.multiple_of(i * BLOCK, BLOCK), BLOCK)
        return pltpu.make_async_copy(made_tok.at[part], grad_tokens.at[part], store_sem.at[i])

    def input_block(i, _):
        part = pl.ds(pl.multiple_of(i * BLOCK, BLOCK), BLOCK)
        order = [6 * (pair // 2) + 2 * kind + pair % 2 for kind in range(3) for pair in range(4)]
        d_projected = jnp.concatenate([d_proj[c, part, :] for c in order], axis=1)
        d_normed = lax.dot_general(d_projected, w_qkv[...], NT, preferred_element_type=F32)
        normed, scale = normalize(tok[part, :].astype(F32))
        gain_one_sum[...] += fold_rows(d_normed * normed)
        back = normalize_back(d_normed * gain_one[...], normed, scale)
        made_tok[part, :] = (resid[part, :] + back).astype(BF16)
        store_tok(i).start()
        for k in range(1, blocks, 2):

            @pl.when(i == k)
            def _():
                sums.advance(finish)

        return 0

    lax.fori_loop(0, blocks, input_block, 0)

    gain_plan = sums.plans[2]

    def gain_copies(s):
        return [
            pltpu.make_async_remote_copy(
                src_ref=gain_slots.at[s, 0],
                dst_ref=gain_slots.at[s, n + 1],
                send_sem=gain_send.at[s, n],
                recv_sem=gain_recv.at[s, n],
                device_id=to,
                device_id_type=MESH,
            )
            for n, (_, to) in enumerate(sums.peers(*gain_plan[s])[1])
        ]

    gain_slots[0, 0, :8] = gain_one_sum[...]
    gain_slots[0, 0, 8:] = gains[...]
    for copy in gain_copies(0):
        copy.start()
    for s in range(len(gain_plan)):
        if sums.active:
            sums.advance(finish)
        joined = gain_slots[s, 0]
        for n, copy in enumerate(gain_copies(s)):
            copy.wait()
            joined += gain_slots[s, n + 1]
        if s + 1 < len(gain_plan):
            gain_slots[s + 1, 0] = joined
            for copy in gain_copies(s + 1):
                copy.start()
        else:
            gains_out[...] = joined
    while sums.active:
        sums.advance(finish)
    for i in range(blocks):
        store_tok(i).wait()
    for chunk in stored:
        store(chunk).wait()


def backward(
    devices, rows, table, gains, w_qkv, gain_one, normed_two_t, cotangent_t, mixed_t, normed_one_t,
    d_hidden, activated, d_attn, d_mixed, tokens, d_resid, packed,
):
    count, width = tokens.shape
    local_len = count // rows
    most = max_tiles(local_len)
    held = local_len + 2 * HALO
    steps = max(len(plan) for plan in sum_plan(devices))
    chunks = len(chunk_pieces(devices))
    shape = jax.ShapeDtypeStruct
    anywhere = pl.BlockSpec(memory_space=pl.ANY)
    vmem = pl.BlockSpec(memory_space=pltpu.VMEM)
    dma = pltpu.SemaphoreType.DMA
    return pl.pallas_call(
        functools.partial(backward_kernel, devices, (most, local_len)),
        out_shape=(
            shape((count, width), BF16),
            shape((48 * PIECE, 128), BF16),
            shape((16, width), F32),
        ),
        in_specs=[smem_spec(), vmem, vmem, vmem] + [anywhere] * 11,
        out_specs=(anywhere, anywhere, vmem),
        scratch_shapes=[
            pltpu.VMEM((48 * PIECE, 128), BF16),
            pltpu.VMEM((48 * PIECE, 128), BF16),
            pltpu.VMEM((48 * PIECE, 128), BF16),
            pltpu.VMEM((width, count), BF16),
            pltpu.VMEM((width, count), BF16),
            pltpu.VMEM((BLOCKS_AHEAD + 1, count, 256), BF16),
            pltpu.VMEM((2, rows, HALO, width), BF16),
            pltpu.VMEM((count, width), BF16),
            pltpu.VMEM((count, width), BF16),
            pltpu.VMEM((count, width), F32),
            pltpu.VMEM((count, width), BF16),
            pltpu.VMEM((12, count, 128), BF16),
            pltpu.VMEM((6, most * TILE + WINDOW, 128), F32),
            pltpu.VMEM((2, held, 128), F32),
            pltpu.VMEM((AHEAD + 1, 9, TILE, 128), BF16),
            pltpu.VMEM((steps, 4, 16, width), F32),
            pltpu.VMEM((8, width), F32),
            dma((chunks, 2 * steps, 3)),
            dma((chunks, 2 * steps, 3)),
            dma((steps, 3)),
            dma((steps, 3)),
            dma((2, 2, rows)),
            dma((7,)),
            dma((BLOCKS_AHEAD + 1,)),
            dma((AHEAD + 1,)),
            dma((count // BLOCK,)),
            dma((chunks,)),
        ],
        compiler_params=pltpu.CompilerParams(
            collective_id=0, has_side_effects=True, vmem_limit_bytes=60 * MIB
        ),
        name="backward",
    )(
        table, gains, w_qkv, gain_one, normed_two_t, cotangent_t, mixed_t, normed_one_t,
        d_hidden, activated, d_attn, d_mixed, tokens, d_resid, packed,
    )


def unpack_kernel(up, down, out, *refs):
    grad_qkv, grad_out, grad_up, grad_down = refs[3:]
    for c in range(4):
        columns = slice(c * 128, (c + 1) * 128)
        grad_up[:, columns] = up[c].astype(F32)
        grad_down[:, columns] = down[c].astype(F32)
    grad_out[...] = out[0].astype(F32)
    for n in range(3):
        grad_qkv[:, n * 128 : (n + 1) * 128] = refs[n][0].astype(F32)


def unpack(summed, width, hidden, wide):
    pieces = summed.reshape(48, PIECE, 128)

    def qkv_piece(n):
        def place(i):
            block = 3 * i + n
            kind, pair = block // 4, block % 4
            return (36 + 6 * (pair // 2) + 2 * kind + pair % 2, 0, 0)

        return pl.BlockSpec((1, PIECE, 128), place)

    shape = jax.ShapeDtypeStruct
    return pl.pallas_call(
        unpack_kernel,
        grid=(4,),
        out_shape=(
            shape((width, wide), F32),
            shape((width, width), F32),
            shape((width, hidden), F32),
            shape((hidden, width), F32),
        ),
        in_specs=[
            pl.BlockSpec((4, PIECE, 128), lambda i: (i, 0, 0)),
            pl.BlockSpec((4, PIECE, 128), lambda i: (4 + i, 0, 0)),
            pl.BlockSpec((1, PIECE, 128), lambda i: (32 + i, 0, 0)),
        ]
        + [qkv_piece(n) for n in range(3)],
        out_specs=(
            pl.BlockSpec((width, wide // 4), lambda i: (0, i)),
            pl.BlockSpec((width, width // 4), lambda i: (0, i)),
            pl.BlockSpec((width, hidden // 4), lambda i: (0, i)),
            pl.BlockSpec((hidden // 4, width), lambda i: (i, 0)),
        ),
        compiler_params=pltpu.CompilerParams(vmem_limit_bytes=60 * MIB),
        name="unpack",
    )(*[pieces] * 6)


def body(
    devices, tokens, item_lengths, w_qkv, w_out, w_up, w_down, gain_one, gain_two, cotangent
):
    rows, local_len, width = tokens.shape
    count = rows * local_len
    gain_one, gain_two = gain_one.reshape(1, width), gain_two.reshape(1, width)
    flat = tokens.reshape(count, width)
    projected, normed_one_t, halo = project(devices, rows, flat, w_qkv, gain_one)
    mixed, packed, table = attend_forward(item_lengths, projected, halo, w_qkv, gain_one)
    (
        output, activated, d_hidden, d_resid, d_attn, d_mixed, normed_two_t, mixed_t, cotangent_t, grad_gain_two
    ) = mlp(local_len, table, flat, mixed, cotangent.reshape(count, width), w_out, w_up, w_down, gain_two)
    grad_tokens, summed, gains = backward(
        devices, rows, table, grad_gain_two, w_qkv, gain_one, normed_two_t, cotangent_t, mixed_t, normed_one_t,
        d_hidden, activated, d_attn, d_mixed, flat, d_resid, packed,
    )
    grads = tuple(unpack(summed, width, w_up.shape[1], w_qkv.shape[1]))
    gains = jnp.sum(gains.reshape(2, 8, width), axis=1)
    placed = (output.reshape(tokens.shape), grad_tokens.reshape(tokens.shape))
    return placed + grads + (gains[0], gains[1])


def solution(mesh):
    rows = P("dp", "seq", None)
    placed = (rows, P("dp", None), P(), P(), P(), P(), P(), P(), rows)
    return jax.shard_map(
        functools.partial(body, (mesh.shape["dp"], mesh.shape["seq"])),
        mesh=mesh,
        in_specs=placed,
        out_specs=(rows, rows, P(), P(), P(), P(), P(), P()),
        check_vma=False,
    )
```

```python
import functools

import jax
import jax.numpy as jnp
from jax import lax
from jax.experimental import pallas as pl
from jax.experimental.pallas import tpu as pltpu
from jax.sharding import PartitionSpec as P

H = 8
E = 64
SEQ_LEN = 4096
LEN_LONG = 250
HALO = 256
TILE = 256
ENTRIES = 8
BLOCK = 256
MLP_BLOCK = 512
PIECE = 512
WINDOW = 64
GROUPS = 2
MOVES = (6, 13, 20, 27, 34)
LATE = 2
APART = 1
AHEAD = 5
BLOCKS_AHEAD = 3

EPSILON = 1e-05
NEGATIVE = -1e30
SCALE2 = 0.125 * 1.4426950408889634
GELU_A = 0.7978845608028654
GELU_B = 0.044715
MIB = 2**20
F32 = jnp.float32
BF16 = jnp.bfloat16
NT = (((1,), (1,)), ((), ()))
TN = (((0,), (0,)), ((), ()))
MESH = pl.DeviceIdType.MESH


def layer_norm(values, scaling):
    centered = values - jnp.mean(values, axis=-1, keepdims=True)
    variance = jnp.mean(centered * centered, axis=-1, keepdims=True)
    return centered * lax.rsqrt(variance + EPSILON) * scaling


def normalize(values):
    centered = values - jnp.mean(values, axis=-1, keepdims=True)
    scale = lax.rsqrt(jnp.mean(centered * centered, axis=-1, keepdims=True) + EPSILON)
    return centered * scale, scale


def normalize_back(upstream, normed, scale):
    mean = jnp.mean(upstream, axis=-1, keepdims=True)
    along = jnp.mean(upstream * normed, axis=-1, keepdims=True)
    return scale * (upstream - mean - normed * along)


def max_tiles(local_len):
    count = 1
    while (count // 2) * 314 + (count % 2) * 64 <= local_len + LEN_LONG - 2:
        count += 1
    return count


def fold_rows(values):
    return jnp.sum(values.reshape(values.shape[0] // 8, 8, values.shape[1]), axis=0)


def plan_tiles(lengths, table, row, tiles):
    slots = lengths.shape[1]
    local_len = tiles[1]
    low = lax.axis_index("seq") * local_len
    high = low + local_len
    base = row * (tiles[0] + 1) * ENTRIES

    def step(k, carry):
        begin, count, tile_begin, in_tile, fitted_end = carry
        true_end = begin + lengths[row, k]
        end = jnp.minimum(true_end, SEQ_LEN)
        touches = (end > low) & (begin < high) & (end > begin)
        fresh = touches & ((count == 0) | (end - tile_begin > TILE))
        count = jnp.where(fresh, count + 1, count)
        tile_begin = jnp.where(fresh, begin, tile_begin)
        in_tile = jnp.where(fresh, 0, in_tile + 1)

        @pl.when(touches)
        def _():
            spot = base + (count - 1) * ENTRIES
            table[spot] = tile_begin - low + HALO
            for j in range(4):

                @pl.when(j >= in_tile)
                def _():
                    table[spot + 1 + j] = end - tile_begin

        fitted_end = jnp.where(true_end <= SEQ_LEN, true_end, fitted_end)
        return (end, count, tile_begin, in_tile, fitted_end)

    zero = jnp.int32(0)
    for b in range(tiles[0]):
        table[base + b * ENTRIES] = 0
    _, count, _, _, fitted_end = lax.fori_loop(0, slots, step, (zero, zero, zero, zero, zero), unroll=5)
    table[base + tiles[0] * ENTRIES] = count
    table[base + tiles[0] * ENTRIES + 1] = fitted_end
    windows = local_len // WINDOW
    unpack_from = tiles[2] * (tiles[0] + 1) * ENTRIES + row * windows * 4

    def window(w, b):
        at = HALO + w * WINDOW

        def end_of(n):
            return table[base + n * ENTRIES] + table[base + n * ENTRIES + 4]

        b = jnp.where(end_of(b) <= at, b + 1, b)
        cut = end_of(b) - at
        table[unpack_from + w * 4] = b * TILE + at - table[base + b * ENTRIES]
        table[unpack_from + w * 4 + 1] = (b + 1) * TILE - cut
        table[unpack_from + w * 4 + 2] = cut
        return b

    lax.fori_loop(0, windows, window, zero)
    return count


def tile_fills(table, spot):
    def segments(positions):
        return sum((positions >= table[spot + 1 + j]).astype(jnp.int32) for j in range(4))

    seg = segments(lax.broadcasted_iota(jnp.int32, (TILE, 128), 0))
    lane = lax.broadcasted_iota(jnp.int32, (TILE, 128), 1) % E
    same = seg == lane
    one_hot = jnp.where(same, 1.0, 0.0)
    across = jnp.where(same, 0.0, NEGATIVE)
    keys = jnp.where(lane < 5, across, jnp.where(lane < 8, 1.0, 0.0))
    return one_hot, keys


def project_kernel(
    devices, local_len, tokens, w_qkv, gain, source, projected, normed_t, halo, zero, halo_sem, zero_sem
):
    step = pl.program_id(0)
    rows = halo.shape[1]
    seq = lax.axis_index("seq")
    after, before = seq < devices[1] - 1, seq > 0

    def halo_copy(side, row):
        start = row * local_len + (local_len - HALO if side == 0 else 0)
        return pltpu.make_async_remote_copy(
            src_ref=source.at[start : start + HALO],
            dst_ref=halo.at[side, row],
            send_sem=halo_sem.at[0, side, row],
            recv_sem=halo_sem.at[1, side, row],
            device_id={"seq": seq + 1 if side == 0 else seq - 1},
            device_id_type=MESH,
        )

    def fill(side, row):
        return pltpu.make_async_copy(zero, halo.at[side, row], zero_sem.at[side, row])

    sides = ((0, after, before), (1, before, after))

    @pl.when(step == 0)
    def _():
        barrier = pltpu.get_barrier_semaphore()
        for d in range(1, devices[1]):
            peer = {"seq": lax.rem(seq + d, devices[1])}
            pl.semaphore_signal(barrier, inc=1, device_id=peer, device_id_type=MESH)
        zero[...] = jnp.zeros_like(zero)
        pl.semaphore_wait(barrier, devices[1] - 1)
        for side, sends, receives in sides:

            @pl.when(sends)
            def _():
                for row in range(rows):
                    halo_copy(side, row).start()

            @pl.when(jnp.logical_not(receives))
            def _():
                for row in range(rows):
                    fill(side, row).start()

    normed, _ = normalize(tokens[...].astype(F32))
    low = (normed * gain[...]).astype(BF16)
    normed_t[...] = low.T
    projected[...] = jnp.dot(low, w_qkv[...], preferred_element_type=F32).astype(BF16)

    @pl.when(step == pl.num_programs(0) - 1)
    def _():
        for side, sends, receives in sides:

            @pl.when(sends)
            def _():
                for row in range(rows):
                    halo_copy(side, row).wait_send()

            @pl.when(receives)
            def _():
                for row in range(rows):
                    halo_copy(side, row).wait_recv()

            @pl.when(jnp.logical_not(receives))
            def _():
                for row in range(rows):
                    fill(side, row).wait()


def project(devices, rows, tokens, w_qkv, gain):
    count, width = tokens.shape
    wide = w_qkv.shape[1]
    block = BLOCK
    dma = pltpu.SemaphoreType.DMA
    return pl.pallas_call(
        functools.partial(project_kernel, devices, count // rows),
        grid=(count // block,),
        out_shape=(
            jax.ShapeDtypeStruct((count, wide), BF16),
            jax.ShapeDtypeStruct((width, count), BF16),
            jax.ShapeDtypeStruct((2, rows, HALO, width), BF16),
        ),
        in_specs=[
            pl.BlockSpec((block, width), lambda i: (i, 0)),
            whole_spec(width, wide),
            whole_spec(1, width),
            pl.BlockSpec(memory_space=pl.ANY),
        ],
        out_specs=(
            pl.BlockSpec((block, wide), lambda i: (i, 0)),
            pl.BlockSpec((width, block), lambda i: (0, i)),
            pl.BlockSpec(memory_space=pl.ANY),
        ),
        scratch_shapes=[pltpu.VMEM((HALO, width), BF16), dma((2, 2, rows)), dma((2, rows))],
        compiler_params=pltpu.CompilerParams(
            collective_id=1, has_side_effects=True, vmem_limit_bytes=60 * MIB
        ),
        name="project",
    )(tokens, w_qkv, gain, tokens)


def attend_forward_kernel(
    tiles, lengths, local, left, right, w_qkv, gain, mixed, packed, table,
    spread, out, hot, stage, sems,
):
    row = pl.program_id(0)
    local_len = local.shape[0]
    count = plan_tiles(lengths, table, row, tiles)
    for side, tokens in enumerate((left, right)):
        normed = layer_norm(tokens[0, 0].astype(F32), gain[...]).astype(BF16)
        made = jnp.dot(normed, w_qkv[...], preferred_element_type=F32).astype(BF16)
        start = side * (HALO + local_len)
        for c in range(12):
            spread[c, start : start + HALO, :] = made[:, c * 128 : (c + 1) * 128].astype(F32)
    for c in range(12):
        spread[c, HALO : HALO + local_len, :] = local[:, c * 128 : (c + 1) * 128].astype(F32)
    low = lax.broadcasted_iota(jnp.int32, (TILE, 128), 1) < E
    place = lax.broadcasted_iota(jnp.int32, (TILE, 128), 1) % E

    def store(slot, at):
        return pltpu.make_async_copy(stage.at[slot], packed.at[at], sems.at[slot])

    def one_tile(b, _):
        spot = (row * (tiles[0] + 1) + b) * ENTRIES
        begin = table[spot]
        slot = lax.rem(b, 2)
        at = row * tiles[0] + b

        @pl.when(b >= 2)
        def _():
            store(slot, at - 2).wait()

        one_hot, key_fill = tile_fills(table, spot)
        hot[...] = one_hot
        for group in range(GROUPS):
            stage[slot, group, 8] = key_fill.astype(BF16)
        loaded, held = {}, {}
        key_fill = key_fill.astype(BF16)

        def front(h):
            pair, side = h // 2, h % 2
            group, i = pair // 2, pair % 2
            if side == 0:
                loaded[pair] = tuple(spread[4 * n + pair, pl.ds(begin, TILE), :].astype(BF16) for n in range(3))
                for n in range(3):
                    stage[slot, group, 2 * n + i] = loaded[pair][n]
            q, k, _ = loaded[pair]
            own = low if side == 0 else ~low
            return lax.dot_general(
                jnp.where(own, q, hot[...].astype(BF16)),
                jnp.where(own, k, key_fill),
                NT,
                preferred_element_type=F32,
            )

        def back(h, scores):
            pair, side = h // 2, h % 2
            v = loaded[pair][2]
            zero = jnp.zeros_like(v)
            own = low if side == 0 else ~low
            peak = jnp.max(scores, axis=1, keepdims=True)
            weights = jnp.exp2((scores - peak) * SCALE2).astype(BF16)
            both = jnp.concatenate([jnp.where(own, v, zero), jnp.where(own, zero + 1, zero)], axis=1)
            if side == 0:
                held[pair] = ((weights, both), peak)
                return
            made = jnp.dot(
                jnp.concatenate([held[pair][0][0], weights], axis=1),
                jnp.concatenate([held[pair][0][1], both], axis=0),
                preferred_element_type=F32,
            )
            total = made[:, 128:]
            out[pair, pl.ds(begin, TILE), :] = made[:, :128] / total
            total = pltpu.roll(total, E, 1)
            log_sum = jnp.where(low, peak, held[pair][1]) + jnp.log2(total) * (1.0 / SCALE2)
            first = log_sum.astype(BF16).astype(F32)
            rest = log_sum - first
            second = rest.astype(BF16).astype(F32)
            fill = jnp.where(place == 7, second - rest, hot[...])
            fill = jnp.where(place == 6, -second, fill)
            stage[slot, pair // 2, 6 + pair % 2] = jnp.where(place == 5, -first, fill).astype(BF16)

        ahead = [front(h) for h in range(2)]
        for h in range(8):
            now = ahead.pop(0)
            if h + 2 < 8:
                ahead.append(front(h + 2))
            back(h, now)
        store(slot, at).start()
        return 0

    lax.fori_loop(0, count, one_tile, 0)
    for c in range(4):
        mixed[:, c * 128 : (c + 1) * 128] = out[c, HALO : HALO + local_len, :].astype(BF16)

    @pl.when(count >= 2)
    def _():
        store(lax.rem(count, 2), row * tiles[0] + count - 2).wait()

    store(lax.rem(count + 1, 2), row * tiles[0] + count - 1).wait()


def attend_forward(lengths, local, halo, w_qkv, gain):
    rows = lengths.shape[0]
    width = halo.shape[3]
    local_len = local.shape[0] // rows
    most = max_tiles(local_len)
    held = local_len + 2 * HALO
    return pl.pallas_call(
        functools.partial(attend_forward_kernel, (most, local_len, rows)),
        grid=(rows,),
        out_shape=(
            jax.ShapeDtypeStruct((rows * local_len, width), BF16),
            jax.ShapeDtypeStruct((rows * most, GROUPS, 9, TILE, 128), BF16),
            jax.ShapeDtypeStruct(
                (rows * (most + 1) * ENTRIES + rows * (local_len // WINDOW) * 4,), jnp.int32
            ),
        ),
        in_specs=[
            smem_spec(),
            pl.BlockSpec((local_len, 3 * width), lambda r: (r, 0)),
            pl.BlockSpec((1, 1, HALO, width), lambda r: (0, r, 0, 0)),
            pl.BlockSpec((1, 1, HALO, width), lambda r: (1, r, 0, 0)),
            whole_spec(width, 3 * width),
            whole_spec(1, width),
        ],
        out_specs=(
            pl.BlockSpec((local_len, width), lambda r: (r, 0)),
            pl.BlockSpec(memory_space=pl.ANY),
            smem_spec(),
        ),
        scratch_shapes=[
            pltpu.VMEM((12, held, 128), F32),
            pltpu.VMEM((4, held, 128), F32),
            pltpu.VMEM((TILE, 128), F32),
            pltpu.VMEM((2, GROUPS, 9, TILE, 128), BF16),
            pltpu.SemaphoreType.DMA((2,)),
        ],
        compiler_params=pltpu.CompilerParams(vmem_limit_bytes=60 * MIB),
        name="attend_forward",
    )(lengths, local, halo, halo, w_qkv, gain)


def interleave(chains, lag):
    live = {n: chain for n, chain in enumerate(chains)}
    turn = 0
    while live:
        for n in list(live):
            if turn >= n * lag and next(live[n], None) is None:
                del live[n]
        turn += 1


def mlp_kernel(
    tiles, table, tokens, mixed, cotangent, w_out, w_up, w_down, gain,
    output, activated, d_hidden, d_resid, d_attn, d_mixed, normed_t, mixed_t, cotangent_t, grad_gain,
):
    step = pl.program_id(0)
    most, local_len = tiles
    block = tokens.shape[0]
    per_row = local_len // block
    row = step // per_row
    begin = lax.axis_index("seq") * local_len + (step % per_row) * block
    fitted_end = table[(row * (most + 1) + most) * ENTRIES + 1]
    piece = 256
    pieces = w_up.shape[1] // piece

    @pl.when(step == 0)
    def _():
        grad_gain[...] = jnp.zeros_like(grad_gain)

    def chain(first):
        part = slice(first, first + BLOCK)
        positions = begin + first + lax.broadcasted_iota(jnp.int32, (BLOCK, 1), 0)
        valid = positions < fitted_end
        attn = jnp.dot(mixed[part, :], w_out[...], preferred_element_type=F32)
        dy = cotangent[part, :]
        yield True
        resid = tokens[part, :].astype(F32) + jnp.where(valid, attn, 0.0)
        normed, scale = normalize(resid)
        low = (normed * gain[...]).astype(BF16)
        yield True

        def front(j):
            columns = slice(j * piece, (j + 1) * piece)
            hidden = jnp.dot(low, w_up[:, columns], preferred_element_type=F32)
            return hidden, lax.dot_general(dy, w_down[columns, :], NT, preferred_element_type=F32)

        dense, d_normed = resid, 0.0
        ahead = front(0)
        for j in range(pieces):
            columns = slice(j * piece, (j + 1) * piece)
            hidden, d_act = ahead
            if j + 1 < pieces:
                ahead = front(j + 1)
            square = hidden * hidden
            bent = jnp.tanh(hidden * (GELU_A + (GELU_A * GELU_B) * square))
            half = 0.5 + 0.5 * bent
            act = (hidden * half).astype(BF16)
            slope = half + (0.5 - 0.5 * bent * bent) * hidden * (GELU_A + (3.0 * GELU_A * GELU_B) * square)
            grad = (d_act * slope).astype(BF16)
            activated[j, part, :] = act
            d_hidden[j, part, :] = grad
            dense += jnp.dot(act, w_down[columns, :], preferred_element_type=F32)
            d_normed += lax.dot_general(grad, w_up[:, columns], NT, preferred_element_type=F32)
            if j == 1:
                normed_t[:, part] = low.T
            if j == 2:
                mixed_t[:, part] = mixed[part, :].T
            if j == 3:
                cotangent_t[:, part] = dy.T
            yield True
        output[part, :] = dense.astype(BF16)
        grad_gain[...] += fold_rows(d_normed * normed)
        made = dy.astype(F32) + normalize_back(d_normed * gain[...], normed, scale)
        yield True
        d_resid[part, :] = made
        attn_low = jnp.where(valid, made, 0.0).astype(BF16)
        for n in range(attn_low.shape[1] // 256):
            d_attn[n, part, :] = attn_low[:, n * 256 : (n + 1) * 256]
        d_mixed[part, :] = lax.dot_general(attn_low, w_out[...], NT, preferred_element_type=F32).astype(BF16)

    interleave([chain(first) for first in range(0, block, BLOCK)], 3)


def mlp(local_len, table, tokens, mixed, cotangent, w_out, w_up, w_down, gain):
    count, width = tokens.shape
    hidden = w_up.shape[1]
    rows_of = lambda w: pl.BlockSpec((MLP_BLOCK, w), lambda i: (i, 0))
    blocks_of = lambda w: pl.BlockSpec((w // 256, MLP_BLOCK, 256), lambda i: (0, i, 0))
    turned = pl.BlockSpec((width, MLP_BLOCK), lambda i: (0, i))
    shape = jax.ShapeDtypeStruct
    return pl.pallas_call(
        functools.partial(mlp_kernel, (max_tiles(local_len), local_len)),
        grid=(count // MLP_BLOCK,),
        out_shape=(
            shape((count, width), BF16),
            shape((hidden // 256, count, 256), BF16),
            shape((hidden // 256, count, 256), BF16),
            shape((count, width), F32),
            shape((width // 256, count, 256), BF16),
            shape((count, width), BF16),
            shape((width, count), BF16),
            shape((width, count), BF16),
            shape((width, count), BF16),
            shape((8, width), F32),
        ),
        in_specs=[
            smem_spec(),
            rows_of(width),
            rows_of(width),
            rows_of(width),
            whole_spec(width, width),
            whole_spec(width, hidden),
            whole_spec(hidden, width),
            whole_spec(1, width),
        ],
        out_specs=(
            rows_of(width),
            blocks_of(hidden),
            blocks_of(hidden),
            rows_of(width),
            blocks_of(width),
            rows_of(width),
            turned,
            turned,
            turned,
            whole_spec(8, width),
        ),
        compiler_params=pltpu.CompilerParams(vmem_limit_bytes=60 * MIB),
        name="mlp",
    )(table, tokens, mixed, cotangent, w_out, w_up, w_down, gain)


def tile_backward(pairs, packed, fills, grad_of, put):
    low = lax.broadcasted_iota(jnp.int32, (TILE, 128), 1) < E
    key_fill = fills(pairs)
    loaded = {}

    def front(h):
        pair, side = h // 2, h % 2
        if side == 0:
            loaded[pair] = (packed(pair), packed(pairs + pair), packed(2 * pairs + pair), grad_of(pair), fills(pair))
        q, k, v, o, fill = loaded[pair]
        own = low if side == 0 else ~low
        own_o = jnp.where(own, o, jnp.zeros_like(o))
        scores = lax.dot_general(
            jnp.where(own, k, key_fill), jnp.where(own, q, fill), NT, preferred_element_type=F32
        )
        d_probs = lax.dot_general(v, own_o, NT, preferred_element_type=F32)
        return scores, d_probs, own_o

    made = {}

    def back(h, scores, d_probs, own_o):
        pair, side = h // 2, h % 2
        q, k, _, _, _ = loaded[pair]
        own = low if side == 0 else ~low
        zero = jnp.zeros_like(q)
        probs = jnp.exp2(scores * SCALE2)
        weighted = probs * d_probs
        inner = jnp.sum(weighted, axis=0, keepdims=True)
        d_scores = (weighted - probs * inner).astype(BF16)
        dv = jnp.dot(probs.astype(BF16), own_o, preferred_element_type=F32)
        dk = jnp.dot(d_scores, jnp.where(own, q, zero), preferred_element_type=F32)
        dq = lax.dot_general(d_scores, jnp.where(own, k, zero), TN, preferred_element_type=F32)
        if side == 0:
            made[pair] = (dq, dk, dv)
        else:
            first = made[pair]
            put(pair, (first[0] + dq) * 0.125)
            put(pairs + pair, (first[1] + dk) * 0.125)
            put(2 * pairs + pair, first[2] + dv)

    ahead = [front(0), front(1)]
    for h in range(2 * pairs):
        now = ahead.pop(0)
        if h + 2 < 2 * pairs:
            ahead.append(front(h + 2))
        back(h, *now)


def whole_spec(*shape):
    return pl.BlockSpec(shape, lambda r: (0,) * len(shape))


def smem_spec():
    return pl.BlockSpec(memory_space=pltpu.SMEM)


def sum_plan(devices):
    dp, seq = devices
    chip = [1 << b for b in range(1, dp.bit_length() - 1)]
    along = [1 << b for b in range(seq.bit_length() - 1)]

    def paired(axis, bits):
        return [(axis, tuple(bits[n : n + 2])) for n in range(0, len(bits), 2)]

    core, z = [("dp", (1,))], paired("seq", along)
    one = [("dp", (bit,)) for bit in chip]
    return [core + one + z, core + one[::-1] + z, core + paired("dp", chip) + z]


def chunk_pieces(devices):
    unit = max(1, 16 * devices[0] * devices[1] // PIECE)
    if unit == 1:
        return [4] * 8 + [5, 5, 3, 3]
    return [unit] * (48 // unit)


class GradSum:
    def __init__(self, devices, work, slots, done, send_sem, recv_sem):
        self.plans = sum_plan(devices)
        self.work, self.slots, self.done = work, slots, done
        self.send_sem, self.recv_sem = send_sem, recv_sem
        self.here = {"dp": lax.axis_index("dp"), "seq": lax.axis_index("seq")}
        self.sizes = chunk_pieces(devices)
        self.paths, self.active = [], []
        self.queue, self.clock, self.free_at = [], 0, 0
        base = 0
        for chunk, pieces in enumerate(self.sizes):
            offset, rows, slot, path = base, pieces * PIECE, base, []
            for axis, bits in self.plan(chunk):
                mine, others = self.peers(axis, bits)
                rows //= 1 << len(bits)
                keep = offset + mine * rows
                path.append((keep, [offset + n * rows for n, _ in others], slot, rows))
                offset, slot = keep, slot + rows * len(others)
            self.paths.append(path)
            base += pieces * PIECE

    def plan(self, chunk):
        return self.plans[2 if chunk >= len(self.sizes) - LATE else chunk % 2]

    def peers(self, axis, bits):
        index = self.here[axis]
        own = [(index // bit) % 2 for bit in bits]
        others = []
        for mask in range(1, 1 << len(bits)):
            number, to = 0, index
            for i, bit in enumerate(bits):
                flip = (mask >> i) % 2
                number = number + (1 - own[i] if flip else own[i]) * (1 << i)
                to = to + flip * (bit - 2 * bit * own[i])
            others.append((number, {axis: to}))
        return sum(own[i] * (1 << i) for i in range(len(bits))), others

    def copies(self, chunk, t, pairs):
        axis, bits = self.plan(chunk)[min(t, 2 * len(self.plan(chunk)) - 1 - t)]
        return [
            pltpu.make_async_remote_copy(
                src_ref=source,
                dst_ref=target,
                send_sem=self.send_sem.at[chunk, t, n],
                recv_sem=self.recv_sem.at[chunk, t, n],
                device_id=to,
                device_id_type=MESH,
            )
            for n, ((source, target), (_, to)) in enumerate(zip(pairs, self.peers(axis, bits)[1]))
        ]

    def spreading(self, chunk, s):
        _, gives, slot, rows = self.paths[chunk][s]
        return self.copies(
            chunk,
            s,
            [
                (
                    self.work.at[pl.ds(pl.multiple_of(give, 16), rows)],
                    self.slots.at[slot + n * rows : slot + (n + 1) * rows],
                )
                for n, give in enumerate(gives)
            ],
        )

    def gathering(self, chunk, s, received):
        keep, gives, _, rows = self.paths[chunk][s]
        parts = [
            self.done.at[pl.ds(pl.multiple_of(give if received else keep, 16), rows)] for give in gives
        ]
        return self.copies(chunk, 2 * len(self.plan(chunk)) - 1 - s, [(part, part) for part in parts])

    def add(self, chunk, s):
        keep, gives, slot, rows = self.paths[chunk][s]
        into = self.done if s + 1 == len(self.plan(chunk)) else self.work
        count = next(n for n in range(1, rows) if rows % (16 * n) == 0 and rows // n <= 512)
        block = rows // count

        @pl.loop(0, count)
        def _(i):
            at = pl.ds(pl.multiple_of(keep + i * block, 16), block)
            total = self.work[at, :].astype(F32)
            for n in range(len(gives)):
                from_at = pl.ds(pl.multiple_of(slot + n * rows + i * block, 16), block)
                total += self.slots[from_at, :].astype(F32)
            into[at, :] = total.astype(BF16)

    def event(self, chunk, t):
        steps = len(self.plan(chunk))
        if 0 < t <= steps:
            for copy in self.spreading(chunk, t - 1):
                copy.wait()
            self.add(chunk, t - 1)
        elif t > steps:
            for copy in self.gathering(chunk, 2 * steps - t, False):
                copy.wait_send()
            for copy in self.gathering(chunk, 2 * steps - t, True):
                copy.wait_recv()
        if t < steps:
            for copy in self.spreading(chunk, t):
                copy.start()
        elif t < 2 * steps:
            for copy in self.gathering(chunk, 2 * steps - 1 - t, False):
                copy.start()
        return t == 2 * steps

    def begin(self, chunks, now=False):
        self.queue += chunks
        while self.queue and (now or self.clock >= self.free_at):
            for chunk in self.queue[:2]:
                self.event(chunk, 0)
                self.active.append([chunk, 1])
            self.queue = self.queue[2:]
            self.free_at = self.clock + APART

    def advance(self, finish):
        self.clock += 1
        for entry in list(self.active):
            if self.event(*entry):
                finish(entry[0])
                self.active.remove(entry)
            entry[1] += 1
        self.begin([])


def backward_kernel(
    devices, tiles, table, gains, w_qkv, gain_one,
    normed_two_t, cotangent_t, mixed_t, normed_one_t, d_hidden, activated, d_attn, d_mixed, tokens, d_resid,
    packed,
    grad_tokens, summed, gains_out,
    work, slots, done, left_a, left_b, right_block, halo, d_mix, tok, resid, made_tok, d_proj, bins, d_out,
    tile_in, gain_slots, gain_one_sum,
    send_sem, recv_sem, gain_send, gain_recv, halo_sem, load_sem, block_sem, tile_sem, store_sem, out_sem,
):
    most, local_len = tiles
    count = tok.shape[0]
    rows = count // local_len
    seq = lax.axis_index("seq")
    sums = GradSum(devices, work, slots, done, send_sem, recv_sem)

    barrier = pltpu.get_barrier_semaphore()
    after, before = seq < devices[1] - 1, seq > 0
    peers = [to for axis, bits in sums.plans[2] if axis == "dp" for _, to in sums.peers(axis, bits)[1]]
    peers += [{"seq": lax.rem(seq + d, devices[1])} for d in range(1, devices[1])]
    for peer in peers:
        pl.semaphore_signal(barrier, inc=1, device_id=peer, device_id_type=MESH)

    load_a = lambda ref, k: pltpu.make_async_copy(ref, left_a, load_sem.at[k])
    load_b = lambda ref, k: pltpu.make_async_copy(ref, left_b, load_sem.at[k])
    load_block = lambda ref, block, slot: pltpu.make_async_copy(
        ref.at[block], right_block.at[slot], block_sem.at[slot]
    )
    load_mix = pltpu.make_async_copy(d_mixed, d_mix, load_sem.at[4])
    load_tok = pltpu.make_async_copy(tokens, tok, load_sem.at[5])
    load_resid = pltpu.make_async_copy(d_resid, resid, load_sem.at[6])
    load_a(normed_two_t, 0).start()
    for n in range(BLOCKS_AHEAD):
        load_block(d_hidden, n, n).start()
    load_b(cotangent_t, 1).start()
    load_mix.start()

    pl.semaphore_wait(barrier, len(peers))

    def halo_copy(side, row):
        start = row * local_len + (local_len - HALO if side == 0 else 0)
        return pltpu.make_async_remote_copy(
            src_ref=d_mixed.at[start : start + HALO],
            dst_ref=halo.at[side, row],
            send_sem=halo_sem.at[0, side, row],
            recv_sem=halo_sem.at[1, side, row],
            device_id={"seq": seq + 1 if side == 0 else seq - 1},
            device_id_type=MESH,
        )

    for side, sends, receives in ((0, after, before), (1, before, after)):

        @pl.when(sends)
        def _():
            for row in range(rows):
                halo_copy(side, row).start()

        @pl.when(jnp.logical_not(receives))
        def _():
            for row in range(rows):
                halo[side, row] = jnp.zeros(halo.shape[2:], BF16)

    stored = []

    def store(chunk):
        part = pl.ds(sum(sums.sizes[:chunk]) * PIECE, sums.sizes[chunk] * PIECE)
        return pltpu.make_async_copy(done.at[part], summed.at[part], out_sem.at[chunk])

    def finish(chunk):
        store(chunk).start()
        stored.append(chunk)

    begun = [0]

    def ready(pieces):
        chunks = []
        while begun[0] < len(sums.sizes) and sum(sums.sizes[: begun[0] + 1]) <= pieces:
            chunks.append(begun[0])
            begun[0] += 1
        sums.begin(chunks, pieces >= 48)

    def put_columns(base, block, product):
        low = product.astype(BF16)
        for i in range(2):
            at = pl.multiple_of((base + 2 * block + i) * PIECE, PIECE)
            work[pl.ds(at, PIECE), :] = low[:, i * 128 : (i + 1) * 128]

    def put_rows(base, block, product):
        low = product.T.astype(BF16)
        for c in range(4):
            at = (base + (block // 2) * 4 + c) * PIECE + (block % 2) * 256
            work[pl.ds(pl.multiple_of(at, 256), 256), :] = low[:, c * 128 : (c + 1) * 128]

    half = d_hidden.shape[0] // 2
    runs = [
        (left_a, d_hidden, 0, half, 0, put_columns),
        (left_a, d_hidden, half, half, 0, put_columns),
        (left_b, activated, 0, half, 16, put_rows),
        (left_b, activated, half, half, 16, put_rows),
        (left_a, d_attn, 0, 2, 32, put_columns),
    ]
    waits = {0: load_a(normed_two_t, 0), 2: load_b(cotangent_t, 1), 4: load_a(mixed_t, 2)}
    at = 0
    for n, (lhs, ref, first, blocks, base, put) in enumerate(runs):
        if n in waits:
            waits[n].wait()

        upcoming = [(run[1], run[2], run[3]) for run in runs[n:]][:3]

        def one_block(j, _, n=n, upcoming=upcoming, lhs=lhs, ref=ref, first=first, blocks=blocks, base=base, put=put, at=at):
            slot, later = lax.rem(at + j, BLOCKS_AHEAD + 1), lax.rem(at + j + BLOCKS_AHEAD, BLOCKS_AHEAD + 1)
            load_block(ref, first + j, slot).wait()
            until = 0
            for next_ref, next_first, next_blocks in upcoming:
                since, until = until, until + next_blocks

                @pl.when((j + BLOCKS_AHEAD >= since) & (j + BLOCKS_AHEAD < until))
                def _():
                    load_block(next_ref, next_first + j + BLOCKS_AHEAD - since, later).start()

            put(base, first + j, jnp.dot(lhs[...], right_block[slot], preferred_element_type=F32))
            return 0

        lax.fori_loop(0, blocks, one_block, 0)
        at += blocks
        if n == 1:
            load_a(mixed_t, 2).start()
        if n == 3:
            load_b(normed_one_t, 3).start()
            load_tok.start()
            load_resid.start()
        if n > 0:
            sums.advance(finish)
        if n < 4:
            ready(8 * (n + 1))

    per_group = rows * most
    total = GROUPS * per_group
    unpack_from = rows * (most + 1) * ENTRIES
    windows = local_len // WINDOW

    def load_tile(step, slot):
        group, spot = step // per_group, lax.rem(step, per_group)
        return pltpu.make_async_copy(packed.at[spot, group], tile_in.at[slot], tile_sem.at[slot])

    for n in range(AHEAD):
        load_tile(n, n).start()
    load_mix.wait()
    for side, sends, receives in ((0, after, before), (1, before, after)):

        @pl.when(sends)
        def _():
            for row in range(rows):
                halo_copy(side, row).wait_send()

        @pl.when(receives)
        def _():
            for row in range(rows):
                halo_copy(side, row).wait_recv()

    def one_tile(step, _):
        slot = lax.rem(step, AHEAD + 1)
        group, spot = step // per_group, lax.rem(step, per_group)
        row, b = spot // most, lax.rem(spot, most)
        load_tile(step, slot).wait()

        @pl.when(step + AHEAD < total)
        def _():
            load_tile(step + AHEAD, lax.rem(step + AHEAD, AHEAD + 1)).start()

        @pl.when(b == 0)
        def _():
            start = pl.multiple_of(row * local_len, local_len)
            for i in range(2):
                columns = pl.ds(pl.multiple_of((2 * group + i) * 128, 128), 128)
                d_out[i, :HALO, :] = halo[0, row, :, columns].astype(F32)
                d_out[i, HALO : HALO + local_len, :] = d_mix[pl.ds(start, local_len), columns].astype(F32)
                d_out[i, HALO + local_len :, :] = halo[1, row, :, columns].astype(F32)

        begin = table[(row * (most + 1) + b) * ENTRIES]

        def put(c, values):
            bins[c, pl.ds(pl.multiple_of(b * TILE, TILE), TILE), :] = values

        tile_backward(
            2,
            lambda c: tile_in[slot, c],
            lambda c: tile_in[slot, 6 + c],
            lambda c: d_out[c, pl.ds(begin, TILE), :].astype(BF16),
            put,
        )

        @pl.when(b == most - 1)
        def _():
            @pl.loop(0, windows)
            def _(w):
                entry = unpack_from + (row * windows + w) * 4
                one, two, cut = table[entry], table[entry + 1], table[entry + 2]
                in_one = lax.broadcasted_iota(jnp.int32, (WINDOW, 128), 0) < cut
                to = pl.multiple_of(row * local_len + w * WINDOW, WINDOW)
                for c in range(6):
                    values = jnp.where(
                        in_one, bins[c, pl.ds(one, WINDOW), :], bins[c, pl.ds(two, WINDOW), :]
                    )
                    d_proj[group * 6 + c, pl.ds(to, WINDOW), :] = values.astype(BF16)

        def qkv_gradient(g):
            for kind in range(3):
                both = jnp.concatenate([d_proj[g * 6 + 2 * kind + i] for i in range(2)], axis=1)
                product = jnp.dot(left_b[...], both, preferred_element_type=F32).astype(BF16)
                for i in range(2):
                    piece = 36 + 6 * g + 2 * kind + i
                    work[piece * PIECE : (piece + 1) * PIECE, :] = product[:, i * 128 : (i + 1) * 128]

        for k in range(total):
            ends_group = (k + 1) % per_group == 0
            moves = k in MOVES and sums.active
            if not (ends_group or moves):
                continue

            @pl.when(step == k)
            def _():
                if moves:
                    sums.advance(finish)
                if ends_group:
                    g = k // per_group
                    if g == 0:
                        load_b(normed_one_t, 3).wait()
                    qkv_gradient(g)
                    ready(42 + 6 * g)

        return 0

    lax.fori_loop(0, total, one_tile, 0)

    load_tok.wait()
    load_resid.wait()
    gain_one_sum[...] = jnp.zeros_like(gain_one_sum)
    blocks = count // BLOCK

    def store_tok(i):
        part = pl.ds(pl.multiple_of(i * BLOCK, BLOCK), BLOCK)
        return pltpu.make_async_copy(made_tok.at[part], grad_tokens.at[part], store_sem.at[i])

    def input_block(i, _):
        part = pl.ds(pl.multiple_of(i * BLOCK, BLOCK), BLOCK)
        order = [6 * (pair // 2) + 2 * kind + pair % 2 for kind in range(3) for pair in range(4)]
        d_projected = jnp.concatenate([d_proj[c, part, :] for c in order], axis=1)
        d_normed = lax.dot_general(d_projected, w_qkv[...], NT, preferred_element_type=F32)
        normed, scale = normalize(tok[part, :].astype(F32))
        gain_one_sum[...] += fold_rows(d_normed * normed)
        back = normalize_back(d_normed * gain_one[...], normed, scale)
        made_tok[part, :] = (resid[part, :] + back).astype(BF16)
        store_tok(i).start()
        for k in range(2, blocks, 3):

            @pl.when(i == k)
            def _():
                sums.advance(finish)

        return 0

    lax.fori_loop(0, blocks, input_block, 0)

    gain_plan = sums.plans[2]

    def gain_copies(s):
        return [
            pltpu.make_async_remote_copy(
                src_ref=gain_slots.at[s, 0],
                dst_ref=gain_slots.at[s, n + 1],
                send_sem=gain_send.at[s, n],
                recv_sem=gain_recv.at[s, n],
                device_id=to,
                device_id_type=MESH,
            )
            for n, (_, to) in enumerate(sums.peers(*gain_plan[s])[1])
        ]

    gain_slots[0, 0, :8] = gain_one_sum[...]
    gain_slots[0, 0, 8:] = gains[...]
    for copy in gain_copies(0):
        copy.start()
    for s in range(len(gain_plan)):
        if sums.active:
            sums.advance(finish)
        joined = gain_slots[s, 0]
        for n, copy in enumerate(gain_copies(s)):
            copy.wait()
            joined += gain_slots[s, n + 1]
        if s + 1 < len(gain_plan):
            gain_slots[s + 1, 0] = joined
            for copy in gain_copies(s + 1):
                copy.start()
        else:
            gains_out[...] = joined
    while sums.active:
        sums.advance(finish)
    for i in range(blocks):
        store_tok(i).wait()
    for chunk in stored:
        store(chunk).wait()


def backward(
    devices, rows, table, gains, w_qkv, gain_one, normed_two_t, cotangent_t, mixed_t, normed_one_t,
    d_hidden, activated, d_attn, d_mixed, tokens, d_resid, packed,
):
    count, width = tokens.shape
    local_len = count // rows
    most = max_tiles(local_len)
    held = local_len + 2 * HALO
    steps = max(len(plan) for plan in sum_plan(devices))
    chunks = len(chunk_pieces(devices))
    shape = jax.ShapeDtypeStruct
    anywhere = pl.BlockSpec(memory_space=pl.ANY)
    vmem = pl.BlockSpec(memory_space=pltpu.VMEM)
    dma = pltpu.SemaphoreType.DMA
    return pl.pallas_call(
        functools.partial(backward_kernel, devices, (most, local_len)),
        out_shape=(
            shape((count, width), BF16),
            shape((48 * PIECE, 128), BF16),
            shape((16, width), F32),
        ),
        in_specs=[smem_spec(), vmem, vmem, vmem] + [anywhere] * 11,
        out_specs=(anywhere, anywhere, vmem),
        scratch_shapes=[
            pltpu.VMEM((48 * PIECE, 128), BF16),
            pltpu.VMEM((48 * PIECE, 128), BF16),
            pltpu.VMEM((48 * PIECE, 128), BF16),
            pltpu.VMEM((width, count), BF16),
            pltpu.VMEM((width, count), BF16),
            pltpu.VMEM((BLOCKS_AHEAD + 1, count, 256), BF16),
            pltpu.VMEM((2, rows, HALO, width), BF16),
            pltpu.VMEM((count, width), BF16),
            pltpu.VMEM((count, width), BF16),
            pltpu.VMEM((count, width), F32),
            pltpu.VMEM((count, width), BF16),
            pltpu.VMEM((12, count, 128), BF16),
            pltpu.VMEM((6, most * TILE + WINDOW, 128), F32),
            pltpu.VMEM((2, held, 128), F32),
            pltpu.VMEM((AHEAD + 1, 9, TILE, 128), BF16),
            pltpu.VMEM((steps, 4, 16, width), F32),
            pltpu.VMEM((8, width), F32),
            dma((chunks, 2 * steps, 3)),
            dma((chunks, 2 * steps, 3)),
            dma((steps, 3)),
            dma((steps, 3)),
            dma((2, 2, rows)),
            dma((7,)),
            dma((BLOCKS_AHEAD + 1,)),
            dma((AHEAD + 1,)),
            dma((count // BLOCK,)),
            dma((chunks,)),
        ],
        compiler_params=pltpu.CompilerParams(
            collective_id=0, has_side_effects=True, vmem_limit_bytes=60 * MIB
        ),
        name="backward",
    )(
        table, gains, w_qkv, gain_one, normed_two_t, cotangent_t, mixed_t, normed_one_t,
        d_hidden, activated, d_attn, d_mixed, tokens, d_resid, packed,
    )


def unpack_kernel(up, down, out, *refs):
    grad_qkv, grad_out, grad_up, grad_down = refs[3:]
    for c in range(4):
        columns = slice(c * 128, (c + 1) * 128)
        grad_up[:, columns] = up[c].astype(F32)
        grad_down[:, columns] = down[c].astype(F32)
    grad_out[...] = out[0].astype(F32)
    for n in range(3):
        grad_qkv[:, n * 128 : (n + 1) * 128] = refs[n][0].astype(F32)


def unpack(summed, width, hidden, wide):
    pieces = summed.reshape(48, PIECE, 128)

    def qkv_piece(n):
        def place(i):
            block = 3 * i + n
            kind, pair = block // 4, block % 4
            return (36 + 6 * (pair // 2) + 2 * kind + pair % 2, 0, 0)

        return pl.BlockSpec((1, PIECE, 128), place)

    shape = jax.ShapeDtypeStruct
    return pl.pallas_call(
        unpack_kernel,
        grid=(4,),
        out_shape=(
            shape((width, wide), F32),
            shape((width, width), F32),
            shape((width, hidden), F32),
            shape((hidden, width), F32),
        ),
        in_specs=[
            pl.BlockSpec((4, PIECE, 128), lambda i: (i, 0, 0)),
            pl.BlockSpec((4, PIECE, 128), lambda i: (4 + i, 0, 0)),
            pl.BlockSpec((1, PIECE, 128), lambda i: (32 + i, 0, 0)),
        ]
        + [qkv_piece(n) for n in range(3)],
        out_specs=(
            pl.BlockSpec((width, wide // 4), lambda i: (0, i)),
            pl.BlockSpec((width, width // 4), lambda i: (0, i)),
            pl.BlockSpec((width, hidden // 4), lambda i: (0, i)),
            pl.BlockSpec((hidden // 4, width), lambda i: (i, 0)),
        ),
        compiler_params=pltpu.CompilerParams(vmem_limit_bytes=60 * MIB),
        name="unpack",
    )(*[pieces] * 6)


def body(
    devices, tokens, item_lengths, w_qkv, w_out, w_up, w_down, gain_one, gain_two, cotangent
):
    rows, local_len, width = tokens.shape
    count = rows * local_len
    gain_one, gain_two = gain_one.reshape(1, width), gain_two.reshape(1, width)
    flat = tokens.reshape(count, width)
    projected, normed_one_t, halo = project(devices, rows, flat, w_qkv, gain_one)
    mixed, packed, table = attend_forward(item_lengths, projected, halo, w_qkv, gain_one)
    (
        output, activated, d_hidden, d_resid, d_attn, d_mixed, normed_two_t, mixed_t, cotangent_t, grad_gain_two
    ) = mlp(local_len, table, flat, mixed, cotangent.reshape(count, width), w_out, w_up, w_down, gain_two)
    grad_tokens, summed, gains = backward(
        devices, rows, table, grad_gain_two, w_qkv, gain_one, normed_two_t, cotangent_t, mixed_t, normed_one_t,
        d_hidden, activated, d_attn, d_mixed, flat, d_resid, packed,
    )
    grads = tuple(unpack(summed, width, w_up.shape[1], w_qkv.shape[1]))
    gains = jnp.sum(gains.reshape(2, 8, width), axis=1)
    placed = (output.reshape(tokens.shape), grad_tokens.reshape(tokens.shape))
    return placed + grads + (gains[0], gains[1])


def solution(mesh):
    rows = P("dp", "seq", None)
    placed = (rows, P("dp", None), P(), P(), P(), P(), P(), P(), rows)
    return jax.shard_map(
        functools.partial(body, (mesh.shape["dp"], mesh.shape["seq"])),
        mesh=mesh,
        in_specs=placed,
        out_specs=(rows, rows, P(), P(), P(), P(), P(), P()),
        check_vma=False,
    )
```

```python
import functools

import jax
import jax.numpy as jnp
from jax import lax
from jax.experimental import pallas as pl
from jax.experimental.pallas import tpu as pltpu
from jax.sharding import PartitionSpec as P

H = 8
E = 64
SEQ_LEN = 4096
LEN_LONG = 250
HALO = 256
TILE = 256
ENTRIES = 8
BLOCK = 256
MLP_BLOCK = 512
PIECE = 512
WINDOW = 64
GROUPS = 2
MOVES = (2, 8, 14, 20, 27, 34)
LATE = 2
APART = 1
AHEAD = 5
BLOCKS_AHEAD = 3

EPSILON = 1e-05
NEGATIVE = -1e30
SCALE2 = 0.125 * 1.4426950408889634
GELU_A = 0.7978845608028654
GELU_B = 0.044715
MIB = 2**20
F32 = jnp.float32
BF16 = jnp.bfloat16
NT = (((1,), (1,)), ((), ()))
TN = (((0,), (0,)), ((), ()))
MESH = pl.DeviceIdType.MESH


def layer_norm(values, scaling):
    centered = values - jnp.mean(values, axis=-1, keepdims=True)
    variance = jnp.mean(centered * centered, axis=-1, keepdims=True)
    return centered * lax.rsqrt(variance + EPSILON) * scaling


def normalize(values):
    centered = values - jnp.mean(values, axis=-1, keepdims=True)
    scale = lax.rsqrt(jnp.mean(centered * centered, axis=-1, keepdims=True) + EPSILON)
    return centered * scale, scale


def normalize_back(upstream, normed, scale):
    mean = jnp.mean(upstream, axis=-1, keepdims=True)
    along = jnp.mean(upstream * normed, axis=-1, keepdims=True)
    return scale * (upstream - mean - normed * along)


def max_tiles(local_len):
    count = 1
    while (count // 2) * 314 + (count % 2) * 64 <= local_len + LEN_LONG - 2:
        count += 1
    return count


def fold_rows(values):
    return jnp.sum(values.reshape(values.shape[0] // 8, 8, values.shape[1]), axis=0)


def plan_tiles(lengths, table, row, tiles):
    slots = lengths.shape[1]
    local_len = tiles[1]
    low = lax.axis_index("seq") * local_len
    high = low + local_len
    base = row * (tiles[0] + 1) * ENTRIES

    def step(k, carry):
        begin, count, tile_begin, in_tile, fitted_end = carry
        true_end = begin + lengths[row, k]
        end = jnp.minimum(true_end, SEQ_LEN)
        touches = (end > low) & (begin < high) & (end > begin)
        fresh = touches & ((count == 0) | (end - tile_begin > TILE))
        count = jnp.where(fresh, count + 1, count)
        tile_begin = jnp.where(fresh, begin, tile_begin)
        in_tile = jnp.where(fresh, 0, in_tile + 1)

        @pl.when(touches)
        def _():
            spot = base + (count - 1) * ENTRIES
            table[spot] = tile_begin - low + HALO
            for j in range(4):

                @pl.when(j >= in_tile)
                def _():
                    table[spot + 1 + j] = end - tile_begin

        fitted_end = jnp.where(true_end <= SEQ_LEN, true_end, fitted_end)
        return (end, count, tile_begin, in_tile, fitted_end)

    zero = jnp.int32(0)
    for b in range(tiles[0]):
        table[base + b * ENTRIES] = 0
    _, count, _, _, fitted_end = lax.fori_loop(0, slots, step, (zero, zero, zero, zero, zero), unroll=5)
    table[base + tiles[0] * ENTRIES] = count
    table[base + tiles[0] * ENTRIES + 1] = fitted_end
    windows = local_len // WINDOW
    unpack_from = tiles[2] * (tiles[0] + 1) * ENTRIES + row * windows * 4

    def window(w, b):
        at = HALO + w * WINDOW

        def end_of(n):
            return table[base + n * ENTRIES] + table[base + n * ENTRIES + 4]

        b = jnp.where(end_of(b) <= at, b + 1, b)
        cut = end_of(b) - at
        table[unpack_from + w * 4] = b * TILE + at - table[base + b * ENTRIES]
        table[unpack_from + w * 4 + 1] = (b + 1) * TILE - cut
        table[unpack_from + w * 4 + 2] = cut
        return b

    lax.fori_loop(0, windows, window, zero)
    return count


def tile_fills(table, spot):
    def segments(positions):
        return sum((positions >= table[spot + 1 + j]).astype(jnp.int32) for j in range(4))

    seg = segments(lax.broadcasted_iota(jnp.int32, (TILE, 128), 0))
    lane = lax.broadcasted_iota(jnp.int32, (TILE, 128), 1) % E
    same = seg == lane
    one_hot = jnp.where(same, 1.0, 0.0)
    across = jnp.where(same, 0.0, NEGATIVE)
    keys = jnp.where(lane < 5, across, jnp.where(lane < 8, 1.0, 0.0))
    return one_hot, keys


def project_kernel(
    devices, local_len, tokens, w_qkv, gain, source, projected, normed_t, halo, zero, halo_sem, zero_sem
):
    step = pl.program_id(0)
    rows = halo.shape[1]
    seq = lax.axis_index("seq")
    after, before = seq < devices[1] - 1, seq > 0

    def halo_copy(side, row):
        start = row * local_len + (local_len - HALO if side == 0 else 0)
        return pltpu.make_async_remote_copy(
            src_ref=source.at[start : start + HALO],
            dst_ref=halo.at[side, row],
            send_sem=halo_sem.at[0, side, row],
            recv_sem=halo_sem.at[1, side, row],
            device_id={"seq": seq + 1 if side == 0 else seq - 1},
            device_id_type=MESH,
        )

    def fill(side, row):
        return pltpu.make_async_copy(zero, halo.at[side, row], zero_sem.at[side, row])

    sides = ((0, after, before), (1, before, after))

    @pl.when(step == 0)
    def _():
        barrier = pltpu.get_barrier_semaphore()
        for d in range(1, devices[1]):
            peer = {"seq": lax.rem(seq + d, devices[1])}
            pl.semaphore_signal(barrier, inc=1, device_id=peer, device_id_type=MESH)
        zero[...] = jnp.zeros_like(zero)
        pl.semaphore_wait(barrier, devices[1] - 1)
        for side, sends, receives in sides:

            @pl.when(sends)
            def _():
                for row in range(rows):
                    halo_copy(side, row).start()

            @pl.when(jnp.logical_not(receives))
            def _():
                for row in range(rows):
                    fill(side, row).start()

    normed, _ = normalize(tokens[...].astype(F32))
    low = (normed * gain[...]).astype(BF16)
    normed_t[...] = low.T
    projected[...] = jnp.dot(low, w_qkv[...], preferred_element_type=F32).astype(BF16)

    @pl.when(step == pl.num_programs(0) - 1)
    def _():
        for side, sends, receives in sides:

            @pl.when(sends)
            def _():
                for row in range(rows):
                    halo_copy(side, row).wait_send()

            @pl.when(receives)
            def _():
                for row in range(rows):
                    halo_copy(side, row).wait_recv()

            @pl.when(jnp.logical_not(receives))
            def _():
                for row in range(rows):
                    fill(side, row).wait()


def project(devices, rows, tokens, w_qkv, gain):
    count, width = tokens.shape
    wide = w_qkv.shape[1]
    block = BLOCK
    dma = pltpu.SemaphoreType.DMA
    return pl.pallas_call(
        functools.partial(project_kernel, devices, count // rows),
        grid=(count // block,),
        out_shape=(
            jax.ShapeDtypeStruct((count, wide), BF16),
            jax.ShapeDtypeStruct((width, count), BF16),
            jax.ShapeDtypeStruct((2, rows, HALO, width), BF16),
        ),
        in_specs=[
            pl.BlockSpec((block, width), lambda i: (i, 0)),
            whole_spec(width, wide),
            whole_spec(1, width),
            pl.BlockSpec(memory_space=pl.ANY),
        ],
        out_specs=(
            pl.BlockSpec((block, wide), lambda i: (i, 0)),
            pl.BlockSpec((width, block), lambda i: (0, i)),
            pl.BlockSpec(memory_space=pl.ANY),
        ),
        scratch_shapes=[pltpu.VMEM((HALO, width), BF16), dma((2, 2, rows)), dma((2, rows))],
        compiler_params=pltpu.CompilerParams(
            collective_id=1, has_side_effects=True, vmem_limit_bytes=60 * MIB
        ),
        name="project",
    )(tokens, w_qkv, gain, tokens)


def attend_forward_kernel(
    tiles, lengths, local, left, right, w_qkv, gain, mixed, packed, table,
    spread, out, hot, stage, sems,
):
    row = pl.program_id(0)
    local_len = local.shape[0]
    count = plan_tiles(lengths, table, row, tiles)
    for side, tokens in enumerate((left, right)):
        normed = layer_norm(tokens[0, 0].astype(F32), gain[...]).astype(BF16)
        made = jnp.dot(normed, w_qkv[...], preferred_element_type=F32).astype(BF16)
        start = side * (HALO + local_len)
        for c in range(12):
            spread[c, start : start + HALO, :] = made[:, c * 128 : (c + 1) * 128].astype(F32)
    for c in range(12):
        spread[c, HALO : HALO + local_len, :] = local[:, c * 128 : (c + 1) * 128].astype(F32)
    low = lax.broadcasted_iota(jnp.int32, (TILE, 128), 1) < E
    place = lax.broadcasted_iota(jnp.int32, (TILE, 128), 1) % E

    def store(slot, at):
        return pltpu.make_async_copy(stage.at[slot], packed.at[at], sems.at[slot])

    def one_tile(b, _):
        spot = (row * (tiles[0] + 1) + b) * ENTRIES
        begin = table[spot]
        slot = lax.rem(b, 2)
        at = row * tiles[0] + b

        @pl.when(b >= 2)
        def _():
            store(slot, at - 2).wait()

        one_hot, key_fill = tile_fills(table, spot)
        hot[...] = one_hot
        for group in range(GROUPS):
            stage[slot, group, 8] = key_fill.astype(BF16)
        loaded, held = {}, {}
        key_fill = key_fill.astype(BF16)

        def front(h):
            pair, side = h // 2, h % 2
            group, i = pair // 2, pair % 2
            if side == 0:
                loaded[pair] = tuple(spread[4 * n + pair, pl.ds(begin, TILE), :].astype(BF16) for n in range(3))
                for n in range(3):
                    stage[slot, group, 2 * n + i] = loaded[pair][n]
            q, k, _ = loaded[pair]
            own = low if side == 0 else ~low
            return lax.dot_general(
                jnp.where(own, q, hot[...].astype(BF16)),
                jnp.where(own, k, key_fill),
                NT,
                preferred_element_type=F32,
            )

        def back(h, scores):
            pair, side = h // 2, h % 2
            v = loaded[pair][2]
            zero = jnp.zeros_like(v)
            own = low if side == 0 else ~low
            peak = jnp.max(scores, axis=1, keepdims=True)
            weights = jnp.exp2((scores - peak) * SCALE2).astype(BF16)
            both = jnp.concatenate([jnp.where(own, v, zero), jnp.where(own, zero + 1, zero)], axis=1)
            if side == 0:
                held[pair] = ((weights, both), peak)
                return
            made = jnp.dot(
                jnp.concatenate([held[pair][0][0], weights], axis=1),
                jnp.concatenate([held[pair][0][1], both], axis=0),
                preferred_element_type=F32,
            )
            total = made[:, 128:]
            out[pair, pl.ds(begin, TILE), :] = made[:, :128] / total
            total = pltpu.roll(total, E, 1)
            log_sum = jnp.where(low, peak, held[pair][1]) + jnp.log2(total) * (1.0 / SCALE2)
            first = log_sum.astype(BF16).astype(F32)
            rest = log_sum - first
            second = rest.astype(BF16).astype(F32)
            fill = jnp.where(place == 7, second - rest, hot[...])
            fill = jnp.where(place == 6, -second, fill)
            stage[slot, pair // 2, 6 + pair % 2] = jnp.where(place == 5, -first, fill).astype(BF16)

        ahead = [front(h) for h in range(2)]
        for h in range(8):
            now = ahead.pop(0)
            if h + 2 < 8:
                ahead.append(front(h + 2))
            back(h, now)
        store(slot, at).start()
        return 0

    lax.fori_loop(0, count, one_tile, 0)
    for c in range(4):
        mixed[:, c * 128 : (c + 1) * 128] = out[c, HALO : HALO + local_len, :].astype(BF16)

    @pl.when(count >= 2)
    def _():
        store(lax.rem(count, 2), row * tiles[0] + count - 2).wait()

    store(lax.rem(count + 1, 2), row * tiles[0] + count - 1).wait()


def attend_forward(lengths, local, halo, w_qkv, gain):
    rows = lengths.shape[0]
    width = halo.shape[3]
    local_len = local.shape[0] // rows
    most = max_tiles(local_len)
    held = local_len + 2 * HALO
    return pl.pallas_call(
        functools.partial(attend_forward_kernel, (most, local_len, rows)),
        grid=(rows,),
        out_shape=(
            jax.ShapeDtypeStruct((rows * local_len, width), BF16),
            jax.ShapeDtypeStruct((rows * most, GROUPS, 9, TILE, 128), BF16),
            jax.ShapeDtypeStruct(
                (rows * (most + 1) * ENTRIES + rows * (local_len // WINDOW) * 4,), jnp.int32
            ),
        ),
        in_specs=[
            smem_spec(),
            pl.BlockSpec((local_len, 3 * width), lambda r: (r, 0)),
            pl.BlockSpec((1, 1, HALO, width), lambda r: (0, r, 0, 0)),
            pl.BlockSpec((1, 1, HALO, width), lambda r: (1, r, 0, 0)),
            whole_spec(width, 3 * width),
            whole_spec(1, width),
        ],
        out_specs=(
            pl.BlockSpec((local_len, width), lambda r: (r, 0)),
            pl.BlockSpec(memory_space=pl.ANY),
            smem_spec(),
        ),
        scratch_shapes=[
            pltpu.VMEM((12, held, 128), F32),
            pltpu.VMEM((4, held, 128), F32),
            pltpu.VMEM((TILE, 128), F32),
            pltpu.VMEM((2, GROUPS, 9, TILE, 128), BF16),
            pltpu.SemaphoreType.DMA((2,)),
        ],
        compiler_params=pltpu.CompilerParams(vmem_limit_bytes=60 * MIB),
        name="attend_forward",
    )(lengths, local, halo, halo, w_qkv, gain)


def interleave(chains, lag):
    live = {n: chain for n, chain in enumerate(chains)}
    turn = 0
    while live:
        for n in list(live):
            if turn >= n * lag and next(live[n], None) is None:
                del live[n]
        turn += 1


def mlp_kernel(
    tiles, table, tokens, mixed, cotangent, w_out, w_up, w_down, gain,
    output, activated, d_hidden, d_resid, d_attn, d_mixed, normed_t, mixed_t, cotangent_t, grad_gain,
):
    step = pl.program_id(0)
    most, local_len = tiles
    block = tokens.shape[0]
    per_row = local_len // block
    row = step // per_row
    begin = lax.axis_index("seq") * local_len + (step % per_row) * block
    fitted_end = table[(row * (most + 1) + most) * ENTRIES + 1]
    piece = 256
    pieces = w_up.shape[1] // piece

    @pl.when(step == 0)
    def _():
        grad_gain[...] = jnp.zeros_like(grad_gain)

    def chain(first):
        part = slice(first, first + BLOCK)
        positions = begin + first + lax.broadcasted_iota(jnp.int32, (BLOCK, 1), 0)
        valid = positions < fitted_end
        attn = jnp.dot(mixed[part, :], w_out[...], preferred_element_type=F32)
        dy = cotangent[part, :]
        yield True
        resid = tokens[part, :].astype(F32) + jnp.where(valid, attn, 0.0)
        normed, scale = normalize(resid)
        low = (normed * gain[...]).astype(BF16)
        yield True

        def front(j):
            columns = slice(j * piece, (j + 1) * piece)
            hidden = jnp.dot(low, w_up[:, columns], preferred_element_type=F32)
            return hidden, lax.dot_general(dy, w_down[columns, :], NT, preferred_element_type=F32)

        dense, d_normed = resid, 0.0
        ahead = front(0)
        for j in range(pieces):
            columns = slice(j * piece, (j + 1) * piece)
            hidden, d_act = ahead
            if j + 1 < pieces:
                ahead = front(j + 1)
            square = hidden * hidden
            bent = jnp.tanh(hidden * (GELU_A + (GELU_A * GELU_B) * square))
            half = 0.5 + 0.5 * bent
            act = (hidden * half).astype(BF16)
            slope = half + (0.5 - 0.5 * bent * bent) * hidden * (GELU_A + (3.0 * GELU_A * GELU_B) * square)
            grad = (d_act * slope).astype(BF16)
            activated[j, part, :] = act
            d_hidden[j, part, :] = grad
            dense += jnp.dot(act, w_down[columns, :], preferred_element_type=F32)
            d_normed += lax.dot_general(grad, w_up[:, columns], NT, preferred_element_type=F32)
            if j == 1:
                normed_t[:, part] = low.T
            if j == 2:
                mixed_t[:, part] = mixed[part, :].T
            if j == 3:
                cotangent_t[:, part] = dy.T
            yield True
        output[part, :] = dense.astype(BF16)
        grad_gain[...] += fold_rows(d_normed * normed)
        made = dy.astype(F32) + normalize_back(d_normed * gain[...], normed, scale)
        yield True
        d_resid[part, :] = made
        attn_low = jnp.where(valid, made, 0.0).astype(BF16)
        for n in range(attn_low.shape[1] // 256):
            d_attn[n, part, :] = attn_low[:, n * 256 : (n + 1) * 256]
        d_mixed[part, :] = lax.dot_general(attn_low, w_out[...], NT, preferred_element_type=F32).astype(BF16)

    interleave([chain(first) for first in range(0, block, BLOCK)], 3)


def mlp(local_len, table, tokens, mixed, cotangent, w_out, w_up, w_down, gain):
    count, width = tokens.shape
    hidden = w_up.shape[1]
    rows_of = lambda w: pl.BlockSpec((MLP_BLOCK, w), lambda i: (i, 0))
    blocks_of = lambda w: pl.BlockSpec((w // 256, MLP_BLOCK, 256), lambda i: (0, i, 0))
    turned = pl.BlockSpec((width, MLP_BLOCK), lambda i: (0, i))
    shape = jax.ShapeDtypeStruct
    return pl.pallas_call(
        functools.partial(mlp_kernel, (max_tiles(local_len), local_len)),
        grid=(count // MLP_BLOCK,),
        out_shape=(
            shape((count, width), BF16),
            shape((hidden // 256, count, 256), BF16),
            shape((hidden // 256, count, 256), BF16),
            shape((count, width), F32),
            shape((width // 256, count, 256), BF16),
            shape((count, width), BF16),
            shape((width, count), BF16),
            shape((width, count), BF16),
            shape((width, count), BF16),
            shape((8, width), F32),
        ),
        in_specs=[
            smem_spec(),
            rows_of(width),
            rows_of(width),
            rows_of(width),
            whole_spec(width, width),
            whole_spec(width, hidden),
            whole_spec(hidden, width),
            whole_spec(1, width),
        ],
        out_specs=(
            rows_of(width),
            blocks_of(hidden),
            blocks_of(hidden),
            rows_of(width),
            blocks_of(width),
            rows_of(width),
            turned,
            turned,
            turned,
            whole_spec(8, width),
        ),
        compiler_params=pltpu.CompilerParams(vmem_limit_bytes=60 * MIB),
        name="mlp",
    )(table, tokens, mixed, cotangent, w_out, w_up, w_down, gain)


def tile_backward(pairs, packed, fills, grad_of, put):
    low = lax.broadcasted_iota(jnp.int32, (TILE, 128), 1) < E
    key_fill = fills(pairs)
    loaded = {}

    def front(h):
        pair, side = h // 2, h % 2
        if side == 0:
            loaded[pair] = (packed(pair), packed(pairs + pair), packed(2 * pairs + pair), grad_of(pair), fills(pair))
        q, k, v, o, fill = loaded[pair]
        own = low if side == 0 else ~low
        own_o = jnp.where(own, o, jnp.zeros_like(o))
        scores = lax.dot_general(
            jnp.where(own, k, key_fill), jnp.where(own, q, fill), NT, preferred_element_type=F32
        )
        d_probs = lax.dot_general(v, own_o, NT, preferred_element_type=F32)
        return scores, d_probs, own_o

    made = {}

    def back(h, scores, d_probs, own_o):
        pair, side = h // 2, h % 2
        q, k, _, _, _ = loaded[pair]
        own = low if side == 0 else ~low
        zero = jnp.zeros_like(q)
        probs = jnp.exp2(scores * SCALE2)
        weighted = probs * d_probs
        inner = jnp.sum(weighted, axis=0, keepdims=True)
        d_scores = (weighted - probs * inner).astype(BF16)
        dv = jnp.dot(probs.astype(BF16), own_o, preferred_element_type=F32)
        dk = jnp.dot(d_scores, jnp.where(own, q, zero), preferred_element_type=F32)
        dq = lax.dot_general(d_scores, jnp.where(own, k, zero), TN, preferred_element_type=F32)
        if side == 0:
            made[pair] = (dq, dk, dv)
        else:
            first = made[pair]
            put(pair, (first[0] + dq) * 0.125)
            put(pairs + pair, (first[1] + dk) * 0.125)
            put(2 * pairs + pair, first[2] + dv)

    ahead = [front(0), front(1)]
    for h in range(2 * pairs):
        now = ahead.pop(0)
        if h + 2 < 2 * pairs:
            ahead.append(front(h + 2))
        back(h, *now)


def whole_spec(*shape):
    return pl.BlockSpec(shape, lambda r: (0,) * len(shape))


def smem_spec():
    return pl.BlockSpec(memory_space=pltpu.SMEM)


def sum_plan(devices):
    dp, seq = devices
    chip = [1 << b for b in range(1, dp.bit_length() - 1)]
    along = [1 << b for b in range(seq.bit_length() - 1)]

    def paired(axis, bits):
        return [(axis, tuple(bits[n : n + 2])) for n in range(0, len(bits), 2)]

    core, z = [("dp", (1,))], paired("seq", along)
    one = [("dp", (bit,)) for bit in chip]
    return [core + one + z, core + one[::-1] + z, core + paired("dp", chip) + z]


def chunk_pieces(devices):
    unit = max(1, 16 * devices[0] * devices[1] // PIECE)
    if unit == 1:
        return [4] * 8 + [5, 5, 3, 3]
    return [unit] * (48 // unit)


class GradSum:
    def __init__(self, devices, work, slots, done, send_sem, recv_sem):
        self.plans = sum_plan(devices)
        self.work, self.slots, self.done = work, slots, done
        self.send_sem, self.recv_sem = send_sem, recv_sem
        self.here = {"dp": lax.axis_index("dp"), "seq": lax.axis_index("seq")}
        self.sizes = chunk_pieces(devices)
        self.paths, self.active = [], []
        self.queue, self.clock, self.free_at = [], 0, 0
        base = 0
        for chunk, pieces in enumerate(self.sizes):
            offset, rows, slot, path = base, pieces * PIECE, base, []
            for axis, bits in self.plan(chunk):
                mine, others = self.peers(axis, bits)
                rows //= 1 << len(bits)
                keep = offset + mine * rows
                path.append((keep, [offset + n * rows for n, _ in others], slot, rows))
                offset, slot = keep, slot + rows * len(others)
            self.paths.append(path)
            base += pieces * PIECE

    def plan(self, chunk):
        return self.plans[2 if chunk >= len(self.sizes) - LATE else chunk % 2]

    def peers(self, axis, bits):
        index = self.here[axis]
        own = [(index // bit) % 2 for bit in bits]
        others = []
        for mask in range(1, 1 << len(bits)):
            number, to = 0, index
            for i, bit in enumerate(bits):
                flip = (mask >> i) % 2
                number = number + (1 - own[i] if flip else own[i]) * (1 << i)
                to = to + flip * (bit - 2 * bit * own[i])
            others.append((number, {axis: to}))
        return sum(own[i] * (1 << i) for i in range(len(bits))), others

    def copies(self, chunk, t, pairs):
        axis, bits = self.plan(chunk)[min(t, 2 * len(self.plan(chunk)) - 1 - t)]
        return [
            pltpu.make_async_remote_copy(
                src_ref=source,
                dst_ref=target,
                send_sem=self.send_sem.at[chunk, t, n],
                recv_sem=self.recv_sem.at[chunk, t, n],
                device_id=to,
                device_id_type=MESH,
            )
            for n, ((source, target), (_, to)) in enumerate(zip(pairs, self.peers(axis, bits)[1]))
        ]

    def spreading(self, chunk, s):
        _, gives, slot, rows = self.paths[chunk][s]
        return self.copies(
            chunk,
            s,
            [
                (
                    self.work.at[pl.ds(pl.multiple_of(give, 16), rows)],
                    self.slots.at[slot + n * rows : slot + (n + 1) * rows],
                )
                for n, give in enumerate(gives)
            ],
        )

    def gathering(self, chunk, s, received):
        keep, gives, _, rows = self.paths[chunk][s]
        parts = [
            self.done.at[pl.ds(pl.multiple_of(give if received else keep, 16), rows)] for give in gives
        ]
        return self.copies(chunk, 2 * len(self.plan(chunk)) - 1 - s, [(part, part) for part in parts])

    def add(self, chunk, s):
        keep, gives, slot, rows = self.paths[chunk][s]
        into = self.done if s + 1 == len(self.plan(chunk)) else self.work
        count = next(n for n in range(1, rows) if rows % (16 * n) == 0 and rows // n <= 512)
        block = rows // count

        @pl.loop(0, count)
        def _(i):
            at = pl.ds(pl.multiple_of(keep + i * block, 16), block)
            total = self.work[at, :].astype(F32)
            for n in range(len(gives)):
                from_at = pl.ds(pl.multiple_of(slot + n * rows + i * block, 16), block)
                total += self.slots[from_at, :].astype(F32)
            into[at, :] = total.astype(BF16)

    def event(self, chunk, t):
        steps = len(self.plan(chunk))
        if 0 < t <= steps:
            for copy in self.spreading(chunk, t - 1):
                copy.wait()
            self.add(chunk, t - 1)
        elif t > steps:
            for copy in self.gathering(chunk, 2 * steps - t, False):
                copy.wait_send()
            for copy in self.gathering(chunk, 2 * steps - t, True):
                copy.wait_recv()
        if t < steps:
            for copy in self.spreading(chunk, t):
                copy.start()
        elif t < 2 * steps:
            for copy in self.gathering(chunk, 2 * steps - 1 - t, False):
                copy.start()
        return t == 2 * steps

    def begin(self, chunks, now=False):
        self.queue += chunks
        while self.queue and (now or self.clock >= self.free_at):
            for chunk in self.queue[:2]:
                self.event(chunk, 0)
                self.active.append([chunk, 1])
            self.queue = self.queue[2:]
            self.free_at = self.clock + APART

    def advance(self, finish):
        self.clock += 1
        for entry in list(self.active):
            if self.event(*entry):
                finish(entry[0])
                self.active.remove(entry)
            entry[1] += 1
        self.begin([])


def backward_kernel(
    devices, tiles, table, gains, w_qkv, gain_one,
    normed_two_t, cotangent_t, mixed_t, normed_one_t, d_hidden, activated, d_attn, d_mixed, tokens, d_resid,
    packed,
    grad_tokens, summed, gains_out,
    work, slots, done, left_a, left_b, right_block, halo, d_mix, tok, resid, made_tok, d_proj, bins, d_out,
    tile_in, gain_slots, gain_one_sum,
    send_sem, recv_sem, gain_send, gain_recv, halo_sem, load_sem, block_sem, tile_sem, store_sem, out_sem,
):
    most, local_len = tiles
    count = tok.shape[0]
    rows = count // local_len
    seq = lax.axis_index("seq")
    sums = GradSum(devices, work, slots, done, send_sem, recv_sem)

    barrier = pltpu.get_barrier_semaphore()
    after, before = seq < devices[1] - 1, seq > 0
    peers = [to for axis, bits in sums.plans[2] if axis == "dp" for _, to in sums.peers(axis, bits)[1]]
    peers += [{"seq": lax.rem(seq + d, devices[1])} for d in range(1, devices[1])]
    for peer in peers:
        pl.semaphore_signal(barrier, inc=1, device_id=peer, device_id_type=MESH)

    load_a = lambda ref, k: pltpu.make_async_copy(ref, left_a, load_sem.at[k])
    load_b = lambda ref, k: pltpu.make_async_copy(ref, left_b, load_sem.at[k])
    load_block = lambda ref, block, slot: pltpu.make_async_copy(
        ref.at[block], right_block.at[slot], block_sem.at[slot]
    )
    load_mix = pltpu.make_async_copy(d_mixed, d_mix, load_sem.at[4])
    load_tok = pltpu.make_async_copy(tokens, tok, load_sem.at[5])
    load_resid = pltpu.make_async_copy(d_resid, resid, load_sem.at[6])
    load_a(normed_two_t, 0).start()
    for n in range(BLOCKS_AHEAD):
        load_block(d_hidden, n, n).start()
    load_b(cotangent_t, 1).start()
    load_mix.start()

    pl.semaphore_wait(barrier, len(peers))

    def halo_copy(side, row):
        start = row * local_len + (local_len - HALO if side == 0 else 0)
        return pltpu.make_async_remote_copy(
            src_ref=d_mixed.at[start : start + HALO],
            dst_ref=halo.at[side, row],
            send_sem=halo_sem.at[0, side, row],
            recv_sem=halo_sem.at[1, side, row],
            device_id={"seq": seq + 1 if side == 0 else seq - 1},
            device_id_type=MESH,
        )

    for side, sends, receives in ((0, after, before), (1, before, after)):

        @pl.when(sends)
        def _():
            for row in range(rows):
                halo_copy(side, row).start()

        @pl.when(jnp.logical_not(receives))
        def _():
            for row in range(rows):
                halo[side, row] = jnp.zeros(halo.shape[2:], BF16)

    stored = []

    def store(chunk):
        part = pl.ds(sum(sums.sizes[:chunk]) * PIECE, sums.sizes[chunk] * PIECE)
        return pltpu.make_async_copy(done.at[part], summed.at[part], out_sem.at[chunk])

    def finish(chunk):
        store(chunk).start()
        stored.append(chunk)

    begun = [0]

    def ready(pieces):
        chunks = []
        while begun[0] < len(sums.sizes) and sum(sums.sizes[: begun[0] + 1]) <= pieces:
            chunks.append(begun[0])
            begun[0] += 1
        sums.begin(chunks, pieces >= 48)

    def put_columns(base, block, product):
        low = product.astype(BF16)
        for i in range(2):
            at = pl.multiple_of((base + 2 * block + i) * PIECE, PIECE)
            work[pl.ds(at, PIECE), :] = low[:, i * 128 : (i + 1) * 128]

    def put_rows(base, block, product):
        low = product.T.astype(BF16)
        for c in range(4):
            at = (base + (block // 2) * 4 + c) * PIECE + (block % 2) * 256
            work[pl.ds(pl.multiple_of(at, 256), 256), :] = low[:, c * 128 : (c + 1) * 128]

    half = d_hidden.shape[0] // 2
    runs = [
        (left_a, d_hidden, 0, half, 0, put_columns),
        (left_a, d_hidden, half, half, 0, put_columns),
        (left_b, activated, 0, half, 16, put_rows),
        (left_b, activated, half, half, 16, put_rows),
        (left_a, d_attn, 0, 2, 32, put_columns),
    ]
    waits = {0: load_a(normed_two_t, 0), 2: load_b(cotangent_t, 1), 4: load_a(mixed_t, 2)}
    at = 0
    for n, (lhs, ref, first, blocks, base, put) in enumerate(runs):
        if n in waits:
            waits[n].wait()

        upcoming = [(run[1], run[2], run[3]) for run in runs[n:]][:3]

        def one_block(j, _, n=n, upcoming=upcoming, lhs=lhs, ref=ref, first=first, blocks=blocks, base=base, put=put, at=at):
            slot, later = lax.rem(at + j, BLOCKS_AHEAD + 1), lax.rem(at + j + BLOCKS_AHEAD, BLOCKS_AHEAD + 1)
            load_block(ref, first + j, slot).wait()
            until = 0
            for next_ref, next_first, next_blocks in upcoming:
                since, until = until, until + next_blocks

                @pl.when((j + BLOCKS_AHEAD >= since) & (j + BLOCKS_AHEAD < until))
                def _():
                    load_block(next_ref, next_first + j + BLOCKS_AHEAD - since, later).start()

            put(base, first + j, jnp.dot(lhs[...], right_block[slot], preferred_element_type=F32))
            return 0

        lax.fori_loop(0, blocks, one_block, 0)
        at += blocks
        if n == 1:
            load_a(mixed_t, 2).start()
        if n == 3:
            load_b(normed_one_t, 3).start()
            load_tok.start()
            load_resid.start()
        if 0 < n < 4:
            sums.advance(finish)
        if n < 4:
            ready(8 * (n + 1))

    per_group = rows * most
    total = GROUPS * per_group
    unpack_from = rows * (most + 1) * ENTRIES
    windows = local_len // WINDOW

    def load_tile(step, slot):
        group, spot = step // per_group, lax.rem(step, per_group)
        return pltpu.make_async_copy(packed.at[spot, group], tile_in.at[slot], tile_sem.at[slot])

    for n in range(AHEAD):
        load_tile(n, n).start()
    load_mix.wait()
    for side, sends, receives in ((0, after, before), (1, before, after)):

        @pl.when(sends)
        def _():
            for row in range(rows):
                halo_copy(side, row).wait_send()

        @pl.when(receives)
        def _():
            for row in range(rows):
                halo_copy(side, row).wait_recv()

    def one_tile(step, _):
        slot = lax.rem(step, AHEAD + 1)
        group, spot = step // per_group, lax.rem(step, per_group)
        row, b = spot // most, lax.rem(spot, most)
        load_tile(step, slot).wait()

        @pl.when(step + AHEAD < total)
        def _():
            load_tile(step + AHEAD, lax.rem(step + AHEAD, AHEAD + 1)).start()

        @pl.when(b == 0)
        def _():
            start = pl.multiple_of(row * local_len, local_len)
            for i in range(2):
                columns = pl.ds(pl.multiple_of((2 * group + i) * 128, 128), 128)
                d_out[i, :HALO, :] = halo[0, row, :, columns].astype(F32)
                d_out[i, HALO : HALO + local_len, :] = d_mix[pl.ds(start, local_len), columns].astype(F32)
                d_out[i, HALO + local_len :, :] = halo[1, row, :, columns].astype(F32)

        begin = table[(row * (most + 1) + b) * ENTRIES]

        def put(c, values):
            bins[c, pl.ds(pl.multiple_of(b * TILE, TILE), TILE), :] = values

        tile_backward(
            2,
            lambda c: tile_in[slot, c],
            lambda c: tile_in[slot, 6 + c],
            lambda c: d_out[c, pl.ds(begin, TILE), :].astype(BF16),
            put,
        )

        @pl.when(b == most - 1)
        def _():
            @pl.loop(0, windows)
            def _(w):
                entry = unpack_from + (row * windows + w) * 4
                one, two, cut = table[entry], table[entry + 1], table[entry + 2]
                in_one = lax.broadcasted_iota(jnp.int32, (WINDOW, 128), 0) < cut
                to = pl.multiple_of(row * local_len + w * WINDOW, WINDOW)
                for c in range(6):
                    values = jnp.where(
                        in_one, bins[c, pl.ds(one, WINDOW), :], bins[c, pl.ds(two, WINDOW), :]
                    )
                    d_proj[group * 6 + c, pl.ds(to, WINDOW), :] = values.astype(BF16)

        def qkv_gradient(g):
            for kind in range(3):
                both = jnp.concatenate([d_proj[g * 6 + 2 * kind + i] for i in range(2)], axis=1)
                product = jnp.dot(left_b[...], both, preferred_element_type=F32).astype(BF16)
                for i in range(2):
                    piece = 36 + 6 * g + 2 * kind + i
                    work[piece * PIECE : (piece + 1) * PIECE, :] = product[:, i * 128 : (i + 1) * 128]

        for k in range(total):
            ends_group = (k + 1) % per_group == 0
            moves = k in MOVES and sums.active
            if not (ends_group or moves):
                continue

            @pl.when(step == k)
            def _():
                if moves:
                    sums.advance(finish)
                if ends_group:
                    g = k // per_group
                    if g == 0:
                        load_b(normed_one_t, 3).wait()
                    qkv_gradient(g)
                    ready(42 + 6 * g)

        return 0

    lax.fori_loop(0, total, one_tile, 0)

    load_tok.wait()
    load_resid.wait()
    gain_one_sum[...] = jnp.zeros_like(gain_one_sum)
    blocks = count // BLOCK

    def store_tok(i):
        part = pl.ds(pl.multiple_of(i * BLOCK, BLOCK), BLOCK)
        return pltpu.make_async_copy(made_tok.at[part], grad_tokens.at[part], store_sem.at[i])

    def input_block(i, _):
        part = pl.ds(pl.multiple_of(i * BLOCK, BLOCK), BLOCK)
        order = [6 * (pair // 2) + 2 * kind + pair % 2 for kind in range(3) for pair in range(4)]
        d_projected = jnp.concatenate([d_proj[c, part, :] for c in order], axis=1)
        d_normed = lax.dot_general(d_projected, w_qkv[...], NT, preferred_element_type=F32)
        normed, scale = normalize(tok[part, :].astype(F32))
        gain_one_sum[...] += fold_rows(d_normed * normed)
        back = normalize_back(d_normed * gain_one[...], normed, scale)
        made_tok[part, :] = (resid[part, :] + back).astype(BF16)
        store_tok(i).start()
        for k in range(2, blocks, 3):

            @pl.when(i == k)
            def _():
                sums.advance(finish)

        return 0

    lax.fori_loop(0, blocks, input_block, 0)

    gain_plan = sums.plans[2]

    def gain_copies(s):
        return [
            pltpu.make_async_remote_copy(
                src_ref=gain_slots.at[s, 0],
                dst_ref=gain_slots.at[s, n + 1],
                send_sem=gain_send.at[s, n],
                recv_sem=gain_recv.at[s, n],
                device_id=to,
                device_id_type=MESH,
            )
            for n, (_, to) in enumerate(sums.peers(*gain_plan[s])[1])
        ]

    gain_slots[0, 0, :8] = gain_one_sum[...]
    gain_slots[0, 0, 8:] = gains[...]
    for copy in gain_copies(0):
        copy.start()
    for s in range(len(gain_plan)):
        if sums.active:
            sums.advance(finish)
        joined = gain_slots[s, 0]
        for n, copy in enumerate(gain_copies(s)):
            copy.wait()
            joined += gain_slots[s, n + 1]
        if s + 1 < len(gain_plan):
            gain_slots[s + 1, 0] = joined
            for copy in gain_copies(s + 1):
                copy.start()
        else:
            gains_out[...] = joined
    while sums.active:
        sums.advance(finish)
    for i in range(blocks):
        store_tok(i).wait()
    for chunk in stored:
        store(chunk).wait()


def backward(
    devices, rows, table, gains, w_qkv, gain_one, normed_two_t, cotangent_t, mixed_t, normed_one_t,
    d_hidden, activated, d_attn, d_mixed, tokens, d_resid, packed,
):
    count, width = tokens.shape
    local_len = count // rows
    most = max_tiles(local_len)
    held = local_len + 2 * HALO
    steps = max(len(plan) for plan in sum_plan(devices))
    chunks = len(chunk_pieces(devices))
    shape = jax.ShapeDtypeStruct
    anywhere = pl.BlockSpec(memory_space=pl.ANY)
    vmem = pl.BlockSpec(memory_space=pltpu.VMEM)
    dma = pltpu.SemaphoreType.DMA
    return pl.pallas_call(
        functools.partial(backward_kernel, devices, (most, local_len)),
        out_shape=(
            shape((count, width), BF16),
            shape((48 * PIECE, 128), BF16),
            shape((16, width), F32),
        ),
        in_specs=[smem_spec(), vmem, vmem, vmem] + [anywhere] * 11,
        out_specs=(anywhere, anywhere, vmem),
        scratch_shapes=[
            pltpu.VMEM((48 * PIECE, 128), BF16),
            pltpu.VMEM((48 * PIECE, 128), BF16),
            pltpu.VMEM((48 * PIECE, 128), BF16),
            pltpu.VMEM((width, count), BF16),
            pltpu.VMEM((width, count), BF16),
            pltpu.VMEM((BLOCKS_AHEAD + 1, count, 256), BF16),
            pltpu.VMEM((2, rows, HALO, width), BF16),
            pltpu.VMEM((count, width), BF16),
            pltpu.VMEM((count, width), BF16),
            pltpu.VMEM((count, width), F32),
            pltpu.VMEM((count, width), BF16),
            pltpu.VMEM((12, count, 128), BF16),
            pltpu.VMEM((6, most * TILE + WINDOW, 128), F32),
            pltpu.VMEM((2, held, 128), F32),
            pltpu.VMEM((AHEAD + 1, 9, TILE, 128), BF16),
            pltpu.VMEM((steps, 4, 16, width), F32),
            pltpu.VMEM((8, width), F32),
            dma((chunks, 2 * steps, 3)),
            dma((chunks, 2 * steps, 3)),
            dma((steps, 3)),
            dma((steps, 3)),
            dma((2, 2, rows)),
            dma((7,)),
            dma((BLOCKS_AHEAD + 1,)),
            dma((AHEAD + 1,)),
            dma((count // BLOCK,)),
            dma((chunks,)),
        ],
        compiler_params=pltpu.CompilerParams(
            collective_id=0, has_side_effects=True, vmem_limit_bytes=60 * MIB
        ),
        name="backward",
    )(
        table, gains, w_qkv, gain_one, normed_two_t, cotangent_t, mixed_t, normed_one_t,
        d_hidden, activated, d_attn, d_mixed, tokens, d_resid, packed,
    )


def unpack_kernel(up, down, out, *refs):
    grad_qkv, grad_out, grad_up, grad_down = refs[3:]
    for c in range(4):
        columns = slice(c * 128, (c + 1) * 128)
        grad_up[:, columns] = up[c].astype(F32)
        grad_down[:, columns] = down[c].astype(F32)
    grad_out[...] = out[0].astype(F32)
    for n in range(3):
        grad_qkv[:, n * 128 : (n + 1) * 128] = refs[n][0].astype(F32)


def unpack(summed, width, hidden, wide):
    pieces = summed.reshape(48, PIECE, 128)

    def qkv_piece(n):
        def place(i):
            block = 3 * i + n
            kind, pair = block // 4, block % 4
            return (36 + 6 * (pair // 2) + 2 * kind + pair % 2, 0, 0)

        return pl.BlockSpec((1, PIECE, 128), place)

    shape = jax.ShapeDtypeStruct
    return pl.pallas_call(
        unpack_kernel,
        grid=(4,),
        out_shape=(
            shape((width, wide), F32),
            shape((width, width), F32),
            shape((width, hidden), F32),
            shape((hidden, width), F32),
        ),
        in_specs=[
            pl.BlockSpec((4, PIECE, 128), lambda i: (i, 0, 0)),
            pl.BlockSpec((4, PIECE, 128), lambda i: (4 + i, 0, 0)),
            pl.BlockSpec((1, PIECE, 128), lambda i: (32 + i, 0, 0)),
        ]
        + [qkv_piece(n) for n in range(3)],
        out_specs=(
            pl.BlockSpec((width, wide // 4), lambda i: (0, i)),
            pl.BlockSpec((width, width // 4), lambda i: (0, i)),
            pl.BlockSpec((width, hidden // 4), lambda i: (0, i)),
            pl.BlockSpec((hidden // 4, width), lambda i: (i, 0)),
        ),
        compiler_params=pltpu.CompilerParams(vmem_limit_bytes=60 * MIB),
        name="unpack",
    )(*[pieces] * 6)


def body(
    devices, tokens, item_lengths, w_qkv, w_out, w_up, w_down, gain_one, gain_two, cotangent
):
    rows, local_len, width = tokens.shape
    count = rows * local_len
    gain_one, gain_two = gain_one.reshape(1, width), gain_two.reshape(1, width)
    flat = tokens.reshape(count, width)
    projected, normed_one_t, halo = project(devices, rows, flat, w_qkv, gain_one)
    mixed, packed, table = attend_forward(item_lengths, projected, halo, w_qkv, gain_one)
    (
        output, activated, d_hidden, d_resid, d_attn, d_mixed, normed_two_t, mixed_t, cotangent_t, grad_gain_two
    ) = mlp(local_len, table, flat, mixed, cotangent.reshape(count, width), w_out, w_up, w_down, gain_two)
    grad_tokens, summed, gains = backward(
        devices, rows, table, grad_gain_two, w_qkv, gain_one, normed_two_t, cotangent_t, mixed_t, normed_one_t,
        d_hidden, activated, d_attn, d_mixed, flat, d_resid, packed,
    )
    grads = tuple(unpack(summed, width, w_up.shape[1], w_qkv.shape[1]))
    gains = jnp.sum(gains.reshape(2, 8, width), axis=1)
    placed = (output.reshape(tokens.shape), grad_tokens.reshape(tokens.shape))
    return placed + grads + (gains[0], gains[1])


def solution(mesh):
    rows = P("dp", "seq", None)
    placed = (rows, P("dp", None), P(), P(), P(), P(), P(), P(), rows)
    return jax.shard_map(
        functools.partial(body, (mesh.shape["dp"], mesh.shape["seq"])),
        mesh=mesh,
        in_specs=placed,
        out_specs=(rows, rows, P(), P(), P(), P(), P(), P()),
        check_vma=False,
    )
```
